32 devices in a mesh: lat: 4 (over y, x), lon: 8 (over z, core).
Axes of the slice: x: 2, y: 2, z: 4, core: 2. Of those that a mesh axis runs over, the one named last changes fastest.
Arguments:
- nodes: bfloat16 [64, 512, 512], P('lat', 'lon'), may hold values from -6 to 6
- cotangent: bfloat16 [64, 512, 512], P('lat', 'lon'), may hold values from -6 to 6
- w_send: bfloat16 [512, 512], replicated, may hold values from -0.25 to 0.25
- w_recv: bfloat16 [512, 512], replicated, may hold values from -0.25 to 0.25
- edge_bias: float32 [512], replicated, may hold values from -4 to 4
- w_self: bfloat16 [512, 512], replicated, may hold values from -0.25 to 0.25
- w_agg: bfloat16 [512, 512], replicated, may hold values from -0.25 to 0.25
- node_bias: float32 [512], replicated, may hold values from -3 to 3
- w_out: bfloat16 [512, 512], replicated, may hold values from -0.25 to 0.25
- gain: float32 [512], replicated, may hold values from 0.5 to 1.5
- coarse_slots: int32 [4, 8, 16], P('lat', 'lon'), may hold values from 0 to 1023, as said below
- long_senders: int32 [4, 8, 8, 8], P('lat', 'lon'), may hold values from 0 to 15
- long_receivers: int32 [4, 8, 8, 8], P('lat', 'lon'), may hold values from 0 to 15
Outputs:
- new_nodes: bfloat16 [64, 512, 512], P('lat', 'lon')
- grad_nodes: bfloat16 [64, 512, 512], P('lat', 'lon')
- grad_send: float32 [512, 512], replicated
- grad_recv: float32 [512, 512], replicated
- grad_edge_bias: float32 [512], replicated
- grad_self: float32 [512, 512], replicated
- grad_agg: float32 [512, 512], replicated
- grad_node_bias: float32 [512], replicated
- grad_out: float32 [512, 512], replicated
- grad_gain: float32 [512], replicated
The draws below stay inside these ranges and needn't reach their ends.
Inputs may be any that keep to these rules, and one draw needn't show every extreme that they name: `coarse_slots`: the 16 entries of one patch are distinct positions r * 64 + c of that patch.
All inputs are finite; a program needn't handle non-finite values.
Results may differ from the reference program's by a relative error of at most 0.008.
Values may be sent and summed in bfloat16 or wider, within the bound.
No kernel may reach another device: no remote copies, remote signals or barrier semaphores. Data moves between devices by JAX's collectives and lax.ppermute only.
A program may use at most 128 MiB of HBM per device.

```python
import jax
import jax.numpy as jnp
from jax import lax

D = 512
PATCH_ROWS = 16
PATCH_COLS = 64
COARSE = 16
LONG_EDGES = 8
GRID_ROWS = 64
GRID_COLS = 512
NODES = 32768
N_LAT = 4
N_LON = 8


def bring_front(perm, target, place):
    where_now = jnp.argmax(perm == target).astype(jnp.int32)
    former = perm[place]
    return perm.at[place].set(target).at[where_now].set(former)


def draw_coarse_slots(key, part):
    key = jax.random.fold_in(key, 7)
    patch_size = PATCH_ROWS * PATCH_COLS
    patches = N_LAT * N_LON
    keys = jax.random.split(key, patches + 1)
    perms = jax.vmap(lambda single: jax.random.permutation(single, patch_size))(keys[:patches])
    perms = perms.astype(jnp.int32)
    chosen = jax.random.randint(keys[patches], (2,), 0, patches)
    patch_ids = jnp.arange(patches)[:, None]
    highest = jax.vmap(lambda perm: bring_front(perm, patch_size - 1, 0))(perms)
    perms = jnp.where(patch_ids == chosen[0], highest, perms)
    lowest = jax.vmap(lambda perm: bring_front(perm, 0, 1))(perms)
    perms = jnp.where(patch_ids == chosen[1], lowest, perms)
    return perms[:, :COARSE].reshape(N_LAT, N_LON, COARSE).astype(jnp.int32)


def set_ends(values, rng, smallest, top_value):
    longest = values.shape.index(max(values.shape))
    spots = []
    for shift in (0, 1):
        where = [jax.random.randint(jax.random.fold_in(rng, axis), (), 0, length) for axis, length in enumerate(values.shape)]
        where[longest] = (where[longest] + shift) % values.shape[longest]
        spots.append(tuple(where))
    return values.at[spots[0]].set(smallest).at[spots[1]].set(top_value)


def level_of(key, extent, cuts, low, top_value):
    level, own = 1.0, jax.random.fold_in(key, 6)
    for axis_at, blocks in cuts:
        draws = jnp.exp(jax.random.uniform(jax.random.fold_in(own, axis_at), (blocks,), jnp.float32, low / len(cuts), top_value / len(cuts)))
        level = level * jnp.repeat(draws, extent[axis_at] // blocks).reshape([-1 if axis == axis_at else 1 for axis in range(len(extent))])
    return level


def bell_draw(key, shape, deviation, most, shards=(), held_as=jnp.bfloat16):
    result = jax.random.normal(key, shape, jnp.float32) * deviation
    if len(shards) > 0:
        result = level_of(key, shape, shards, -0.22, 0.18) * result
    return jnp.clip(result, min=-most, max=most).astype(held_as)


def setup_inputs(seed: int = 0) -> dict:
    seeds = jax.random.split(jax.random.key(seed), 14)
    return {
        "nodes": bell_draw(seeds[0], (GRID_ROWS, GRID_COLS, D), 1.0, 6.0, ((0, 4), (1, 8))),
        "cotangent": bell_draw(seeds[1], (GRID_ROWS, GRID_COLS, D), 1.0, 6.0, ((0, 4), (1, 8))),
        "w_send": bell_draw(seeds[2], (D, D), D ** -0.5, 0.25),
        "w_recv": bell_draw(seeds[3], (D, D), D ** -0.5, 0.25),
        "edge_bias": bell_draw(seeds[4], (D,), 1.0, 4.0, (), jnp.float32),
        "w_self": bell_draw(seeds[5], (D, D), D ** -0.5, 0.25),
        "w_agg": bell_draw(seeds[6], (D, D), D ** -0.5, 0.25),
        "node_bias": bell_draw(seeds[7], (D,), 0.5, 3.0, (), jnp.float32),
        "w_out": bell_draw(seeds[8], (D, D), D ** -0.5, 0.25),
        "gain": jnp.clip(1.0 + 0.1 * jax.random.normal(seeds[9], (D,), jnp.float32), 0.5, 1.5),
        "coarse_slots": draw_coarse_slots(jax.random.fold_in(seeds[13], 71), 0),
        "long_senders": set_ends(jax.random.randint(seeds[11], (N_LAT, N_LON, N_LON, LONG_EDGES), 0, COARSE), jax.random.fold_in(seeds[11], 1), 0, COARSE - 1).astype(jnp.int32),
        "long_receivers": set_ends(jax.random.randint(seeds[12], (N_LAT, N_LON, N_LON, LONG_EDGES), 0, COARSE), jax.random.fold_in(seeds[12], 1), 0, COARSE - 1).astype(jnp.int32),
    }


OFFSETS = ((1, 0), (-1, 0), (0, 1), (0, -1), (1, -1), (-1, 1))
epsilon = 1e-05

def silu_slope(values):
    sigmoid = jax.nn.sigmoid(values)
    return sigmoid * (1.0 + values * (1.0 - sigmoid))

def matmul(left, right):
    return jnp.dot(left, right, preferred_element_type=jnp.float32)

def to_blocks(field):
    depth = field.shape[-1]
    split = field.reshape(N_LAT, PATCH_ROWS, N_LON, PATCH_COLS, depth).transpose(0, 2, 1, 3, 4)
    return split.reshape(N_LAT, N_LON, PATCH_ROWS * PATCH_COLS, depth)

def from_blocks(blocks):
    depth = blocks.shape[-1]
    split = blocks.reshape(N_LAT, N_LON, PATCH_ROWS, PATCH_COLS, depth).transpose(0, 2, 1, 3, 4)
    return split.reshape(GRID_ROWS, GRID_COLS, depth)

def reference(nodes, cotangent, w_send, w_recv, edge_bias, w_self, w_agg, node_bias, w_out, gain, coarse_slots, long_senders, long_receivers):
    flat_nodes = nodes.reshape(NODES, D)
    send_proj = matmul(flat_nodes, w_send).astype(jnp.bfloat16).reshape(GRID_ROWS, GRID_COLS, D)
    recv_proj = matmul(flat_nodes, w_recv).reshape(GRID_ROWS, GRID_COLS, D)
    grid_row = jnp.arange(GRID_ROWS)

    def row_valid(lat_step):
        inside = (grid_row + lat_step >= 0) & (grid_row + lat_step < GRID_ROWS)
        return inside.astype(jnp.float32)[:, None, None]
    fine_sum = jnp.zeros((GRID_ROWS, GRID_COLS, D), jnp.float32)
    for lat_step, lon_step in OFFSETS:
        sender = jnp.roll(send_proj, (-lat_step, -lon_step), axis=(0, 1)).astype(jnp.float32)
        fine_sum = fine_sum + row_valid(lat_step) * jax.nn.silu(sender + recv_proj + edge_bias)
    lat_idx = jnp.arange(N_LAT)[:, None, None]
    lon_idx = jnp.arange(N_LON)[None, :, None]
    coarse_send = to_blocks(send_proj)[lat_idx, lon_idx, coarse_slots]
    coarse_recv = to_blocks(recv_proj)[lat_idx, lon_idx, coarse_slots]
    lat_grid = jnp.arange(N_LAT)[:, None, None, None]
    lon_grid = jnp.arange(N_LON)[None, :, None, None]
    src_grid = jnp.arange(N_LON)[None, None, :, None]
    edge_send = coarse_send[lat_grid, src_grid, long_senders].astype(jnp.float32)
    edge_recv = coarse_recv[lat_grid, lon_grid, long_receivers]
    pre_long = edge_send + edge_recv + edge_bias
    empty_blocks = jnp.zeros((N_LAT, N_LON, COARSE, D), jnp.float32)
    coarse_sum = empty_blocks.at[lat_grid, lon_grid, long_receivers].add(jax.nn.silu(pre_long))
    total = from_blocks(to_blocks(fine_sum).at[lat_idx, lon_idx, coarse_slots].add(coarse_sum))
    gathered = total.astype(jnp.bfloat16).reshape(NODES, D)
    pre_node = matmul(flat_nodes, w_self) + matmul(gathered, w_agg) + node_bias
    hidden = jax.nn.silu(pre_node).astype(jnp.bfloat16)
    output = matmul(hidden, w_out)
    row_mean = lax.optimization_barrier(jnp.mean(output, axis=-1, keepdims=True))
    centred = output - row_mean
    inv_std = lax.rsqrt(lax.optimization_barrier(jnp.mean(centred * centred, axis=-1, keepdims=True)) + epsilon)
    normed = centred * inv_std
    new_flat = (flat_nodes.astype(jnp.float32) + gain * normed).astype(jnp.bfloat16)
    grad_scale = float(NODES) ** (-0.5)
    cot_flat = cotangent.reshape(NODES, D).astype(jnp.float32)
    grad_gain = lax.optimization_barrier(jnp.sum(cot_flat * normed, axis=0))
    d_norm = cot_flat * gain
    d_output = (inv_std * (d_norm - lax.optimization_barrier(jnp.mean(d_norm, axis=-1, keepdims=True)) - normed * lax.optimization_barrier(jnp.mean(d_norm * normed, axis=-1, keepdims=True)))).astype(jnp.bfloat16)
    grad_out = matmul(hidden.T, d_output)
    d_pre = matmul(d_output, w_out.T) * silu_slope(pre_node)
    grad_node_bias = lax.optimization_barrier(jnp.sum(d_pre, axis=0))
    d_pre_b = d_pre.astype(jnp.bfloat16)
    grad_self = matmul(flat_nodes.T, d_pre_b)
    grad_agg = matmul(gathered.T, d_pre_b)
    d_sum_b = lax.optimization_barrier(matmul(d_pre_b, w_agg.T).astype(jnp.bfloat16))
    d_sum = d_sum_b.astype(jnp.float32).reshape(GRID_ROWS, GRID_COLS, D)
    d_recv = jnp.zeros((GRID_ROWS, GRID_COLS, D), jnp.float32)
    d_send = jnp.zeros((GRID_ROWS, GRID_COLS, D), jnp.float32)
    grad_edge_bias = jnp.zeros((D,), jnp.float32)
    for lat_step, lon_step in OFFSETS:
        sender = jnp.roll(send_proj, (-lat_step, -lon_step), axis=(0, 1)).astype(jnp.float32)
        slope_in = row_valid(lat_step) * d_sum * silu_slope(sender + recv_proj + edge_bias)
        d_recv = d_recv + slope_in
        d_send = d_send + jnp.roll(slope_in, (lat_step, lon_step), axis=(0, 1))
        grad_edge_bias = grad_edge_bias + lax.optimization_barrier(jnp.sum(slope_in, axis=(0, 1)))
    coarse_dsum = to_blocks(d_sum)[lat_idx, lon_idx, coarse_slots]
    slope_long = coarse_dsum[lat_grid, lon_grid, long_receivers] * silu_slope(pre_long)
    grad_edge_bias = grad_edge_bias + lax.optimization_barrier(jnp.sum(slope_long, axis=(0, 1, 2, 3)))
    recv_long = empty_blocks.at[lat_grid, lon_grid, long_receivers].add(slope_long)
    send_long = empty_blocks.at[lat_grid, src_grid, long_senders].add(slope_long)
    d_recv_b = from_blocks(to_blocks(d_recv).at[lat_idx, lon_idx, coarse_slots].add(recv_long))
    d_send_b = from_blocks(to_blocks(d_send).at[lat_idx, lon_idx, coarse_slots].add(send_long))
    d_recv_b = d_recv_b.astype(jnp.bfloat16).reshape(NODES, D)
    d_send_b = d_send_b.astype(jnp.bfloat16).reshape(NODES, D)
    grad_recv = matmul(flat_nodes.T, d_recv_b)
    grad_send = matmul(flat_nodes.T, d_send_b)
    grad_flat = (cot_flat + matmul(d_pre_b, w_self.T) + matmul(d_recv_b, w_recv.T) + matmul(d_send_b, w_send.T)).astype(jnp.bfloat16)
    return (new_flat.reshape(GRID_ROWS, GRID_COLS, D), grad_flat.reshape(GRID_ROWS, GRID_COLS, D), grad_scale * grad_send, grad_scale * grad_recv, grad_scale * grad_edge_bias, grad_scale * grad_self, grad_scale * grad_agg, grad_scale * grad_node_bias, grad_scale * grad_out, grad_scale * grad_gain)
```

```python
import jax
import jax.numpy as jnp
from jax import lax
from jax.sharding import PartitionSpec as P

OFFSETS = ((1, 0), (-1, 0), (0, 1), (0, -1), (1, -1), (-1, 1))
epsilon = 1e-05


def extended(cells, sides, width):
    for axis, dim in sides:
        count = lax.axis_size(axis)
        head = lax.slice_in_dim(cells, 0, width, axis=dim)
        tail = lax.slice_in_dim(cells, cells.shape[dim] - width, cells.shape[dim], axis=dim)
        cells = jnp.concatenate(
            [
                lax.ppermute(tail, axis, [(i, (i + 1) % count) for i in range(count)]),
                cells,
                lax.ppermute(head, axis, [((i + 1) % count, i) for i in range(count)]),
            ],
            axis=dim,
        )
    return cells


def silu_slope(values):
    sigmoid = jax.nn.sigmoid(values)
    return sigmoid * (1.0 + values * (1.0 - sigmoid))


def matmul(left, right):
    return jnp.dot(left, right, preferred_element_type=jnp.float32)


def exchanged(values, axis, bit):
    count = lax.axis_size(axis)
    return lax.ppermute(values, axis, [(i, i ^ bit) for i in range(count)])


def scatter_sum(values, axis, place, steps):
    parts = values.reshape(len(steps) + 1, -1, values.shape[-1])
    total = parts[place].astype(jnp.float32)
    for rank, step in enumerate(steps):
        total = total + exchanged(parts[place ^ (rank + 1)], axis, step).astype(jnp.float32)
    return total.astype(jnp.bfloat16)


def gather_all(values, axis, place, steps):
    parts = jnp.stack([values] + [exchanged(values, axis, step) for step in steps])
    return parts[place ^ jnp.arange(len(steps) + 1)].reshape(-1, values.shape[-1])


def sum_everywhere(values):
    lat_steps = range(1, lax.axis_size("lat"))
    chip_steps = range(2, lax.axis_size("lon"), 2)
    lat_place = lax.axis_index("lat")
    core_place = lax.axis_index("lon") % 2
    chip_place = lax.axis_index("lon") // 2
    values = scatter_sum(values, "lon", core_place, (1,))
    values = scatter_sum(values, "lat", lat_place, lat_steps)
    values = scatter_sum(values, "lon", chip_place, chip_steps)
    values = gather_all(values, "lon", chip_place, chip_steps)
    values = gather_all(values, "lat", lat_place, lat_steps)
    return gather_all(values, "lon", core_place, (1,))


def on_device(
    nodes,
    cotangent,
    w_send,
    w_recv,
    edge_bias,
    w_self,
    w_agg,
    node_bias,
    w_out,
    gain,
    coarse_slots,
    long_senders,
    long_receivers,
):
    patch_rows, patch_cols, depth = nodes.shape
    patch_size = patch_rows * patch_cols
    lat_count = lax.axis_size("lat")
    lon_count = lax.axis_size("lon")
    grid_rows = patch_rows * lat_count
    grad_scale = float(patch_size * lat_count * lon_count) ** (-0.5)
    highest = lax.Precision.HIGHEST
    flat_nodes = nodes.reshape(patch_size, depth)
    send_flat = matmul(flat_nodes, w_send).astype(jnp.bfloat16)
    recv_flat = matmul(flat_nodes, w_recv)
    send_proj = send_flat.reshape(patch_rows, patch_cols, depth)
    recv_proj = recv_flat.reshape(patch_rows, patch_cols, depth)
    padded = extended(send_proj, (("lat", 0), ("lon", 1)), 1)
    grid_row = lax.axis_index("lat") * patch_rows + jnp.arange(patch_rows)

    def row_valid(lat_step):
        inside = (grid_row + lat_step >= 0) & (grid_row + lat_step < grid_rows)
        return inside.astype(jnp.float32)[:, None, None]

    def sender_of(lat_step, lon_step):
        window = padded[
            1 + lat_step : 1 + lat_step + patch_rows, 1 + lon_step : 1 + lon_step + patch_cols
        ]
        return window.astype(jnp.float32)

    fine_sum = jnp.zeros((patch_rows, patch_cols, depth), jnp.float32)
    for lat_step, lon_step in OFFSETS:
        fine_sum = fine_sum + row_valid(lat_step) * jax.nn.silu(
            sender_of(lat_step, lon_step) + recv_proj + edge_bias
        )
    coarse_pos = coarse_slots.reshape(-1)
    coarse_count = coarse_pos.shape[0]
    senders = long_senders.reshape(lon_count, -1)
    receivers = long_receivers.reshape(lon_count, -1)
    coarse_send = jnp.take(send_flat, coarse_pos, axis=0)
    coarse_recv = jnp.take(recv_flat, coarse_pos, axis=0)
    blocks = lax.all_gather(coarse_send, "lon", axis=0, tiled=True).reshape(
        lon_count, coarse_count, depth
    )
    edge_send = jnp.take_along_axis(blocks, senders[:, :, None], axis=1).astype(jnp.float32)
    edge_recv = jnp.take(coarse_recv, receivers, axis=0)
    pre_long = edge_send + edge_recv + edge_bias
    slot_ids = jnp.arange(coarse_count)
    recv_hot = (receivers[:, :, None] == slot_ids).astype(jnp.float32)
    send_hot = (senders[:, :, None] == slot_ids).astype(jnp.float32)
    coarse_sum = jnp.einsum("seb,sed->bd", recv_hot, jax.nn.silu(pre_long), precision=highest)
    total = fine_sum.reshape(patch_size, depth).at[coarse_pos].add(coarse_sum)
    gathered = total.astype(jnp.bfloat16)
    pre_node = matmul(flat_nodes, w_self) + matmul(gathered, w_agg) + node_bias
    hidden = jax.nn.silu(pre_node).astype(jnp.bfloat16)
    output = matmul(hidden, w_out)
    row_mean = jnp.mean(output, axis=-1, keepdims=True)
    centred = output - row_mean
    inv_std = lax.rsqrt(jnp.mean(centred * centred, axis=-1, keepdims=True) + epsilon)
    normed = centred * inv_std
    new_flat = (flat_nodes.astype(jnp.float32) + gain * normed).astype(jnp.bfloat16)
    cot_flat = cotangent.reshape(patch_size, depth).astype(jnp.float32)
    gain_grad = jnp.sum(cot_flat * normed, axis=0)
    d_norm = cot_flat * gain
    d_output = (
        inv_std
        * (
            d_norm
            - jnp.mean(d_norm, axis=-1, keepdims=True)
            - normed * jnp.mean(d_norm * normed, axis=-1, keepdims=True)
        )
    ).astype(jnp.bfloat16)
    out_grad = matmul(hidden.T, d_output)
    d_pre = matmul(d_output, w_out.T) * silu_slope(pre_node)
    node_bias_grad = jnp.sum(d_pre, axis=0)
    d_pre_b = d_pre.astype(jnp.bfloat16)
    self_grad = matmul(flat_nodes.T, d_pre_b)
    agg_grad = matmul(gathered.T, d_pre_b)
    d_sum_b = lax.optimization_barrier(matmul(d_pre_b, w_agg.T).astype(jnp.bfloat16))
    dsum_flat = d_sum_b.astype(jnp.float32)
    d_sum = dsum_flat.reshape(patch_rows, patch_cols, depth)
    beside_all = extended(
        jnp.stack([d_sum, recv_proj]).astype(jnp.bfloat16), (("lat", 1), ("lon", 2)), 1
    ).astype(jnp.float32)
    dsum_around = beside_all[0]
    recv_around = beside_all[1]
    own_send = send_proj.astype(jnp.float32)
    d_recv = jnp.zeros((patch_rows, patch_cols, depth), jnp.float32)
    d_send = jnp.zeros((patch_rows, patch_cols, depth), jnp.float32)
    edge_bias_grad = jnp.zeros((depth,), jnp.float32)
    for lat_step, lon_step in OFFSETS:
        slope_in = (
            row_valid(lat_step)
            * d_sum
            * silu_slope(sender_of(lat_step, lon_step) + recv_proj + edge_bias)
        )
        d_recv = d_recv + slope_in
        edge_bias_grad = edge_bias_grad + jnp.sum(slope_in, axis=(0, 1))
        far_dsum = dsum_around[
            1 - lat_step : 1 - lat_step + patch_rows, 1 - lon_step : 1 - lon_step + patch_cols
        ]
        far_recv = recv_around[
            1 - lat_step : 1 - lat_step + patch_rows, 1 - lon_step : 1 - lon_step + patch_cols
        ]
        d_send = d_send + row_valid(-lat_step) * far_dsum * silu_slope(
            own_send + far_recv + edge_bias
        )
    coarse_dsum = jnp.take(dsum_flat, coarse_pos, axis=0)
    slope_long = jnp.take(coarse_dsum, receivers, axis=0) * silu_slope(pre_long)
    edge_bias_grad = edge_bias_grad + jnp.sum(slope_long, axis=(0, 1))
    recv_long = jnp.einsum("seb,sed->bd", recv_hot, slope_long, precision=highest)
    block_grads = jnp.einsum("seb,sed->sbd", send_hot, slope_long, precision=highest)
    flat_grads = block_grads.reshape(lon_count * coarse_count, depth)
    send_long = lax.psum_scatter(
        flat_grads.astype(jnp.bfloat16), "lon", scatter_dimension=0, tiled=True
    ).astype(jnp.float32)
    d_recv_b = d_recv.reshape(patch_size, depth).at[coarse_pos].add(recv_long).astype(jnp.bfloat16)
    d_send_b = d_send.reshape(patch_size, depth).at[coarse_pos].add(send_long).astype(jnp.bfloat16)
    recv_grad = matmul(flat_nodes.T, d_recv_b)
    send_grad = matmul(flat_nodes.T, d_send_b)
    grad_flat = (
        cot_flat
        + matmul(d_pre_b, w_self.T)
        + matmul(d_recv_b, w_recv.T)
        + matmul(d_send_b, w_send.T)
    ).astype(jnp.bfloat16)
    vectors = jnp.stack([edge_bias_grad, node_bias_grad, gain_grad])
    stacked = jnp.concatenate([send_grad, recv_grad, self_grad, agg_grad, out_grad, vectors])
    multiple = 8 * lat_count * lon_count
    padding = -stacked.shape[0] % multiple
    stacked = jnp.pad(stacked.astype(jnp.bfloat16), ((0, padding), (0, 0)))
    summed = grad_scale * sum_everywhere(stacked).astype(jnp.float32)
    matrices = summed[: 5 * depth].reshape(5, depth, depth)
    rows = summed[5 * depth :]
    return (
        new_flat.reshape(patch_rows, patch_cols, depth),
        grad_flat.reshape(patch_rows, patch_cols, depth),
        matrices[0],
        matrices[1],
        rows[0],
        matrices[2],
        matrices[3],
        rows[1],
        matrices[4],
        rows[2],
    )


def solution(mesh):
    placed = (
        P("lat", "lon", None),
        P("lat", "lon", None),
        P(),
        P(),
        P(),
        P(),
        P(),
        P(),
        P(),
        P(),
        P("lat", "lon", None),
        P("lat", "lon", None, None),
        P("lat", "lon", None, None),
    )
    return jax.shard_map(
        on_device,
        mesh=mesh,
        in_specs=placed,
        out_specs=(
            P("lat", "lon", None),
            P("lat", "lon", None),
            P(),
            P(),
            P(),
            P(),
            P(),
            P(),
            P(),
            P(),
        ),
        check_vma=False,
    )
```

```python
import functools

import jax
import jax.numpy as jnp
from jax import lax
from jax.experimental import pallas as pl
from jax.experimental.pallas import tpu as pltpu
from jax.sharding import PartitionSpec as P

epsilon = 1e-05
EXACT = lax.Precision.HIGHEST
ABSENT = -1000.0
VMEM_BYTES = 60 * 1024 * 1024


def dot(left, right):
    return jnp.dot(left, right, preferred_element_type=jnp.float32)


def dot_nt(left, right):
    return lax.dot_general(left, right, (((1,), (1,)), ((), ())), preferred_element_type=jnp.float32)


def dot_tn(left, right):
    return lax.dot_general(left, right, (((0,), (0,)), ((), ())), preferred_element_type=jnp.float32)


def dot_exact(left, right):
    return jnp.dot(left, right, preferred_element_type=jnp.float32, precision=EXACT)


def to_bf16(values):
    return values.astype(jnp.bfloat16)


def to_f32(values):
    return values.astype(jnp.float32)


def half_sum_and_slope(half):
    curve = jnp.tanh(half)
    part = half * curve
    return half + part, (1.0 + curve) * (1.0 + half - part)


def eight_rows(values):
    return jnp.sum(values.reshape(-1, 8, values.shape[-1]), axis=0)


def aligned(start, multiple):
    return pl.multiple_of(start, multiple)


def project_kernel(nodes, w_send, w_recv, w_self, edge_bias, node_bias, send, recv_half, own):
    block = nodes[...]
    send[...] = to_bf16(dot(block, w_send[...]))
    recv_half[...] = 0.5 * (dot(block, w_recv[...]) + edge_bias[...])
    own[...] = dot(block, w_self[...]) + node_bias[...]


def project(nodes, w_send, w_recv, w_self, edge_bias, node_bias):
    rows, depth = nodes.shape
    step = 256
    whole = pl.BlockSpec((depth, depth), lambda i: (0, 0))
    vector = pl.BlockSpec((1, depth), lambda i: (0, 0))
    block = pl.BlockSpec((step, depth), lambda i: (i, 0))
    return pl.pallas_call(
        project_kernel,
        grid=(rows // step,),
        in_specs=[block, whole, whole, whole, vector, vector],
        out_specs=[block, block, block],
        out_shape=[
            jax.ShapeDtypeStruct((rows, depth), jnp.bfloat16),
            jax.ShapeDtypeStruct((rows, depth), jnp.float32),
            jax.ShapeDtypeStruct((rows, depth), jnp.float32),
        ],
        cost_estimate=pl.CostEstimate(
            flops=6 * rows * depth * depth, bytes_accessed=8_000_000, transcendentals=0
        ),
        name="project",
    )(nodes, w_send, w_recv, w_self, edge_bias, node_bias)


def update_kernel(
    dims,
    slots,
    facts,
    nodes,
    cotangent,
    send,
    recv_half,
    own,
    above,
    below,
    corner_above,
    corner_below,
    gathered,
    w_send,
    w_recv,
    w_agg,
    w_out,
    edge_bias,
    gain,
    send_col,
    send_row,
    recv_col,
    recv_row,
    new_nodes,
    d_pre_b,
    d_recv_b,
    d_send,
    d_up,
    d_down,
    d_corner_up,
    d_corner_down,
    d_gathered,
    grads_mine,
    grads_other,
    mid,
    right,
    left,
    slopes,
    slope_sum,
    total,
    work,
    agg_b,
    hidden_b,
    d_out_b,
    d_half,
    d_recv,
    far,
    far_d,
    near_nodes,
    near_d,
    sums,
    coarse,
    coarse_d,
):
    patch_rows, cols, lon_count, coarse_count, lat_count = dims
    rows = patch_rows * cols
    depth = nodes.shape[-1]
    pack = coarse_count + 2 * patch_rows
    top_valid, bottom_valid, right_at, left_at, core, lat = (facts[i] for i in range(6))
    tile = 16

    upper, lower = pl.ds(0, cols), pl.ds(cols, cols)
    corner_up, corner_down = pl.ds(2 * cols, 16), pl.ds(2 * cols + 16, 16)
    near_nodes[upper, :] = above[...]
    near_nodes[lower, :] = below[...]
    near_nodes[corner_up, :] = corner_above[...]
    near_nodes[corner_down, :] = corner_below[...]
    near_half = 0.5 * to_f32(to_bf16(dot(near_nodes[...], w_send[...])))
    far[...] = 0.5 * to_f32(to_bf16(dot(gathered[...], w_send[...])))
    sums[...] = jnp.zeros_like(sums)
    first = lax.broadcasted_iota(jnp.int32, (cols, 1), 0) == 0
    last = lax.broadcasted_iota(jnp.int32, (cols, 1), 0) == cols - 1
    top = jnp.where(top_valid == 1, near_half[:cols], ABSENT)
    bottom = jnp.where(bottom_valid == 1, near_half[cols : 2 * cols], ABSENT)
    top_corner = jnp.where(top_valid == 1, near_half[2 * cols : 2 * cols + 1], ABSENT)
    bottom_corner = jnp.where(
        bottom_valid == 1, near_half[2 * cols + 31 : 2 * cols + 32], ABSENT
    )
    mid[pl.ds(0, cols), :] = top
    mid[pl.ds(rows + cols, cols), :] = bottom
    right[pl.ds(0, cols), :] = jnp.where(last, top_corner, pltpu.roll(top, cols - 1, 0))
    left[pl.ds(rows + cols, cols), :] = jnp.where(first, bottom_corner, pltpu.roll(bottom, 1, 0))

    right_edge = far[pl.ds(aligned(right_at + coarse_count, 16), patch_rows), :]
    left_edge = far[pl.ds(aligned(left_at + coarse_count + patch_rows, 16), patch_rows), :]
    for row in range(patch_rows):
        here, there = pl.ds(row * cols, cols), pl.ds((row + 1) * cols, cols)
        for lane in range(0, depth, 128):
            lanes = pl.ds(lane, 128)
            block = 0.5 * to_f32(send[here, lanes])
            mid[there, lanes] = block
            edge = right_edge[row : row + 1, lane : lane + 128]
            right[there, lanes] = jnp.where(last, edge, pltpu.roll(block, cols - 1, 0))
            edge = left_edge[row : row + 1, lane : lane + 128]
            left[there, lanes] = jnp.where(first, edge, pltpu.roll(block, 1, 0))

    senders = ((mid, 2), (mid, 0), (right, 1), (left, 1), (left, 2), (right, 0))

    def edges(step, carry):
        base = aligned(step * tile, tile)
        here = pl.ds(base, tile)
        recv = recv_half[here, :]
        summed = jnp.zeros((tile, depth), jnp.float32)
        slope_total = jnp.zeros((tile, depth), jnp.float32)
        for which, (source, shift) in enumerate(senders):
            half = source[pl.ds(aligned(base + shift * cols, tile), tile), :] + recv
            value, slope = half_sum_and_slope(half)
            summed = summed + value
            slope_total = slope_total + slope
            slopes[which, pl.ds(aligned(base + cols, tile), tile), :] = to_bf16(slope)
        total[here, :] = summed
        slope_sum[here, :] = slope_total
        return carry

    lax.fori_loop(0, rows // tile, edges, 0)

    edge_count = send_col.shape[0]
    for source in range(lon_count):
        coarse[pl.ds(source * coarse_count, coarse_count), :] = far[
            pl.ds(source * pack, coarse_count), :
        ]
    coarse_ids = lon_count * coarse_count
    send_hot = to_f32(
        send_col[...] == lax.broadcasted_iota(jnp.int32, (edge_count, coarse_ids), 1)
    )
    send_hot_t = to_f32(
        send_row[...] == lax.broadcasted_iota(jnp.int32, (coarse_ids, edge_count), 0)
    )
    recv_hot = to_f32(
        recv_col[...] == lax.broadcasted_iota(jnp.int32, (edge_count, coarse_count), 1)
    )
    recv_hot_t = to_f32(
        recv_row[...] == lax.broadcasted_iota(jnp.int32, (coarse_count, edge_count), 0)
    )
    coarse_recv = 0.5 * (dot(gathered[pl.ds(0, coarse_count), :], w_recv[...]) + edge_bias[...])
    long_half = dot_exact(send_hot, coarse[...]) + dot_exact(recv_hot, coarse_recv)
    long_value, long_slope = half_sum_and_slope(long_half)
    coarse_d[...] = dot_exact(recv_hot_t, long_value)
    for k in range(coarse_count):
        spot = pl.ds(slots[k], 1)
        total[spot, :] = total[spot, :] + coarse_d[pl.ds(k, 1), :]

    step_rows = 256
    blocks = [pl.ds(start, step_rows) for start in range(0, rows, step_rows)]
    for block in blocks:
        agg_b[block, :] = to_bf16(total[block, :])
        work[block, :] = 0.5 * (own[block, :] + dot(agg_b[block, :], w_agg[...]))

    def activate(step, carry):
        here = pl.ds(aligned(step * tile, tile), tile)
        half = work[here, :]
        hidden_b[here, :] = to_bf16(half + half * jnp.tanh(half))
        return carry

    lax.fori_loop(0, rows // tile, activate, 0)
    for block in blocks:
        total[block, :] = dot(hidden_b[block, :], w_out[...])

    wide = 32

    def normalise(step, carry):
        here = pl.ds(aligned(step * wide, wide), wide)
        output = total[here, :]
        cot = to_f32(cotangent[here, :])
        d_norm = cot * gain[...]
        d_mean = jnp.mean(d_norm, axis=-1, keepdims=True)
        centred = output - jnp.mean(output, axis=-1, keepdims=True)
        inv_std = lax.rsqrt(jnp.mean(centred * centred, axis=-1, keepdims=True) + epsilon)
        normed = centred * inv_std
        new_nodes[here, :] = to_bf16(to_f32(nodes[here, :]) + gain[...] * normed)
        sums[2] += eight_rows(cot * normed)
        d_dot = jnp.mean(d_norm * normed, axis=-1, keepdims=True)
        d_out_b[here, :] = to_bf16(inv_std * (d_norm - d_mean - normed * d_dot))
        return carry

    lax.fori_loop(0, rows // wide, normalise, 0, unroll=2)

    for block in blocks:
        total[block, :] = dot_nt(d_out_b[block, :], w_out[...])

    def deactivate(step, carry):
        here = pl.ds(aligned(step * tile, tile), tile)
        slope = half_sum_and_slope(work[here, :])[1]
        d_pre = total[here, :] * (0.5 * slope)
        sums[1] += eight_rows(d_pre)
        d_pre_b[here, :] = to_bf16(d_pre)
        return carry

    lax.fori_loop(0, rows // tile, deactivate, 0)
    share = depth // (2 * lat_count)

    def put(which, half_at, values):
        block = to_bf16(values)
        for grads, core_at in ((grads_mine, half_at), (grads_other, 1 - half_at)):

            @pl.when(core == core_at)
            def _():
                for place in range(lat_count):
                    grads[lat ^ place, pl.ds(which * share, share), :] = block[
                        place * share : (place + 1) * share
                    ]

    for half_at in range(2):
        columns = pl.ds(half_at * (depth // 2), depth // 2)
        put(2, half_at, dot_tn(nodes[:, columns], d_pre_b[...]))
        put(3, half_at, dot_tn(agg_b[:, columns], d_pre_b[...]))
        put(4, half_at, dot_tn(hidden_b[:, columns], d_out_b[...]))
    d_half[pl.ds(0, cols), :] = jnp.zeros((cols, depth), jnp.float32)
    d_half[pl.ds(rows + cols, cols), :] = jnp.zeros((cols, depth), jnp.float32)
    for which in (0, 4):
        slopes[which, pl.ds(0, cols), :] = jnp.zeros((cols, depth), jnp.bfloat16)
    for which in (1, 5):
        slopes[which, pl.ds(rows + cols, cols), :] = jnp.zeros((cols, depth), jnp.bfloat16)
    for start in range(0, rows, step_rows):
        d_sum = dot_nt(d_pre_b[pl.ds(start, step_rows), :], w_agg[...])
        d_half[pl.ds(start + cols, step_rows), :] = 0.5 * to_f32(to_bf16(d_sum))

    def slope_times(which, place, lanes):
        return to_f32(slopes[which, place, lanes]) * d_half[place, lanes]

    def receive(step, carry):
        base = aligned(step * tile, tile)
        here = pl.ds(base, tile)
        value = d_half[pl.ds(aligned(base + cols, tile), tile), :] * slope_sum[here, :]
        d_recv[here, :] = value
        sums[0] += eight_rows(value)
        return carry

    lax.fori_loop(0, rows // tile, receive, 0)
    far_d[...] = jnp.zeros_like(far_d)

    edge_place = lax.broadcasted_iota(jnp.int32, (patch_rows, 1), 0)
    for lane in range(0, depth, 128):
        lanes = pl.ds(lane, 128)
        right_edge = jnp.zeros((patch_rows, 128), jnp.float32)
        left_edge = jnp.zeros((patch_rows, 128), jnp.float32)
        for row in range(patch_rows):
            above_row, out = pl.ds(row * cols, cols), pl.ds(row * cols, cols)
            here, below_row = pl.ds((row + 1) * cols, cols), pl.ds((row + 2) * cols, cols)
            to_mid = slope_times(0, above_row, lanes) + slope_times(1, below_row, lanes)
            to_right = slope_times(2, here, lanes) + slope_times(5, below_row, lanes)
            to_left = slope_times(3, here, lanes) + slope_times(4, above_row, lanes)
            d_send[out, lanes] = (
                to_mid
                + jnp.where(first, 0.0, pltpu.roll(to_right, 1, 0))
                + jnp.where(last, 0.0, pltpu.roll(to_left, cols - 1, 0))
            )
            right_edge = jnp.where(edge_place == row, to_right[cols - 1 : cols], right_edge)
            left_edge = jnp.where(edge_place == row, to_left[0:1], left_edge)
        far_d[pl.ds(aligned(right_at + coarse_count, 16), patch_rows), lanes] = right_edge
        far_d[pl.ds(aligned(left_at + coarse_count + patch_rows, 16), patch_rows), lanes] = left_edge
    row_first, row_last = pl.ds(cols, cols), pl.ds(rows, cols)
    for lane in range(0, depth, 128):
        lanes = pl.ds(lane, 128)
        to_right = slope_times(5, row_first, lanes)
        to_left = slope_times(4, row_last, lanes)
        up = slope_times(1, row_first, lanes) + jnp.where(first, 0.0, pltpu.roll(to_right, 1, 0))
        down = slope_times(0, row_last, lanes) + jnp.where(
            last, 0.0, pltpu.roll(to_left, cols - 1, 0)
        )
        sixteen = lax.broadcasted_iota(jnp.int32, (16, 1), 0)
        near_d[upper, lanes] = to_bf16(up)
        near_d[lower, lanes] = to_bf16(down)
        near_d[corner_up, lanes] = to_bf16(
            jnp.where(sixteen == 0, to_right[cols - 1 : cols], 0.0)
        )
        near_d[corner_down, lanes] = to_bf16(jnp.where(sixteen == 15, to_left[0:1], 0.0))
    d_up[...] = near_d[upper, :]
    d_down[...] = near_d[lower, :]
    d_corner_up[...] = near_d[corner_up, :]
    d_corner_down[...] = near_d[corner_down, :]

    for k in range(coarse_count):
        coarse_d[pl.ds(k, 1), :] = d_half[pl.ds(slots[k] + cols, 1), :]
    long_d = dot_exact(recv_hot, coarse_d[...]) * long_slope
    sums[0] += eight_rows(long_d)
    coarse_d[...] = dot_exact(recv_hot_t, long_d)
    for k in range(coarse_count):
        spot = pl.ds(slots[k], 1)
        d_recv[spot, :] = d_recv[spot, :] + coarse_d[pl.ds(k, 1), :]
    coarse[...] = dot_exact(send_hot_t, long_d)
    for source in range(lon_count):
        far_d[pl.ds(source * pack, coarse_count), :] = coarse[
            pl.ds(source * coarse_count, coarse_count), :
        ]
    d_gathered[...] = to_bf16(far_d[...])
    for block in blocks:
        d_recv_b[block, :] = to_bf16(d_recv[block, :])
        agg_b[block, :] = to_bf16(d_send[block, :])
    for half_at in range(2):
        columns = pl.ds(half_at * (depth // 2), depth // 2)
        put(0, half_at, dot_tn(nodes[:, columns], agg_b[...])
            + dot_tn(near_nodes[:, columns], near_d[...])
            + dot_tn(gathered[:, columns], d_gathered[...]))
        put(1, half_at, dot_tn(nodes[:, columns], d_recv_b[...]))
    place = lax.broadcasted_iota(jnp.int32, (16, depth), 0)
    vectors = jnp.zeros((16, depth), jnp.float32)
    for which in range(3):
        vectors = jnp.where(place == which, jnp.sum(sums[which], axis=0, keepdims=True), vectors)
    for spot in range(lat_count):
        grads_mine[spot, pl.ds(5 * share, 16), :] = to_bf16(vectors)
        grads_other[spot, pl.ds(5 * share, 16), :] = to_bf16(vectors)


def update(dims, ints, arrays):
    patch_rows, cols, lon_count, coarse_count, lat_count = dims
    rows, depth = arrays[0].shape
    share = depth // (2 * lat_count)
    far_rows = lon_count * (coarse_count + 2 * patch_rows)
    long_rows = rows + 2 * cols
    shape = jax.ShapeDtypeStruct
    scratch = lambda *size, kind=jnp.float32: pltpu.VMEM(size, kind)
    smem, vmem = pl.BlockSpec(memory_space=pltpu.SMEM), pl.BlockSpec(memory_space=pltpu.VMEM)
    return pl.pallas_call(
        functools.partial(update_kernel, dims),
        in_specs=[smem] * 2 + [vmem] * len(arrays),
        out_specs=[vmem] * 11,
        out_shape=[
            shape((rows, depth), jnp.bfloat16),
            shape((rows, depth), jnp.bfloat16),
            shape((rows, depth), jnp.bfloat16),
            shape((rows, depth), jnp.float32),
            shape((cols, depth), jnp.bfloat16),
            shape((cols, depth), jnp.bfloat16),
            shape((16, depth), jnp.bfloat16),
            shape((16, depth), jnp.bfloat16),
            shape((far_rows, depth), jnp.bfloat16),
            shape((lat_count, 5 * share + 16, depth), jnp.bfloat16),
            shape((lat_count, 5 * share + 16, depth), jnp.bfloat16),
        ],
        scratch_shapes=[
            scratch(long_rows, depth),
            scratch(long_rows, depth),
            scratch(long_rows, depth),
            scratch(6, long_rows, depth, kind=jnp.bfloat16),
            scratch(rows, depth),
            scratch(rows, depth),
            scratch(rows, depth),
            scratch(rows, depth, kind=jnp.bfloat16),
            scratch(rows, depth, kind=jnp.bfloat16),
            scratch(rows, depth, kind=jnp.bfloat16),
            scratch(long_rows, depth),
            scratch(rows, depth),
            scratch(far_rows, depth),
            scratch(far_rows, depth),
            scratch(2 * cols + 32, depth, kind=jnp.bfloat16),
            scratch(2 * cols + 32, depth, kind=jnp.bfloat16),
            scratch(3, 8, depth),
            scratch(lon_count * coarse_count, depth),
            scratch(coarse_count, depth),
        ],
        compiler_params=pltpu.CompilerParams(vmem_limit_bytes=VMEM_BYTES),
        cost_estimate=pl.CostEstimate(
            flops=20 * rows * depth * depth, bytes_accessed=20_000_000, transcendentals=0
        ),
        name="update",
    )(*ints, *arrays)


def finish_kernel(
    dims,
    slots,
    cotangent,
    d_pre_b,
    d_recv_b,
    d_send,
    from_below,
    from_above,
    corner_below,
    corner_above,
    back,
    w_self,
    w_recv,
    w_send,
    grad_nodes,
    total,
):
    patch_rows, cols, _, coarse_count, _ = dims
    rows = patch_rows * cols
    step_rows = 256
    for start in range(0, rows, step_rows):
        block = pl.ds(start, step_rows)
        total[block, :] = d_send[block, :]
    for start, part in (
        (rows - cols, from_below),
        (0, from_above),
        (rows - cols, corner_below),
        (cols - 16, corner_above),
    ):
        block = pl.ds(start, part.shape[0])
        total[block, :] = total[block, :] + to_f32(part[...])
    returned = to_f32(back[...])
    for row in range(patch_rows):
        for spot, at in ((row * cols, 0), (row * cols + cols - 1, patch_rows)):
            one = coarse_count + at + row
            total[pl.ds(spot, 1), :] = total[pl.ds(spot, 1), :] + returned[one : one + 1]
    for k in range(coarse_count):
        spot = pl.ds(slots[k], 1)
        total[spot, :] = total[spot, :] + returned[k : k + 1]
    for start in range(0, rows, step_rows):
        block = pl.ds(start, step_rows)
        grad_nodes[block, :] = to_bf16(
            to_f32(cotangent[block, :])
            + dot_nt(d_pre_b[block, :], w_self[...])
            + dot_nt(d_recv_b[block, :], w_recv[...])
            + dot_nt(to_bf16(total[block, :]), w_send[...])
        )


def finish(dims, slots, arrays):
    rows, depth = arrays[0].shape
    smem, vmem = pl.BlockSpec(memory_space=pltpu.SMEM), pl.BlockSpec(memory_space=pltpu.VMEM)
    return pl.pallas_call(
        functools.partial(finish_kernel, dims),
        in_specs=[smem] + [vmem] * len(arrays),
        out_specs=vmem,
        out_shape=jax.ShapeDtypeStruct((rows, depth), jnp.bfloat16),
        scratch_shapes=[pltpu.VMEM((rows, depth), jnp.float32)],
        compiler_params=pltpu.CompilerParams(vmem_limit_bytes=VMEM_BYTES),
        cost_estimate=pl.CostEstimate(
            flops=6 * rows * depth * depth, bytes_accessed=8_000_000, transcendentals=0
        ),
        name="finish",
    )(slots, *arrays)


def swapped(values, axis, bit):
    count = lax.axis_size(axis)
    return lax.ppermute(values, axis, [(i, i ^ bit) for i in range(count)])


def summed_shares(mine, other):
    lat_count, _, depth = mine.shape
    chip_count = lax.axis_size("lon") // 2
    chip = lax.axis_index("lon") // 2
    share = depth // (2 * lat_count)
    own = to_bf16(to_f32(mine) + to_f32(swapped(other, "lon", 1)))
    total = to_f32(own[0])
    for step in range(1, lat_count):
        total = total + to_f32(swapped(own[step], "lat", step))
    total = to_bf16(total)
    vectors = total[5 * share :]
    parts = total[: 5 * share].reshape(5, chip_count, share // chip_count, depth)

    def part_of(place):
        part = lax.dynamic_index_in_dim(parts, place, axis=1, keepdims=False)
        return jnp.concatenate([part.reshape(-1, depth), vectors])

    total = to_f32(part_of(chip))
    for step in range(1, chip_count):
        total = total + to_f32(swapped(part_of(chip ^ step), "lon", 2 * step))
    part = to_bf16(total[:-16])
    parts = jnp.stack([part] + [swapped(part, "lon", 2 * k) for k in range(1, chip_count)])
    parts = parts[chip ^ jnp.arange(chip_count)].reshape(chip_count, 5, -1, depth)
    ready = jnp.transpose(parts, (1, 0, 2, 3)).reshape(5 * share, depth)
    shares = [ready] + [swapped(ready, "lat", step) for step in range(1, lat_count)]
    return shares + [swapped(part, "lon", 1) for part in shares], total[-16:]


def unpack_kernel(lat_count, scale, facts, vectors, *refs):
    shares, outs = refs[: 2 * lat_count], refs[2 * lat_count :]
    depth = vectors.shape[-1]
    share = depth // (2 * lat_count)
    core, lat = facts[4], facts[5]
    for flip in range(2):
        for step in range(lat_count):
            start = (core ^ flip) * (depth // 2) + (lat ^ step) * share
            place = pl.ds(aligned(start, share), share)
            for which in range(5):
                block = shares[flip * lat_count + step][pl.ds(which * share, share), :]
                outs[which][place, :] = scale * to_f32(block)
    for which in range(3):
        outs[5 + which][...] = scale * vectors[pl.ds(which, 1), :]


def unpack(lat_count, scale, facts, vectors, shares):
    depth = vectors.shape[-1]
    smem, vmem = pl.BlockSpec(memory_space=pltpu.SMEM), pl.BlockSpec(memory_space=pltpu.VMEM)
    shape = jax.ShapeDtypeStruct
    return pl.pallas_call(
        functools.partial(unpack_kernel, lat_count, scale),
        in_specs=[smem] + [vmem] * (1 + len(shares)),
        out_specs=[vmem] * 8,
        out_shape=[shape((depth, depth), jnp.float32)] * 5 + [shape((1, depth), jnp.float32)] * 3,
        compiler_params=pltpu.CompilerParams(vmem_limit_bytes=VMEM_BYTES),
        name="unpack",
    )(facts, vectors, *shares)


def on_device(
    nodes,
    cotangent,
    w_send,
    w_recv,
    edge_bias,
    w_self,
    w_agg,
    node_bias,
    w_out,
    gain,
    coarse_slots,
    long_senders,
    long_receivers,
):
    patch_rows, cols, depth = nodes.shape
    rows = patch_rows * cols
    lat_count, lon_count = lax.axis_size("lat"), lax.axis_size("lon")
    chip_count = lon_count // 2
    lat, lon = lax.axis_index("lat"), lax.axis_index("lon")
    scale = float(rows * lat_count * lon_count) ** (-0.5)
    slots = coarse_slots.reshape(-1)
    coarse_count = slots.shape[0]
    dims = (patch_rows, cols, lon_count, coarse_count, lat_count)
    flat = nodes.reshape(rows, depth)
    cot = cotangent.reshape(rows, depth)

    down = [(i, i + 1) for i in range(lat_count - 1)]
    up = [(i + 1, i) for i in range(lat_count - 1)]

    def number(lat_place, lon_place):
        return lat_place * lon_count + lon_place % lon_count

    lats, lons = range(lat_count), range(lon_count)
    down_left = [(number(i, j), number(i + 1, j - 1)) for i in lats[:-1] for j in lons]
    up_right = [(number(i, j), number(i - 1, j + 1)) for i in lats[1:] for j in lons]
    above = lax.ppermute(flat[-cols:], "lat", down)
    below = lax.ppermute(flat[:cols], "lat", up)
    corner_above = lax.ppermute(flat[-cols : 16 - cols], ("lat", "lon"), down_left)
    corner_below = lax.ppermute(flat[cols - 16 : cols], ("lat", "lon"), up_right)
    packed = jnp.concatenate([flat[slots], nodes[:, 0], nodes[:, -1]])
    chips = [packed] + [swapped(packed, "lon", 2 * k) for k in range(1, chip_count)]
    chips = jnp.concatenate(chips)
    gathered = jnp.concatenate([chips, swapped(chips, "lon", 1)])

    def place_of(other):
        apart = other ^ lon
        return (apart % 2) * chip_count + apart // 2

    pack = packed.shape[0]
    facts = jnp.stack(
        [
            (lat > 0).astype(jnp.int32),
            (lat < lat_count - 1).astype(jnp.int32),
            place_of((lon + 1) % lon_count) * pack,
            place_of((lon + lon_count - 1) % lon_count) * pack,
            lon % 2,
            lat,
        ]
    ).astype(jnp.int32)
    sources = place_of(jnp.arange(lon_count))[:, None]
    sender_ids = (long_senders.reshape(lon_count, -1) + sources * coarse_count).reshape(-1)
    receiver_ids = long_receivers.reshape(-1)

    send, recv_half, own = project(
        flat, w_send, w_recv, w_self, edge_bias[None], node_bias[None]
    )
    (
        new_nodes,
        d_pre_b,
        d_recv_b,
        d_send,
        d_up,
        d_down,
        d_corner_up,
        d_corner_down,
        d_gathered,
        grads_mine,
        grads_other,
    ) = update(
        dims,
        (slots, facts),
        (
            flat,
            cot,
            send,
            recv_half,
            own,
            above,
            below,
            corner_above,
            corner_below,
            gathered,
            w_send,
            w_recv,
            w_agg,
            w_out,
            edge_bias[None],
            gain[None],
            sender_ids[:, None],
            sender_ids[None],
            receiver_ids[:, None],
            receiver_ids[None],
        ),
    )
    shares, vectors = summed_shares(grads_mine, grads_other)

    from_below = lax.ppermute(d_up, "lat", up)
    from_above = lax.ppermute(d_down, "lat", down)
    at_corner_below = lax.ppermute(d_corner_up, ("lat", "lon"), up_right)
    at_corner_above = lax.ppermute(d_corner_down, ("lat", "lon"), down_left)
    half = chip_count * pack
    chips = to_bf16(to_f32(d_gathered[:half]) + to_f32(swapped(d_gathered[half:], "lon", 1)))
    back = to_f32(chips[:pack])
    for k in range(1, chip_count):
        back = back + to_f32(swapped(chips[k * pack : (k + 1) * pack], "lon", 2 * k))
    grad_nodes = finish(
        dims,
        slots,
        (
            cot,
            d_pre_b,
            d_recv_b,
            d_send,
            from_below,
            from_above,
            at_corner_below,
            at_corner_above,
            back,
            w_self,
            w_recv,
            w_send,
        ),
    )
    outs = unpack(lat_count, scale, facts, vectors, shares)
    return (
        new_nodes.reshape(patch_rows, cols, depth),
        grad_nodes.reshape(patch_rows, cols, depth),
        outs[0],
        outs[1],
        outs[5][0],
        outs[2],
        outs[3],
        outs[6][0],
        outs[4],
        outs[7][0],
    )


def solution(mesh):
    patches = P("lat", "lon", None)
    edges = P("lat", "lon", None, None)
    return jax.shard_map(
        on_device,
        mesh=mesh,
        in_specs=(patches, patches) + (P(),) * 8 + (patches, edges, edges),
        out_specs=(patches, patches) + (P(),) * 8,
        check_vma=False,
    )
```

```python
import functools

import jax
import jax.numpy as jnp
from jax import lax
from jax.experimental import pallas as pl
from jax.experimental.pallas import tpu as pltpu
from jax.sharding import PartitionSpec as P

epsilon = 1e-05
EXACT = lax.Precision.HIGHEST
ABSENT = -1000.0
VMEM_BYTES = 60 * 1024 * 1024


def dot(left, right):
    return jnp.dot(left, right, preferred_element_type=jnp.float32)


def dot_nt(left, right):
    return lax.dot_general(left, right, (((1,), (1,)), ((), ())), preferred_element_type=jnp.float32)


def dot_tn(left, right):
    return lax.dot_general(left, right, (((0,), (0,)), ((), ())), preferred_element_type=jnp.float32)


def dot_exact(left, right):
    return jnp.dot(left, right, preferred_element_type=jnp.float32, precision=EXACT)


def dot_exact_tn(left, right):
    return lax.dot_general(
        left, right, (((0,), (0,)), ((), ())), preferred_element_type=jnp.float32, precision=EXACT
    )


def to_bf16(values):
    return values.astype(jnp.bfloat16)


def to_f32(values):
    return values.astype(jnp.float32)


def half_sum_and_slope(half):
    curve = jnp.tanh(half)
    part = half * curve
    return half + part, (1.0 + curve) * (1.0 + half - part)


def eight_rows(values):
    return jnp.sum(values.reshape(-1, 8, values.shape[-1]), axis=0)


def aligned(start, multiple):
    return pl.multiple_of(start, multiple)


def pack_kernel(cols, slots, nodes, above, below, packed):
    rows = nodes.shape[0]
    count, patch_rows = slots.shape[0], rows // cols
    size = count + 2 * patch_rows
    place = lax.broadcasted_iota(jnp.int32, (size, 1), 0)
    wanted = jnp.where(
        place < count + patch_rows,
        (place - count) * cols,
        (place - count - patch_rows) * cols + cols - 1,
    )
    for k in range(count):
        wanted = jnp.where(place == k, slots[k], wanted)
    column = lax.broadcasted_iota(jnp.int32, (size, rows), 1)
    packed[pl.ds(0, size), :] = to_bf16(dot(to_bf16(to_f32(column == wanted)), nodes[...]))
    place = lax.broadcasted_iota(jnp.int32, (16, 1), 0)
    top = to_f32(above[pl.ds(0, 16), :])[0:1]
    bottom = to_f32(below[pl.ds(cols - 16, 16), :])[15:16]
    corners = jnp.where(place == 0, top, jnp.where(place == 1, bottom, 0.0))
    packed[pl.ds(size, 16), :] = to_bf16(corners)


def pack_nodes(cols, slots, nodes, above, below):
    rows, depth = nodes.shape
    count = slots.shape[0] + 2 * (rows // cols) + 16
    smem, vmem = pl.BlockSpec(memory_space=pltpu.SMEM), pl.BlockSpec(memory_space=pltpu.VMEM)
    return pl.pallas_call(
        functools.partial(pack_kernel, cols),
        in_specs=[smem, vmem, vmem, vmem],
        out_specs=vmem,
        out_shape=jax.ShapeDtypeStruct((count, depth), jnp.bfloat16),
        name="pack_nodes",
    )(slots, nodes, above, below)


def project_send_kernel(nodes, w_send, send):
    send[...] = to_bf16(dot(nodes[...], w_send[...]))


def project_own_kernel(nodes, w_recv, w_self, edge_bias, node_bias, recv_half, own):
    block = nodes[...]
    recv_half[...] = 0.5 * (dot(block, w_recv[...]) + edge_bias[...])
    own[...] = dot(block, w_self[...]) + node_bias[...]


def project(kernel, name, nodes, weights, vectors, kinds):
    rows, depth = nodes.shape
    step = 256
    whole = pl.BlockSpec((depth, depth), lambda i: (0, 0))
    vector = pl.BlockSpec((1, depth), lambda i: (0, 0))
    block = pl.BlockSpec((step, depth), lambda i: (i, 0))
    return pl.pallas_call(
        kernel,
        grid=(rows // step,),
        in_specs=[block] + [whole] * len(weights) + [vector] * len(vectors),
        out_specs=[block] * len(kinds),
        out_shape=[jax.ShapeDtypeStruct((rows, depth), kind) for kind in kinds],
        cost_estimate=pl.CostEstimate(
            flops=2 * len(weights) * rows * depth * depth,
            bytes_accessed=4_000_000 * len(weights),
            transcendentals=0,
        ),
        name=name,
    )(nodes, *weights, *vectors)


def update_kernel(
    dims,
    slots,
    long_senders,
    long_receivers,
    nodes,
    cotangent,
    send,
    recv_half,
    own,
    above,
    below,
    gathered,
    crossed,
    w_send,
    w_recv,
    w_agg,
    w_out,
    edge_bias,
    gain,
    new_nodes,
    d_pre_b,
    d_recv_b,
    d_send,
    d_up,
    d_down,
    d_gathered,
    d_crossed,
    *rest,
):
    patch_rows, cols, lon_count, coarse_count, lat_count = dims
    outs, rest = rest[: 2 * lat_count], rest[2 * lat_count :]
    (
        mid,
        right,
        left,
        slopes,
        slope_sum,
        total,
        work,
        agg_b,
        hidden_b,
        d_out_b,
        d_half,
        far,
        far_d,
        near_nodes,
        near_d,
        sums,
        coarse,
        coarse_d,
        send_hot,
        recv_hot,
        grads,
        out_sems,
    ) = rest
    rows = patch_rows * cols
    depth = nodes.shape[-1]
    pack = coarse_count + 2 * patch_rows + 16
    chip_count = lon_count // 2
    lat, lon = lax.axis_index("lat"), lax.axis_index("lon")
    core = lon % 2
    top_valid, bottom_valid = lat > 0, lat < lat_count - 1

    def place_of(other):
        apart = other ^ lon
        return (apart % 2) * chip_count + apart // 2

    right_at = place_of((lon + 1) % lon_count) * pack
    left_at = place_of((lon + lon_count - 1) % lon_count) * pack
    tile = 16

    upper, lower = pl.ds(0, cols), pl.ds(cols, cols)
    near_nodes[upper, :] = above[...]
    near_nodes[lower, :] = below[...]
    near_half = 0.5 * to_f32(to_bf16(dot(near_nodes[...], w_send[...])))
    half_far = chip_count * pack
    same, cross = pl.ds(0, half_far), pl.ds(half_far, half_far)
    far[same, :] = 0.5 * to_f32(to_bf16(dot(gathered[...], w_send[...])))
    far[cross, :] = 0.5 * to_f32(to_bf16(dot(crossed[...], w_send[...])))
    sums[...] = jnp.zeros_like(sums)
    first = lax.broadcasted_iota(jnp.int32, (cols, 1), 0) == 0
    last = lax.broadcasted_iota(jnp.int32, (cols, 1), 0) == cols - 1
    top = jnp.where(top_valid, near_half[:cols], ABSENT)
    bottom = jnp.where(bottom_valid, near_half[cols : 2 * cols], ABSENT)
    corner_at = pack - 16
    right_corners = far[pl.ds(aligned(right_at + corner_at, 16), 16), :]
    left_corners = far[pl.ds(aligned(left_at + corner_at, 16), 16), :]
    top_corner = jnp.where(top_valid, right_corners[0:1], ABSENT)
    bottom_corner = jnp.where(bottom_valid, left_corners[1:2], ABSENT)
    mid[pl.ds(0, cols), :] = top
    mid[pl.ds(rows + cols, cols), :] = bottom
    right[pl.ds(0, cols), :] = jnp.where(last, top_corner, pltpu.roll(top, cols - 1, 0))
    left[pl.ds(rows + cols, cols), :] = jnp.where(first, bottom_corner, pltpu.roll(bottom, 1, 0))

    right_edge = far[pl.ds(aligned(right_at + coarse_count, 16), patch_rows), :]
    left_edge = far[pl.ds(aligned(left_at + coarse_count + patch_rows, 16), patch_rows), :]
    for row in range(patch_rows):
        here, there = pl.ds(row * cols, cols), pl.ds((row + 1) * cols, cols)
        for lane in range(0, depth, 128):
            lanes = pl.ds(lane, 128)
            block = 0.5 * to_f32(send[here, lanes])
            mid[there, lanes] = block
            edge = right_edge[row : row + 1, lane : lane + 128]
            right[there, lanes] = jnp.where(last, edge, pltpu.roll(block, cols - 1, 0))
            edge = left_edge[row : row + 1, lane : lane + 128]
            left[there, lanes] = jnp.where(first, edge, pltpu.roll(block, 1, 0))

    senders = ((mid, 2), (mid, 0), (right, 1), (left, 1), (left, 2), (right, 0))

    def edges(step, carry):
        base = aligned(step * tile, tile)
        here = pl.ds(base, tile)
        recv = recv_half[here, :]
        summed = jnp.zeros((tile, depth), jnp.float32)
        slope_total = jnp.zeros((tile, depth), jnp.float32)
        for which, (source, shift) in enumerate(senders):
            half = source[pl.ds(aligned(base + shift * cols, tile), tile), :] + recv
            value, slope = half_sum_and_slope(half)
            summed = summed + value
            slope_total = slope_total + slope
            slopes[which, pl.ds(aligned(base + cols, tile), tile), :] = to_bf16(slope)
        total[here, :] = summed
        slope_sum[here, :] = slope_total
        return carry

    lax.fori_loop(0, rows // tile, edges, 0)

    per_source = long_senders.shape[1]
    coarse_lane = lax.broadcasted_iota(jnp.int32, (1, coarse.shape[0]), 1)
    slot_lane = lax.broadcasted_iota(jnp.int32, (1, coarse_count), 1)
    for source in range(lon_count):
        first_id = place_of(source) * coarse_count
        for edge in range(per_source):
            row = pl.ds(source * per_source + edge, 1)
            send_hot[row, :] = to_f32(coarse_lane == first_id + long_senders[source, edge])
            recv_hot[row, :] = to_f32(slot_lane == long_receivers[source, edge])
    for source in range(lon_count):
        coarse[pl.ds(source * coarse_count, coarse_count), :] = far[
            pl.ds(source * pack, coarse_count), :
        ]
    coarse_recv = 0.5 * (dot(gathered[pl.ds(0, coarse_count), :], w_recv[...]) + edge_bias[...])
    long_half = dot_exact(send_hot[...], coarse[...]) + dot_exact(
        recv_hot[...], coarse_recv
    )
    long_value, long_slope = half_sum_and_slope(long_half)
    coarse_d[...] = dot_exact_tn(recv_hot[...], long_value)
    for k in range(coarse_count):
        spot = pl.ds(slots[k], 1)
        total[spot, :] = total[spot, :] + coarse_d[pl.ds(k, 1), :]

    step_rows = 256
    blocks = [pl.ds(start, step_rows) for start in range(0, rows, step_rows)]
    for block in blocks:
        agg_b[block, :] = to_bf16(total[block, :])
        work[block, :] = 0.5 * (own[block, :] + dot(agg_b[block, :], w_agg[...]))

    def activate(step, carry):
        here = pl.ds(aligned(step * tile, tile), tile)
        half = work[here, :]
        hidden_b[here, :] = to_bf16(half + half * jnp.tanh(half))
        return carry

    lax.fori_loop(0, rows // tile, activate, 0)
    for block in blocks:
        total[block, :] = dot(hidden_b[block, :], w_out[...])

    wide = 32

    def normalise(step, carry):
        here = pl.ds(aligned(step * wide, wide), wide)
        output = total[here, :]
        cot = to_f32(cotangent[here, :])
        d_norm = cot * gain[...]
        d_mean = jnp.mean(d_norm, axis=-1, keepdims=True)
        centred = output - jnp.mean(output, axis=-1, keepdims=True)
        inv_std = lax.rsqrt(jnp.mean(centred * centred, axis=-1, keepdims=True) + epsilon)
        normed = centred * inv_std
        new_nodes[here, :] = to_bf16(to_f32(nodes[here, :]) + gain[...] * normed)
        sums[2] += eight_rows(cot * normed)
        d_dot = jnp.mean(d_norm * normed, axis=-1, keepdims=True)
        d_out_b[here, :] = to_bf16(inv_std * (d_norm - d_mean - normed * d_dot))
        return carry

    lax.fori_loop(0, rows // wide, normalise, 0, unroll=2)

    for block in blocks:
        total[block, :] = dot_nt(d_out_b[block, :], w_out[...])

    def deactivate(step, carry):
        here = pl.ds(aligned(step * tile, tile), tile)
        slope = half_sum_and_slope(work[here, :])[1]
        d_pre = total[here, :] * (0.5 * slope)
        sums[1] += eight_rows(d_pre)
        d_pre_b[here, :] = to_bf16(d_pre)
        return carry

    lax.fori_loop(0, rows // tile, deactivate, 0)
    share = depth // (2 * lat_count)

    def put(which, half_at, values):
        block = to_bf16(values)
        for place in range(lat_count):
            grads[half_at ^ core, lat ^ place, pl.ds(which * share, share), :] = block[
                place * share : (place + 1) * share
            ]

    for half_at in range(2):
        columns = pl.ds(half_at * (depth // 2), depth // 2)
        put(2, half_at, dot_tn(nodes[:, columns], d_pre_b[...]))
        put(3, half_at, dot_tn(agg_b[:, columns], d_pre_b[...]))
        put(4, half_at, dot_tn(hidden_b[:, columns], d_out_b[...]))
    d_half[pl.ds(0, cols), :] = jnp.zeros((cols, depth), jnp.float32)
    d_half[pl.ds(rows + cols, cols), :] = jnp.zeros((cols, depth), jnp.float32)
    for which in (0, 4):
        slopes[which, pl.ds(0, cols), :] = jnp.zeros((cols, depth), jnp.bfloat16)
    for which in (1, 5):
        slopes[which, pl.ds(rows + cols, cols), :] = jnp.zeros((cols, depth), jnp.bfloat16)
    for start in range(0, rows, step_rows):
        d_sum = dot_nt(d_pre_b[pl.ds(start, step_rows), :], w_agg[...])
        d_half[pl.ds(start + cols, step_rows), :] = 0.5 * to_f32(to_bf16(d_sum))

    def slope_times(which, place, lanes):
        return to_f32(slopes[which, place, lanes]) * d_half[place, lanes]

    def receive(step, carry):
        base = aligned(step * tile, tile)
        here = pl.ds(base, tile)
        value = d_half[pl.ds(aligned(base + cols, tile), tile), :] * slope_sum[here, :]
        total[here, :] = value
        sums[0] += eight_rows(value)
        return carry

    lax.fori_loop(0, rows // tile, receive, 0)
    far_d[...] = jnp.zeros_like(far_d)

    edge_place = lax.broadcasted_iota(jnp.int32, (patch_rows, 1), 0)
    for lane in range(0, depth, 128):
        lanes = pl.ds(lane, 128)
        right_edge = jnp.zeros((patch_rows, 128), jnp.float32)
        left_edge = jnp.zeros((patch_rows, 128), jnp.float32)
        for row in range(patch_rows):
            above_row, out = pl.ds(row * cols, cols), pl.ds(row * cols, cols)
            here, below_row = pl.ds((row + 1) * cols, cols), pl.ds((row + 2) * cols, cols)
            to_mid = slope_times(0, above_row, lanes) + slope_times(1, below_row, lanes)
            to_right = slope_times(2, here, lanes) + slope_times(5, below_row, lanes)
            to_left = slope_times(3, here, lanes) + slope_times(4, above_row, lanes)
            d_send[out, lanes] = (
                to_mid
                + jnp.where(first, 0.0, pltpu.roll(to_right, 1, 0))
                + jnp.where(last, 0.0, pltpu.roll(to_left, cols - 1, 0))
            )
            right_edge = jnp.where(edge_place == row, to_right[cols - 1 : cols], right_edge)
            left_edge = jnp.where(edge_place == row, to_left[0:1], left_edge)
        far_d[pl.ds(aligned(right_at + coarse_count, 16), patch_rows), lanes] = right_edge
        far_d[pl.ds(aligned(left_at + coarse_count + patch_rows, 16), patch_rows), lanes] = left_edge
    row_first, row_last = pl.ds(cols, cols), pl.ds(rows, cols)
    sixteen = lax.broadcasted_iota(jnp.int32, (16, 1), 0)
    for lane in range(0, depth, 128):
        lanes = pl.ds(lane, 128)
        to_right = slope_times(5, row_first, lanes)
        to_left = slope_times(4, row_last, lanes)
        up = slope_times(1, row_first, lanes) + jnp.where(first, 0.0, pltpu.roll(to_right, 1, 0))
        down = slope_times(0, row_last, lanes) + jnp.where(
            last, 0.0, pltpu.roll(to_left, cols - 1, 0)
        )
        near_d[upper, lanes] = to_bf16(up)
        near_d[lower, lanes] = to_bf16(down)
        corner = jnp.where(sixteen == 0, to_right[cols - 1 : cols], 0.0)
        far_d[pl.ds(aligned(right_at + corner_at, 16), 16), lanes] = corner
        corner = jnp.where(sixteen == 1, to_left[0:1], 0.0)
        far_d[pl.ds(aligned(left_at + corner_at, 16), 16), lanes] = corner
    d_up[...] = near_d[upper, :]
    d_down[...] = near_d[lower, :]

    for k in range(coarse_count):
        coarse_d[pl.ds(k, 1), :] = d_half[pl.ds(slots[k] + cols, 1), :]
    long_d = dot_exact(recv_hot[...], coarse_d[...]) * long_slope
    sums[0] += eight_rows(long_d)
    coarse_d[...] = dot_exact_tn(recv_hot[...], long_d)
    for k in range(coarse_count):
        spot = pl.ds(slots[k], 1)
        total[spot, :] = total[spot, :] + coarse_d[pl.ds(k, 1), :]
    coarse[...] = dot_exact_tn(send_hot[...], long_d)
    for source in range(lon_count):
        far_d[pl.ds(source * pack, coarse_count), :] = coarse[
            pl.ds(source * coarse_count, coarse_count), :
        ]
    d_gathered[...] = to_bf16(far_d[same, :])
    d_crossed[...] = to_bf16(far_d[cross, :])
    for block in blocks:
        d_recv_b[block, :] = to_bf16(total[block, :])
        agg_b[block, :] = to_bf16(d_send[block, :])
    for half_at in range(2):
        columns = pl.ds(half_at * (depth // 2), depth // 2)
        put(0, half_at, dot_tn(nodes[:, columns], agg_b[...])
            + dot_tn(near_nodes[:, columns], near_d[...])
            + dot_tn(gathered[:, columns], d_gathered[...])
            + dot_tn(crossed[:, columns], d_crossed[...]))
        put(1, half_at, dot_tn(nodes[:, columns], d_recv_b[...]))
    place = lax.broadcasted_iota(jnp.int32, (16, depth), 0)
    vectors = jnp.zeros((16, depth), jnp.float32)
    for which in range(3):
        vectors = jnp.where(place == which, jnp.sum(sums[which], axis=0, keepdims=True), vectors)
    for part in range(2):
        for spot in range(lat_count):
            grads[part, spot, pl.ds(5 * share, 16), :] = to_bf16(vectors)
    copies = [
        pltpu.make_async_copy(
            grads.at[part, spot], outs[part * lat_count + spot], out_sems.at[part, spot]
        )
        for part in range(2)
        for spot in range(lat_count)
    ]
    for copy in copies:
        copy.start()
    for copy in copies:
        copy.wait()


def update(dims, ints, arrays):
    patch_rows, cols, lon_count, coarse_count, lat_count = dims
    rows, depth = arrays[0].shape
    share = depth // (2 * lat_count)
    edge_count = ints[1].shape[0] * ints[1].shape[1]
    coarse_ids = lon_count * coarse_count
    far_rows = lon_count * (coarse_count + 2 * patch_rows + 16)
    near_rows = 2 * cols
    long_rows = rows + 2 * cols
    half = lambda *size: jax.ShapeDtypeStruct(size, jnp.bfloat16)
    full = lambda *size: jax.ShapeDtypeStruct(size, jnp.float32)
    vmem_full = lambda *size: pltpu.VMEM(size, jnp.float32)
    vmem_half = lambda *size: pltpu.VMEM(size, jnp.bfloat16)
    smem, vmem = pl.BlockSpec(memory_space=pltpu.SMEM), pl.BlockSpec(memory_space=pltpu.VMEM)
    return pl.pallas_call(
        functools.partial(update_kernel, dims),
        in_specs=[smem] * len(ints) + [vmem] * len(arrays),
        out_specs=[vmem] * 8 + [pl.BlockSpec(memory_space=pl.ANY)] * (2 * lat_count),
        out_shape=[half(rows, depth)] * 3
        + [full(rows, depth)]
        + [half(cols, depth)] * 2
        + [half(far_rows // 2, depth)] * 2
        + [half(5 * share + 16, depth)] * (2 * lat_count),
        scratch_shapes=[vmem_full(long_rows, depth)] * 3
        + [vmem_half(6, long_rows, depth)]
        + [vmem_full(rows, depth)] * 3
        + [vmem_half(rows, depth)] * 3
        + [vmem_full(long_rows, depth)]
        + [vmem_full(far_rows, depth)] * 2
        + [vmem_half(near_rows, depth)] * 2
        + [
            vmem_full(3, 8, depth),
            vmem_full(coarse_ids, depth),
            vmem_full(coarse_count, depth),
            vmem_full(edge_count, coarse_ids),
            vmem_full(edge_count, coarse_count),
            vmem_half(2, lat_count, 5 * share + 16, depth),
            pltpu.SemaphoreType.DMA((2, lat_count)),
        ],
        compiler_params=pltpu.CompilerParams(vmem_limit_bytes=VMEM_BYTES),
        cost_estimate=pl.CostEstimate(
            flops=20 * rows * depth * depth, bytes_accessed=20_000_000, transcendentals=0
        ),
        name="update",
    )(*ints, *arrays)


def finish_kernel(dims, slots, *refs):
    patch_rows, cols, _, coarse_count, lat_count = dims
    rows = patch_rows * cols
    (
        cotangent,
        d_pre_b,
        d_recv_b,
        d_send,
        from_below,
        from_above,
        back,
        w_self,
        w_recv,
        w_send,
        grad_nodes,
        total,
    ) = refs
    step_rows = 256
    for start in range(0, rows, step_rows):
        block = pl.ds(start, step_rows)
        total[block, :] = d_send[block, :]
    for start, part in ((rows - cols, from_below), (0, from_above)):
        total[pl.ds(start, cols), :] += to_f32(part[...])
    returned = back[...]
    for row in range(patch_rows):
        for spot, at in ((row * cols, 0), (row * cols + cols - 1, patch_rows)):
            one = coarse_count + at + row
            total[pl.ds(spot, 1), :] += returned[one : one + 1]
    for k in range(coarse_count):
        total[pl.ds(slots[k], 1), :] += returned[k : k + 1]
    for start in range(0, rows, step_rows):
        block = pl.ds(start, step_rows)
        grad_nodes[block, :] = to_bf16(
            to_f32(cotangent[block, :])
            + dot_nt(d_pre_b[block, :], w_self[...])
            + dot_nt(d_recv_b[block, :], w_recv[...])
            + dot_nt(to_bf16(total[block, :]), w_send[...])
        )


def finish(dims, slots, arrays):
    rows, depth = arrays[0].shape
    smem, vmem = pl.BlockSpec(memory_space=pltpu.SMEM), pl.BlockSpec(memory_space=pltpu.VMEM)
    return pl.pallas_call(
        functools.partial(finish_kernel, dims),
        in_specs=[smem] + [vmem] * len(arrays),
        out_specs=vmem,
        out_shape=jax.ShapeDtypeStruct((rows, depth), jnp.bfloat16),
        scratch_shapes=[pltpu.VMEM((rows, depth), jnp.float32)],
        compiler_params=pltpu.CompilerParams(vmem_limit_bytes=VMEM_BYTES),
        cost_estimate=pl.CostEstimate(
            flops=6 * rows * depth * depth, bytes_accessed=8_000_000, transcendentals=0
        ),
        name="finish",
    )(slots, *arrays)


def swapped(values, axis, bit):
    count = lax.axis_size(axis)
    return lax.ppermute(values, axis, [(i, i ^ bit) for i in range(count)])


def summed_part(mine, other, returning, borders):
    lat_count, depth = len(mine), mine[0].shape[-1]
    chip_count = lax.axis_size("lon") // 2
    chip = lax.axis_index("lon") // 2
    share = depth // (2 * lat_count)
    order = list(range(lat_count - 1, -1, -1))
    crossed = {step: swapped(other[step], "lon", 1) for step in order}
    received = []
    for step in order[:-1]:
        message = to_bf16(to_f32(mine[step]) + to_f32(crossed[step]))
        received.append(swapped(message, "lat", step))
    received, returned = lax.optimization_barrier((received, returning()))
    total = to_f32(mine[0]) + to_f32(crossed[0])
    for part in received:
        total = total + to_f32(part)
    total = to_bf16(total)
    vectors = total[5 * share :]
    parts = total[: 5 * share].reshape(5, chip_count, share // chip_count, depth)

    def message_for(step):
        part = lax.dynamic_index_in_dim(parts, chip ^ step, axis=1, keepdims=False)
        return jnp.concatenate([part.reshape(-1, depth), vectors])

    received = [swapped(message_for(step), "lon", 2 * step) for step in range(1, chip_count)]
    received[0], returned = lax.optimization_barrier((received[0], returned))
    received, bordered = lax.optimization_barrier((received, borders(returned)))
    total = to_f32(message_for(0))
    for part in received:
        total = total + to_f32(part)
    return total, returned, bordered


def gathered_shares(total, lat_count, meanwhile):
    depth = total.shape[-1]
    share = depth // (2 * lat_count)
    chip_count = lax.axis_size("lon") // 2
    chip = lax.axis_index("lon") // 2
    part = to_bf16(total[: 5 * share // chip_count])
    parts = jnp.stack([part] + [swapped(part, "lon", 2 * k) for k in range(1, chip_count)])
    parts = parts[chip ^ jnp.arange(chip_count)].reshape(chip_count, 5, -1, depth)
    ready = jnp.transpose(parts, (1, 0, 2, 3)).reshape(5 * share, depth)
    shares = tuple(swapped(ready, "lat", step) for step in range(1, lat_count))
    shares, meanwhile = lax.optimization_barrier((shares, meanwhile))
    shares = [ready, *shares]
    return shares + [swapped(part, "lon", 1) for part in shares], meanwhile


def unpack_kernel(lat_count, scale, total, *refs):
    shares, outs = refs[: 2 * lat_count], refs[2 * lat_count : 2 * lat_count + 8]
    staged, sems = refs[2 * lat_count + 8 :]
    depth = total.shape[-1]
    share = depth // (2 * lat_count)
    core, lat = lax.axis_index("lon") % 2, lax.axis_index("lat")
    copies = []
    for which in range(5):
        for flip in range(2):
            for step in range(lat_count):
                start = (core ^ flip) * (depth // 2) + (lat ^ step) * share
                block = shares[flip * lat_count + step][pl.ds(which * share, share), :]
                staged[which, pl.ds(aligned(start, share), share), :] = scale * to_f32(block)
        copies.append(pltpu.make_async_copy(staged.at[which], outs[which], sems.at[which]))
        copies[-1].start()
    vectors_at = 5 * share // (lax.axis_size("lon") // 2)
    for which in range(3):
        outs[5 + which][...] = scale * total[pl.ds(vectors_at + which, 1), :]
    for copy in copies:
        copy.wait()


def unpack(lat_count, scale, total, shares):
    depth = total.shape[-1]
    vmem = pl.BlockSpec(memory_space=pltpu.VMEM)
    shape = jax.ShapeDtypeStruct
    return pl.pallas_call(
        functools.partial(unpack_kernel, lat_count, scale),
        in_specs=[vmem] * (1 + len(shares)),
        out_specs=[pl.BlockSpec(memory_space=pl.ANY)] * 5 + [vmem] * 3,
        out_shape=[shape((depth, depth), jnp.float32)] * 5 + [shape((1, depth), jnp.float32)] * 3,
        scratch_shapes=[
            pltpu.VMEM((5, depth, depth), jnp.float32),
            pltpu.SemaphoreType.DMA((5,)),
        ],
        compiler_params=pltpu.CompilerParams(vmem_limit_bytes=VMEM_BYTES),
        name="unpack",
    )(total, *shares)


def on_device(
    nodes,
    cotangent,
    w_send,
    w_recv,
    edge_bias,
    w_self,
    w_agg,
    node_bias,
    w_out,
    gain,
    coarse_slots,
    long_senders,
    long_receivers,
):
    patch_rows, cols, depth = nodes.shape
    rows = patch_rows * cols
    lat_count, lon_count = lax.axis_size("lat"), lax.axis_size("lon")
    chip_count = lon_count // 2
    lon = lax.axis_index("lon")
    scale = float(rows * lat_count * lon_count) ** (-0.5)
    slots = coarse_slots.reshape(-1)
    coarse_count = slots.shape[0]
    dims = (patch_rows, cols, lon_count, coarse_count, lat_count)
    flat = nodes.reshape(rows, depth)
    cot = cotangent.reshape(rows, depth)

    down = [(i, i + 1) for i in range(lat_count - 1)]
    up = [(i + 1, i) for i in range(lat_count - 1)]
    above = lax.ppermute(flat[-cols:], "lat", down)
    below = lax.ppermute(flat[:cols], "lat", up)
    bias, offset = edge_bias[None], node_bias[None]
    (send,) = project(project_send_kernel, "project_send", flat, [w_send], [], [jnp.bfloat16])
    above, below, send = lax.optimization_barrier((above, below, send))
    packed = pack_nodes(cols, slots, flat, above, below)
    chips = [swapped(packed, "lon", 2 * k) for k in range(1, chip_count)]
    recv_half, own = project(
        project_own_kernel, "project_own", flat, [w_recv, w_self], [bias, offset], [jnp.float32] * 2
    )
    chips, recv_half, own = lax.optimization_barrier((chips, recv_half, own))
    gathered = jnp.concatenate([packed, *chips])
    crossed = swapped(gathered, "lon", 1)
    outs = update(
        dims,
        (slots, long_senders.reshape(lon_count, -1), long_receivers.reshape(lon_count, -1)),
        (
            flat,
            cot,
            send,
            recv_half,
            own,
            above,
            below,
            gathered,
            crossed,
            w_send,
            w_recv,
            w_agg,
            w_out,
            bias,
            gain[None],
        ),
    )
    new_nodes, d_pre_b, d_recv_b, d_send, d_up, d_down, d_gathered, d_crossed = outs[:8]
    mine, other = outs[8 : 8 + lat_count], outs[8 + lat_count :]

    def returning():
        chips = to_bf16(to_f32(d_gathered) + to_f32(swapped(d_crossed, "lon", 1)))
        parts = chips.reshape(chip_count, -1, depth)
        received = [swapped(parts[step], "lon", 2 * step) for step in range(1, chip_count)]
        return sum([to_f32(one) for one in received], to_f32(parts[0]))

    def borders(back):
        corners = to_bf16(back[-16:-14])
        ups = jnp.concatenate([to_bf16(to_f32(d_up[:1]) + to_f32(corners[:1])), d_up[1:]])
        downs = jnp.concatenate([d_down[:-1], to_bf16(to_f32(d_down[-1:]) + to_f32(corners[1:]))])
        return lax.ppermute(ups, "lat", up), lax.ppermute(downs, "lat", down)

    total, back, bordered = summed_part(mine, other, returning, borders)
    grad_nodes = finish(
        dims,
        slots,
        (
            cot,
            d_pre_b,
            d_recv_b,
            d_send,
            *bordered,
            back,
            w_self,
            w_recv,
            w_send,
        ),
    )
    shares, grad_nodes = gathered_shares(total, lat_count, grad_nodes)
    outs = unpack(lat_count, scale, total, shares)
    return (
        new_nodes.reshape(patch_rows, cols, depth),
        grad_nodes.reshape(patch_rows, cols, depth),
        outs[0],
        outs[1],
        outs[5][0],
        outs[2],
        outs[3],
        outs[6][0],
        outs[4],
        outs[7][0],
    )


def solution(mesh):
    patches = P("lat", "lon", None)
    edges = P("lat", "lon", None, None)
    return jax.shard_map(
        on_device,
        mesh=mesh,
        in_specs=(patches, patches) + (P(),) * 8 + (patches, edges, edges),
        out_specs=(patches, patches) + (P(),) * 8,
        check_vma=False,
    )
```

```python
import functools

import jax
import jax.numpy as jnp
from jax import lax
from jax.experimental import pallas as pl
from jax.experimental.pallas import tpu as pltpu
from jax.sharding import PartitionSpec as P

epsilon = 1e-05
EXACT = lax.Precision.HIGHEST
ABSENT = -1000.0
VMEM_BYTES = 60 * 1024 * 1024


def dot(left, right):
    return jnp.dot(left, right, preferred_element_type=jnp.float32)


def dot_nt(left, right):
    return lax.dot_general(left, right, (((1,), (1,)), ((), ())), preferred_element_type=jnp.float32)


def dot_tn(left, right):
    return lax.dot_general(left, right, (((0,), (0,)), ((), ())), preferred_element_type=jnp.float32)


def dot_exact(left, right):
    return jnp.dot(left, right, preferred_element_type=jnp.float32, precision=EXACT)


def dot_exact_tn(left, right):
    return lax.dot_general(
        left, right, (((0,), (0,)), ((), ())), preferred_element_type=jnp.float32, precision=EXACT
    )


def to_bf16(values):
    return values.astype(jnp.bfloat16)


def to_f32(values):
    return values.astype(jnp.float32)


def half_sum_and_slope(half):
    curve = jnp.tanh(half)
    part = half * curve
    return half + part, (1.0 + curve) * (1.0 + half - part)


def eight_rows(values):
    return jnp.sum(values.reshape(-1, 8, values.shape[-1]), axis=0)


def aligned(start, multiple):
    return pl.multiple_of(start, multiple)


def pack_kernel(cols, slots, nodes, packed):
    rows = nodes.shape[0]
    count, patch_rows = slots.shape[0], rows // cols
    size = count + 2 * patch_rows
    place = lax.broadcasted_iota(jnp.int32, (size, 1), 0)
    wanted = jnp.where(
        place < count + patch_rows,
        (place - count) * cols,
        (place - count - patch_rows) * cols + cols - 1,
    )
    for k in range(count):
        wanted = jnp.where(place == k, slots[k], wanted)
    column = lax.broadcasted_iota(jnp.int32, (size, rows), 1)
    packed[...] = to_bf16(dot(to_bf16(to_f32(column == wanted)), nodes[...]))


def pack_nodes(cols, slots, nodes):
    rows, depth = nodes.shape
    count = slots.shape[0] + 2 * (rows // cols)
    smem, vmem = pl.BlockSpec(memory_space=pltpu.SMEM), pl.BlockSpec(memory_space=pltpu.VMEM)
    return pl.pallas_call(
        functools.partial(pack_kernel, cols),
        in_specs=[smem, vmem],
        out_specs=vmem,
        out_shape=jax.ShapeDtypeStruct((count, depth), jnp.bfloat16),
        name="pack_nodes",
    )(slots, nodes)


def update_kernel(dims, slots, long_senders, long_receivers, edge_bias, node_bias, gain, *refs):
    patch_rows, cols, lon_count, coarse_count, lat_count = dims
    refs = iter(refs)
    take = lambda count: [next(refs) for _ in range(count)]
    sources, results, outs = take(11), take(8), take(2 * lat_count)
    (
        near_nodes,
        gathered,
        crossed,
        w_send,
        nodes,
        w_recv,
        w_self,
        w_agg,
        w_out,
        cotangent,
    ) = held = take(10)
    d_up, d_down, d_gathered, d_crossed, new_nodes, d_pre_b, d_recv_b = kept = take(7)
    (
        mid,
        right,
        left,
        slopes,
        slope_sum,
        recv_half,
        total,
        work,
        agg_b,
        hidden_b,
        d_out_b,
        d_half,
        far,
        near_d,
        sums,
        coarse,
        coarse_d,
        send_hot,
        recv_hot,
        grads,
        in_sems,
        near_sems,
        out_sems,
        grad_sems,
    ) = take(24)
    rows = patch_rows * cols
    depth = nodes.shape[-1]
    pack = coarse_count + 2 * patch_rows + 16
    chip_count = lon_count // 2
    lat, lon = lax.axis_index("lat"), lax.axis_index("lon")
    core = lon % 2
    top_valid, bottom_valid = lat > 0, lat < lat_count - 1

    def place_of(other):
        apart = other ^ lon
        return (apart % 2) * chip_count + apart // 2

    right_at = place_of((lon + 1) % lon_count) * pack
    left_at = place_of((lon + lon_count - 1) % lon_count) * pack
    tile = 16

    upper, lower = pl.ds(0, cols), pl.ds(cols, cols)
    arriving = [
        pltpu.make_async_copy(source, near_nodes.at[place], near_sems.at[k])
        for k, (source, place) in enumerate(zip(sources[:2], (upper, lower)))
    ]
    loads = {}
    for k, (source, target) in enumerate(zip(sources[2:], held[1:])):
        loads[k] = pltpu.make_async_copy(source, target, in_sems.at[k])
    for copy in (loads[3], loads[2], loads[4], *arriving, loads[0], loads[1]):
        copy.start()
    for k in range(5, 9):
        loads[k].start()
    leaving = []

    def leave(source, target, sem):
        leaving.append(pltpu.make_async_copy(source, target, sem))
        leaving[-1].start()

    for k in (3, 2):
        loads[k].wait()
    mid[pl.ds(cols, rows), :] = 0.5 * to_f32(to_bf16(dot(nodes[...], w_send[...])))
    loads[4].wait()
    recv_half[...] = 0.5 * (dot(nodes[...], w_recv[...]) + edge_bias[...])
    for copy in (*arriving, loads[0], loads[1]):
        copy.wait()
    near_half = 0.5 * to_f32(to_bf16(dot(near_nodes[...], w_send[...])))
    half_far = chip_count * pack
    same, cross = pl.ds(0, half_far), pl.ds(half_far, half_far)
    far[same, :] = 0.5 * to_f32(to_bf16(dot(gathered[...], w_send[...])))
    far[cross, :] = 0.5 * to_f32(to_bf16(dot(crossed[...], w_send[...])))
    sums[...] = jnp.zeros_like(sums)
    first = lax.broadcasted_iota(jnp.int32, (cols, 1), 0) == 0
    last = lax.broadcasted_iota(jnp.int32, (cols, 1), 0) == cols - 1
    top = jnp.where(top_valid, near_half[:cols], ABSENT)
    bottom = jnp.where(bottom_valid, near_half[cols : 2 * cols], ABSENT)
    corner_at = pack - 16
    right_corners = far[pl.ds(aligned(right_at + corner_at, 16), 16), :]
    left_corners = far[pl.ds(aligned(left_at + corner_at, 16), 16), :]
    top_corner = jnp.where(top_valid, right_corners[0:1], ABSENT)
    bottom_corner = jnp.where(bottom_valid, left_corners[15:16], ABSENT)
    mid[pl.ds(0, cols), :] = top
    mid[pl.ds(rows + cols, cols), :] = bottom
    right[pl.ds(0, cols), :] = jnp.where(last, top_corner, pltpu.roll(top, cols - 1, 0))
    left[pl.ds(rows + cols, cols), :] = jnp.where(first, bottom_corner, pltpu.roll(bottom, 1, 0))

    right_edge = far[pl.ds(aligned(right_at + coarse_count, 16), patch_rows), :]
    left_edge = far[pl.ds(aligned(left_at + coarse_count + patch_rows, 16), patch_rows), :]
    for row in range(patch_rows):
        there = pl.ds((row + 1) * cols, cols)
        for lane in range(0, depth, 128):
            lanes = pl.ds(lane, 128)
            block = mid[there, lanes]
            edge = right_edge[row : row + 1, lane : lane + 128]
            right[there, lanes] = jnp.where(last, edge, pltpu.roll(block, cols - 1, 0))
            edge = left_edge[row : row + 1, lane : lane + 128]
            left[there, lanes] = jnp.where(first, edge, pltpu.roll(block, 1, 0))

    senders = ((mid, 2), (mid, 0), (right, 1), (left, 1), (left, 2), (right, 0))

    def edges(step, carry):
        base = aligned(step * tile, tile)
        here = pl.ds(base, tile)
        recv = recv_half[here, :]
        summed = jnp.zeros((tile, depth), jnp.float32)
        slope_total = jnp.zeros((tile, depth), jnp.float32)
        for which, (source, shift) in enumerate(senders):
            half = source[pl.ds(aligned(base + shift * cols, tile), tile), :] + recv
            value, slope = half_sum_and_slope(half)
            summed = summed + value
            slope_total = slope_total + slope
            slopes[which, pl.ds(aligned(base + cols, tile), tile), :] = to_bf16(slope)
        total[here, :] = summed
        slope_sum[here, :] = slope_total
        return carry

    lax.fori_loop(0, rows // tile, edges, 0)

    per_source = long_senders.shape[1]
    coarse_lane = lax.broadcasted_iota(jnp.int32, (1, coarse.shape[0]), 1)
    slot_lane = lax.broadcasted_iota(jnp.int32, (1, coarse_count), 1)
    for source in range(lon_count):
        first_id = place_of(source) * coarse_count
        for edge in range(per_source):
            row = pl.ds(source * per_source + edge, 1)
            send_hot[row, :] = to_f32(coarse_lane == first_id + long_senders[source, edge])
            recv_hot[row, :] = to_f32(slot_lane == long_receivers[source, edge])
    for source in range(lon_count):
        coarse[pl.ds(source * coarse_count, coarse_count), :] = far[
            pl.ds(source * pack, coarse_count), :
        ]
    coarse_recv = 0.5 * (dot(gathered[pl.ds(0, coarse_count), :], w_recv[...]) + edge_bias[...])
    long_half = dot_exact(send_hot[...], coarse[...]) + dot_exact(
        recv_hot[...], coarse_recv
    )
    long_value, long_slope = half_sum_and_slope(long_half)
    coarse_d[...] = dot_exact_tn(recv_hot[...], long_value)
    for k in range(coarse_count):
        spot = pl.ds(slots[k], 1)
        total[spot, :] = total[spot, :] + coarse_d[pl.ds(k, 1), :]

    step_rows = 256
    blocks = [pl.ds(start, step_rows) for start in range(0, rows, step_rows)]
    loads[5].wait()
    loads[6].wait()
    for block in blocks:
        agg_b[block, :] = to_bf16(total[block, :])
        work[block, :] = 0.5 * (
            dot(nodes[block, :], w_self[...])
            + dot(agg_b[block, :], w_agg[...])
            + node_bias[...]
        )

    def activate(step, carry):
        here = pl.ds(aligned(step * tile, tile), tile)
        half = work[here, :]
        hidden_b[here, :] = to_bf16(half + half * jnp.tanh(half))
        return carry

    lax.fori_loop(0, rows // tile, activate, 0)
    loads[7].wait()
    for block in blocks:
        total[block, :] = dot(hidden_b[block, :], w_out[...])

    wide = 64
    loads[8].wait()

    def normalise(step, gain_sum):
        here = pl.ds(aligned(step * wide, wide), wide)
        output = total[here, :]
        cot = to_f32(cotangent[here, :])
        d_norm = cot * gain[...]
        d_mean = jnp.mean(d_norm, axis=-1, keepdims=True)
        centred = output - jnp.mean(output, axis=-1, keepdims=True)
        inv_std = lax.rsqrt(jnp.mean(centred * centred, axis=-1, keepdims=True) + epsilon)
        normed = centred * inv_std
        new_nodes[here, :] = to_bf16(to_f32(nodes[here, :]) + gain[...] * normed)
        d_dot = jnp.mean(d_norm * normed, axis=-1, keepdims=True)
        d_out_b[here, :] = to_bf16(inv_std * (d_norm - d_mean - normed * d_dot))
        return gain_sum + eight_rows(cot * normed)

    nothing = jnp.zeros((8, depth), jnp.float32)
    sums[2] = lax.fori_loop(0, rows // wide, normalise, nothing, unroll=4)
    leave(new_nodes, results[0], out_sems.at[0])

    for block in blocks:
        total[block, :] = dot_nt(d_out_b[block, :], w_out[...])

    def deactivate(step, carry):
        here = pl.ds(aligned(step * tile, tile), tile)
        slope = half_sum_and_slope(work[here, :])[1]
        d_pre = total[here, :] * (0.5 * slope)
        sums[1] += eight_rows(d_pre)
        d_pre_b[here, :] = to_bf16(d_pre)
        return carry

    lax.fori_loop(0, rows // tile, deactivate, 0)
    leave(d_pre_b, results[1], out_sems.at[1])
    share = depth // (2 * lat_count)

    def put(which, half_at, values):
        block = to_bf16(values)
        for place in range(lat_count):
            grads[half_at ^ core, lat ^ place, pl.ds(which * share, share), :] = block[
                place * share : (place + 1) * share
            ]

    for half_at in range(2):
        columns = pl.ds(half_at * (depth // 2), depth // 2)
        put(2, half_at, dot_tn(nodes[:, columns], d_pre_b[...]))
        put(3, half_at, dot_tn(agg_b[:, columns], d_pre_b[...]))
        put(4, half_at, dot_tn(hidden_b[:, columns], d_out_b[...]))
    for part in range(2):
        for spot in range(lat_count):
            place = pl.ds(2 * share, 3 * share)
            leave(
                grads.at[part, spot, place],
                outs[part * lat_count + spot].at[place],
                grad_sems.at[part, spot, 0],
            )
    d_half[pl.ds(0, cols), :] = jnp.zeros((cols, depth), jnp.float32)
    d_half[pl.ds(rows + cols, cols), :] = jnp.zeros((cols, depth), jnp.float32)
    for which in (0, 4):
        slopes[which, pl.ds(0, cols), :] = jnp.zeros((cols, depth), jnp.bfloat16)
    for which in (1, 5):
        slopes[which, pl.ds(rows + cols, cols), :] = jnp.zeros((cols, depth), jnp.bfloat16)
    for start in range(0, rows, step_rows):
        d_sum = dot_nt(d_pre_b[pl.ds(start, step_rows), :], w_agg[...])
        d_half[pl.ds(start + cols, step_rows), :] = 0.5 * to_f32(to_bf16(d_sum))

    def slope_times(which, place, lanes):
        return to_f32(slopes[which, place, lanes]) * d_half[place, lanes]

    def receive(step, carry):
        base = aligned(step * tile, tile)
        here = pl.ds(base, tile)
        value = d_half[pl.ds(aligned(base + cols, tile), tile), :] * slope_sum[here, :]
        total[here, :] = value
        sums[0] += eight_rows(value)
        return carry

    lax.fori_loop(0, rows // tile, receive, 0)
    far[...] = jnp.zeros_like(far)

    edge_place = lax.broadcasted_iota(jnp.int32, (patch_rows, 1), 0)
    for lane in range(0, depth, 128):
        lanes = pl.ds(lane, 128)
        right_edge = jnp.zeros((patch_rows, 128), jnp.float32)
        left_edge = jnp.zeros((patch_rows, 128), jnp.float32)
        for row in range(patch_rows):
            above_row, out = pl.ds(row * cols, cols), pl.ds(row * cols, cols)
            here, below_row = pl.ds((row + 1) * cols, cols), pl.ds((row + 2) * cols, cols)
            to_mid = slope_times(0, above_row, lanes) + slope_times(1, below_row, lanes)
            to_right = slope_times(2, here, lanes) + slope_times(5, below_row, lanes)
            to_left = slope_times(3, here, lanes) + slope_times(4, above_row, lanes)
            work[out, lanes] = (
                to_mid
                + jnp.where(first, 0.0, pltpu.roll(to_right, 1, 0))
                + jnp.where(last, 0.0, pltpu.roll(to_left, cols - 1, 0))
            )
            right_edge = jnp.where(edge_place == row, to_right[cols - 1 : cols], right_edge)
            left_edge = jnp.where(edge_place == row, to_left[0:1], left_edge)
        far[pl.ds(aligned(right_at + coarse_count, 16), patch_rows), lanes] = right_edge
        far[pl.ds(aligned(left_at + coarse_count + patch_rows, 16), patch_rows), lanes] = left_edge
    row_first, row_last = pl.ds(cols, cols), pl.ds(rows, cols)
    sixteen = lax.broadcasted_iota(jnp.int32, (16, 1), 0)
    for lane in range(0, depth, 128):
        lanes = pl.ds(lane, 128)
        to_right = slope_times(5, row_first, lanes)
        to_left = slope_times(4, row_last, lanes)
        up = slope_times(1, row_first, lanes) + jnp.where(first, 0.0, pltpu.roll(to_right, 1, 0))
        down = slope_times(0, row_last, lanes) + jnp.where(
            last, 0.0, pltpu.roll(to_left, cols - 1, 0)
        )
        near_d[upper, lanes] = to_bf16(up)
        near_d[lower, lanes] = to_bf16(down)
        corner = jnp.where(sixteen == 0, to_right[cols - 1 : cols], 0.0)
        far[pl.ds(aligned(right_at + corner_at, 16), 16), lanes] = corner
        corner = jnp.where(sixteen == 15, to_left[0:1], 0.0)
        far[pl.ds(aligned(left_at + corner_at, 16), 16), lanes] = corner
    d_up[...] = near_d[upper, :]
    d_down[...] = near_d[lower, :]
    leave(d_up, results[4], out_sems.at[4])
    leave(d_down, results[5], out_sems.at[5])

    for k in range(coarse_count):
        coarse_d[pl.ds(k, 1), :] = d_half[pl.ds(slots[k] + cols, 1), :]
    long_d = dot_exact(recv_hot[...], coarse_d[...]) * long_slope
    sums[0] += eight_rows(long_d)
    coarse_d[...] = dot_exact_tn(recv_hot[...], long_d)
    for k in range(coarse_count):
        spot = pl.ds(slots[k], 1)
        total[spot, :] = total[spot, :] + coarse_d[pl.ds(k, 1), :]
    coarse[...] = dot_exact_tn(send_hot[...], long_d)
    for source in range(lon_count):
        far[pl.ds(source * pack, coarse_count), :] = coarse[
            pl.ds(source * coarse_count, coarse_count), :
        ]
    d_gathered[...] = to_bf16(far[same, :])
    d_crossed[...] = to_bf16(far[cross, :])
    leave(d_gathered, results[6], out_sems.at[6])
    leave(d_crossed, results[7], out_sems.at[7])
    for block in blocks:
        d_recv_b[block, :] = to_bf16(total[block, :])
        agg_b[block, :] = to_bf16(work[block, :])
    leave(d_recv_b, results[2], out_sems.at[2])
    leave(agg_b, results[3], out_sems.at[3])
    for half_at in range(2):
        columns = pl.ds(half_at * (depth // 2), depth // 2)
        put(0, half_at, dot_tn(nodes[:, columns], agg_b[...])
            + dot_tn(near_nodes[:, columns], near_d[...])
            + dot_tn(gathered[:, columns], d_gathered[...])
            + dot_tn(crossed[:, columns], d_crossed[...]))
        put(1, half_at, dot_tn(nodes[:, columns], d_recv_b[...]))
    place = lax.broadcasted_iota(jnp.int32, (16, depth), 0)
    vectors = jnp.zeros((16, depth), jnp.float32)
    for which in range(3):
        vectors = jnp.where(place == which, jnp.sum(sums[which], axis=0, keepdims=True), vectors)
    for part in range(2):
        for spot in range(lat_count):
            grads[part, spot, pl.ds(5 * share, 16), :] = to_bf16(vectors)
    for part in range(2):
        for spot in range(lat_count):
            for k, place in ((1, pl.ds(0, 2 * share)), (2, pl.ds(5 * share, 16))):
                leave(
                    grads.at[part, spot, place],
                    outs[part * lat_count + spot].at[place],
                    grad_sems.at[part, spot, k],
                )
    for copy in leaving:
        copy.wait()


def update(dims, ints, vectors, arrays):
    patch_rows, cols, lon_count, coarse_count, lat_count = dims
    rows, depth = patch_rows * cols, vectors[0].shape[-1]
    share = depth // (2 * lat_count)
    edge_count = ints[1].shape[0] * ints[1].shape[1]
    coarse_ids = lon_count * coarse_count
    far_rows = lon_count * (coarse_count + 2 * patch_rows + 16)
    near_rows = 2 * cols
    long_rows = rows + 2 * cols
    out = lambda *size: jax.ShapeDtypeStruct(size, jnp.bfloat16)
    full = lambda *size: pltpu.VMEM(size, jnp.float32)
    half = lambda *size: pltpu.VMEM(size, jnp.bfloat16)
    smem, vmem = pl.BlockSpec(memory_space=pltpu.SMEM), pl.BlockSpec(memory_space=pltpu.VMEM)
    anywhere = pl.BlockSpec(memory_space=pl.ANY)
    weight = half(depth, depth)
    return pl.pallas_call(
        functools.partial(update_kernel, dims),
        in_specs=[smem] * len(ints) + [vmem] * len(vectors) + [anywhere] * len(arrays),
        out_specs=[anywhere] * (8 + 2 * lat_count),
        out_shape=[out(rows, depth)] * 4
        + [out(cols, depth)] * 2
        + [out(far_rows // 2, depth)] * 2
        + [out(5 * share + 16, depth)] * (2 * lat_count),
        scratch_shapes=[half(near_rows, depth)]
        + [half(far_rows // 2, depth)] * 2
        + [weight, half(rows, depth)]
        + [weight] * 4
        + [half(rows, depth)]
        + [half(cols, depth)] * 2
        + [half(far_rows // 2, depth)] * 2
        + [half(rows, depth)] * 3
        + [full(long_rows, depth)] * 3
        + [half(6, long_rows, depth)]
        + [full(rows, depth)] * 4
        + [half(rows, depth)] * 3
        + [full(long_rows, depth), full(far_rows, depth)]
        + [half(near_rows, depth)]
        + [
            full(3, 8, depth),
            full(coarse_ids, depth),
            full(coarse_count, depth),
            full(edge_count, coarse_ids),
            full(edge_count, coarse_count),
            half(2, lat_count, 5 * share + 16, depth),
            pltpu.SemaphoreType.DMA((9,)),
            pltpu.SemaphoreType.DMA((2,)),
            pltpu.SemaphoreType.DMA((8,)),
            pltpu.SemaphoreType.DMA((2, lat_count, 3)),
        ],
        compiler_params=pltpu.CompilerParams(vmem_limit_bytes=VMEM_BYTES),
        cost_estimate=pl.CostEstimate(
            flops=26 * rows * depth * depth, bytes_accessed=20_000_000, transcendentals=0
        ),
        name="update",
    )(*ints, *vectors, *arrays)


def finish_kernel(dims, slots, *refs):
    patch_rows, cols, _, coarse_count, lat_count = dims
    rows = patch_rows * cols
    (
        cotangent,
        d_pre_b,
        d_recv_b,
        d_send,
        from_below,
        from_above,
        back,
        w_self,
        w_recv,
        w_send,
        grad_nodes,
        total,
    ) = refs
    step_rows = 256
    for start in range(0, rows, step_rows):
        block = pl.ds(start, step_rows)
        total[block, :] = to_f32(d_send[block, :])
    for start, part in ((rows - cols, from_below), (0, from_above)):
        total[pl.ds(start, cols), :] += to_f32(part[...])
    returned = back[...]
    for row in range(patch_rows):
        for spot, at in ((row * cols, 0), (row * cols + cols - 1, patch_rows)):
            one = coarse_count + at + row
            total[pl.ds(spot, 1), :] += returned[one : one + 1]
    for k in range(coarse_count):
        total[pl.ds(slots[k], 1), :] += returned[k : k + 1]
    for start in range(0, rows, step_rows):
        block = pl.ds(start, step_rows)
        grad_nodes[block, :] = to_bf16(
            to_f32(cotangent[block, :])
            + dot_nt(d_pre_b[block, :], w_self[...])
            + dot_nt(d_recv_b[block, :], w_recv[...])
            + dot_nt(to_bf16(total[block, :]), w_send[...])
        )


def finish(dims, slots, arrays):
    rows, depth = arrays[0].shape
    smem, vmem = pl.BlockSpec(memory_space=pltpu.SMEM), pl.BlockSpec(memory_space=pltpu.VMEM)
    return pl.pallas_call(
        functools.partial(finish_kernel, dims),
        in_specs=[smem] + [vmem] * len(arrays),
        out_specs=vmem,
        out_shape=jax.ShapeDtypeStruct((rows, depth), jnp.bfloat16),
        scratch_shapes=[pltpu.VMEM((rows, depth), jnp.float32)],
        compiler_params=pltpu.CompilerParams(vmem_limit_bytes=VMEM_BYTES),
        cost_estimate=pl.CostEstimate(
            flops=6 * rows * depth * depth, bytes_accessed=8_000_000, transcendentals=0
        ),
        name="finish",
    )(slots, *arrays)


def swapped(values, axis, bit):
    count = lax.axis_size(axis)
    return lax.ppermute(values, axis, [(i, i ^ bit) for i in range(count)])


def summed_part(mine, other, returning, borders):
    lat_count, depth = len(mine), mine[0].shape[-1]
    chip_count = lax.axis_size("lon") // 2
    chip = lax.axis_index("lon") // 2
    share = depth // (2 * lat_count)
    order = list(range(lat_count - 1, -1, -1))
    crossed = {step: swapped(other[step], "lon", 1) for step in order}
    received = []
    for step in order[:-1]:
        message = to_bf16(to_f32(mine[step]) + to_f32(crossed[step]))
        received.append(swapped(message, "lat", step))
    received, returned = lax.optimization_barrier((received, returning()))
    total = to_f32(mine[0]) + to_f32(crossed[0])
    for part in received:
        total = total + to_f32(part)
    total = to_bf16(total)
    vectors = total[5 * share :]
    parts = total[: 5 * share].reshape(5, chip_count, share // chip_count, depth)

    def message_for(step):
        part = lax.dynamic_index_in_dim(parts, chip ^ step, axis=1, keepdims=False)
        return jnp.concatenate([part.reshape(-1, depth), vectors])

    received = [swapped(message_for(step), "lon", 2 * step) for step in range(1, chip_count)]
    received[0], returned = lax.optimization_barrier((received[0], returned))
    received, bordered = lax.optimization_barrier((received, borders(returned)))
    total = to_f32(message_for(0))
    for part in received:
        total = total + to_f32(part)
    return total, returned, bordered


def gathered_shares(total, lat_count, meanwhile):
    depth = total.shape[-1]
    share = depth // (2 * lat_count)
    chip_count = lax.axis_size("lon") // 2
    chip = lax.axis_index("lon") // 2
    part = to_bf16(total[: 5 * share // chip_count])
    parts = jnp.stack([part] + [swapped(part, "lon", 2 * k) for k in range(1, chip_count)])
    parts = parts[chip ^ jnp.arange(chip_count)].reshape(chip_count, 5, -1, depth)
    ready = jnp.transpose(parts, (1, 0, 2, 3)).reshape(5 * share, depth)
    shares = tuple(swapped(ready, "lat", step) for step in range(1, lat_count))
    shares, meanwhile = lax.optimization_barrier((shares, meanwhile))
    shares = [ready, *shares]
    return shares, [swapped(part, "lon", 1) for part in shares], meanwhile


def unpack_kernel(flip, scale, *refs):
    count = len(refs)
    lat_count = lax.axis_size("lat")
    shares = refs[:lat_count]
    staged, sems = refs[count - 2 :]
    outs = refs[count - 7 : count - 2]
    depth = outs[0].shape[-1]
    share = depth // (2 * lat_count)
    core, lat = lax.axis_index("lon") % 2, lax.axis_index("lat")
    place = pl.ds(aligned((core ^ flip) * (depth // 2), depth // 2), depth // 2)
    copies = []
    for which in range(5):
        for step in range(lat_count):
            block = shares[step][pl.ds(which * share, share), :]
            start = aligned((lat ^ step) * share, share)
            staged[which, pl.ds(start, share), :] = scale * to_f32(block)
        copies.append(
            pltpu.make_async_copy(staged.at[which], outs[which].at[place], sems.at[which])
        )
        copies[-1].start()
    for copy in copies:
        copy.wait()


def unpack(flip, scale, shares, begun=()):
    depth = shares[0].shape[-1]
    vmem, anywhere = pl.BlockSpec(memory_space=pltpu.VMEM), pl.BlockSpec(memory_space=pl.ANY)
    return pl.pallas_call(
        functools.partial(unpack_kernel, flip, scale),
        in_specs=[vmem] * len(shares) + [anywhere] * len(begun),
        out_specs=[anywhere] * 5,
        out_shape=[jax.ShapeDtypeStruct((depth, depth), jnp.float32)] * 5,
        scratch_shapes=[
            pltpu.VMEM((5, depth // 2, depth), jnp.float32),
            pltpu.SemaphoreType.DMA((5,)),
        ],
        input_output_aliases={len(shares) + k: k for k in range(len(begun))},
        compiler_params=pltpu.CompilerParams(vmem_limit_bytes=VMEM_BYTES),
        cost_estimate=pl.CostEstimate(flops=0, bytes_accessed=8_000_000, transcendentals=0),
        name=f"unpack_{flip}",
    )(*shares, *begun)


def on_device(
    nodes,
    cotangent,
    w_send,
    w_recv,
    edge_bias,
    w_self,
    w_agg,
    node_bias,
    w_out,
    gain,
    coarse_slots,
    long_senders,
    long_receivers,
):
    patch_rows, cols, depth = nodes.shape
    rows = patch_rows * cols
    lat_count, lon_count = lax.axis_size("lat"), lax.axis_size("lon")
    chip_count = lon_count // 2
    lon = lax.axis_index("lon")
    scale = float(rows * lat_count * lon_count) ** (-0.5)
    slots = coarse_slots.reshape(-1)
    coarse_count = slots.shape[0]
    dims = (patch_rows, cols, lon_count, coarse_count, lat_count)
    flat = nodes.reshape(rows, depth)
    cot = cotangent.reshape(rows, depth)

    down = [(i, i + 1) for i in range(lat_count - 1)]
    up = [(i + 1, i) for i in range(lat_count - 1)]

    above = lax.ppermute(flat[-cols:], "lat", down)
    below = lax.ppermute(flat[:cols], "lat", up)
    packed = pack_nodes(cols, slots, flat)
    filler = jnp.zeros((14, depth), jnp.bfloat16)
    packed = jnp.concatenate([packed, above[:1], filler, below[-1:]])
    chips = [swapped(packed, "lon", 2 * k) for k in range(1, chip_count)]
    gathered = jnp.concatenate([packed, *chips])
    crossed = swapped(gathered, "lon", 1)
    outs = update(
        dims,
        (slots, long_senders.reshape(lon_count, -1), long_receivers.reshape(lon_count, -1)),
        (edge_bias[None], node_bias[None], gain[None]),
        (
            above,
            below,
            gathered,
            crossed,
            w_send,
            flat,
            w_recv,
            w_self,
            w_agg,
            w_out,
            cot,
        ),
    )
    new_nodes, d_pre_b, d_recv_b, d_send, d_up, d_down, d_gathered, d_crossed = outs[:8]
    mine, other = outs[8 : 8 + lat_count], outs[8 + lat_count :]

    def returning():
        chips = to_bf16(to_f32(d_gathered) + to_f32(swapped(d_crossed, "lon", 1)))
        parts = chips.reshape(chip_count, -1, depth)
        received = [swapped(parts[step], "lon", 2 * step) for step in range(1, chip_count)]
        return sum([to_f32(one) for one in received], to_f32(parts[0]))

    def borders(back):
        corners = to_bf16(back[-16:])
        ups = jnp.concatenate([to_bf16(to_f32(d_up[:1]) + to_f32(corners[:1])), d_up[1:]])
        downs = jnp.concatenate([d_down[:-1], to_bf16(to_f32(d_down[-1:]) + to_f32(corners[-1:]))])
        return lax.ppermute(ups, "lat", up), lax.ppermute(downs, "lat", down)

    total, back, bordered = summed_part(mine, other, returning, borders)
    grad_nodes = finish(
        dims,
        slots,
        (
            cot,
            d_pre_b,
            d_recv_b,
            d_send,
            *bordered,
            back,
            w_self,
            w_recv,
            w_send,
        ),
    )
    shares, crossed_shares, grad_nodes = gathered_shares(total, lat_count, grad_nodes)
    outs = unpack(0, scale, shares)
    outs = unpack(1, scale, crossed_shares, outs)
    vectors = scale * total[-16:]
    return (
        new_nodes.reshape(patch_rows, cols, depth),
        grad_nodes.reshape(patch_rows, cols, depth),
        outs[0],
        outs[1],
        vectors[0],
        outs[2],
        outs[3],
        vectors[1],
        outs[4],
        vectors[2],
    )


def solution(mesh):
    patches = P("lat", "lon", None)
    edges = P("lat", "lon", None, None)
    return jax.shard_map(
        on_device,
        mesh=mesh,
        in_specs=(patches, patches) + (P(),) * 8 + (patches, edges, edges),
        out_specs=(patches, patches) + (P(),) * 8,
        check_vma=False,
    )
```

```python
import functools

import jax
import jax.numpy as jnp
from jax import lax
from jax.experimental import pallas as pl
from jax.experimental.pallas import tpu as pltpu
from jax.sharding import PartitionSpec as P

epsilon = 1e-05
EXACT = lax.Precision.HIGHEST
ABSENT = -1000.0
MIB = 1024 * 1024


def dot(left, right):
    return jnp.dot(left, right, preferred_element_type=jnp.float32)


def dot_nt(left, right):
    return lax.dot_general(left, right, (((1,), (1,)), ((), ())), preferred_element_type=jnp.float32)


def dot_tn(left, right):
    return lax.dot_general(left, right, (((0,), (0,)), ((), ())), preferred_element_type=jnp.float32)


def dot_exact(left, right):
    return jnp.dot(left, right, preferred_element_type=jnp.float32, precision=EXACT)


def dot_exact_tn(left, right):
    return lax.dot_general(
        left, right, (((0,), (0,)), ((), ())), preferred_element_type=jnp.float32, precision=EXACT
    )


def to_bf16(values):
    return values.astype(jnp.bfloat16)


def to_f32(values):
    return values.astype(jnp.float32)


def half_sum_and_slope(half):
    curve = jnp.tanh(half)
    part = half * curve
    return half + part, (1.0 + curve) * (1.0 + half - part)


def eight_rows(values):
    return jnp.sum(values.reshape(-1, 8, values.shape[-1]), axis=0)


def aligned(start, multiple):
    return pl.multiple_of(start, multiple)


def pack_kernel(cols, slots, nodes, packed):
    rows = nodes.shape[0]
    count, patch_rows = slots.shape[0], rows // cols
    size = count + 2 * patch_rows
    place = lax.broadcasted_iota(jnp.int32, (size, 1), 0)
    wanted = jnp.where(
        place < count + patch_rows,
        (place - count) * cols,
        (place - count - patch_rows) * cols + cols - 1,
    )
    for k in range(count):
        wanted = jnp.where(place == k, slots[k], wanted)
    column = lax.broadcasted_iota(jnp.int32, (size, rows), 1)
    packed[...] = to_bf16(dot(to_bf16(to_f32(column == wanted)), nodes[...]))


def pack_nodes(cols, slots, nodes):
    rows, depth = nodes.shape
    count = slots.shape[0] + 2 * (rows // cols)
    smem, vmem = pl.BlockSpec(memory_space=pltpu.SMEM), pl.BlockSpec(memory_space=pltpu.VMEM)
    return pl.pallas_call(
        functools.partial(pack_kernel, cols),
        in_specs=[smem, vmem],
        out_specs=vmem,
        out_shape=jax.ShapeDtypeStruct((count, depth), jnp.bfloat16),
        name="pack_nodes",
    )(slots, nodes)


def update_kernel(dims, slots, long_senders, long_receivers, edge_bias, node_bias, gain, *refs):
    patch_rows, cols, lon_count, coarse_count, lat_count = dims
    refs = iter(refs)
    take = lambda count: [next(refs) for _ in range(count)]
    sources, results, outs = take(11), take(8), take(2 * lat_count)
    (
        near_nodes,
        gathered,
        crossed,
        w_send,
        nodes,
        w_recv,
        w_self,
        w_agg,
        w_out,
        cotangent,
    ) = held = take(10)
    d_up, d_down, d_gathered, d_crossed, new_nodes, d_pre_b, d_recv_b = kept = take(7)
    (
        mid,
        right,
        left,
        slopes,
        slope_sum,
        recv_half,
        total,
        work,
        agg_b,
        hidden_b,
        d_out_b,
        d_half,
        far,
        near_d,
        sums,
        coarse,
        coarse_d,
        send_hot,
        recv_hot,
        grads,
        in_sems,
        near_sems,
        out_sems,
        grad_sems,
    ) = take(24)
    rows = patch_rows * cols
    depth = nodes.shape[-1]
    pack = coarse_count + 2 * patch_rows + 16
    chip_count = lon_count // 2
    lat, lon = lax.axis_index("lat"), lax.axis_index("lon")
    core = lon % 2
    top_valid, bottom_valid = lat > 0, lat < lat_count - 1

    def place_of(other):
        apart = other ^ lon
        return (apart % 2) * chip_count + apart // 2

    right_at = place_of((lon + 1) % lon_count) * pack
    left_at = place_of((lon + lon_count - 1) % lon_count) * pack
    tile = 16

    upper, lower = pl.ds(0, cols), pl.ds(cols, cols)
    arriving = [
        pltpu.make_async_copy(source, near_nodes.at[place], near_sems.at[k])
        for k, (source, place) in enumerate(zip(sources[:2], (upper, lower)))
    ]
    loads = {}
    for k, (source, target) in enumerate(zip(sources[2:], held[1:])):
        loads[k] = pltpu.make_async_copy(source, target, in_sems.at[k])
    for copy in (loads[3], loads[2], loads[4], *arriving, loads[0], loads[1]):
        copy.start()
    for k in range(5, 9):
        loads[k].start()
    leaving = []

    def leave(source, target, sem):
        leaving.append(pltpu.make_async_copy(source, target, sem))
        leaving[-1].start()

    for k in (3, 2):
        loads[k].wait()
    mid[pl.ds(cols, rows), :] = 0.5 * to_f32(to_bf16(dot(nodes[...], w_send[...])))
    loads[4].wait()
    recv_half[...] = 0.5 * (dot(nodes[...], w_recv[...]) + edge_bias[...])
    for copy in (*arriving, loads[0], loads[1]):
        copy.wait()
    near_half = 0.5 * to_f32(to_bf16(dot(near_nodes[...], w_send[...])))
    half_far = chip_count * pack
    same, cross = pl.ds(0, half_far), pl.ds(half_far, half_far)
    far[same, :] = 0.5 * to_f32(to_bf16(dot(gathered[...], w_send[...])))
    far[cross, :] = 0.5 * to_f32(to_bf16(dot(crossed[...], w_send[...])))
    sums[...] = jnp.zeros_like(sums)
    first = lax.broadcasted_iota(jnp.int32, (cols, 1), 0) == 0
    last = lax.broadcasted_iota(jnp.int32, (cols, 1), 0) == cols - 1
    top = jnp.where(top_valid, near_half[:cols], ABSENT)
    bottom = jnp.where(bottom_valid, near_half[cols : 2 * cols], ABSENT)
    corner_at = pack - 16
    right_corners = far[pl.ds(aligned(right_at + corner_at, 16), 16), :]
    left_corners = far[pl.ds(aligned(left_at + corner_at, 16), 16), :]
    top_corner = jnp.where(top_valid, right_corners[0:1], ABSENT)
    bottom_corner = jnp.where(bottom_valid, left_corners[15:16], ABSENT)
    mid[pl.ds(0, cols), :] = top
    mid[pl.ds(rows + cols, cols), :] = bottom
    right[pl.ds(0, cols), :] = jnp.where(last, top_corner, pltpu.roll(top, cols - 1, 0))
    left[pl.ds(rows + cols, cols), :] = jnp.where(first, bottom_corner, pltpu.roll(bottom, 1, 0))

    right_edge = far[pl.ds(aligned(right_at + coarse_count, 16), patch_rows), :]
    left_edge = far[pl.ds(aligned(left_at + coarse_count + patch_rows, 16), patch_rows), :]
    for row in range(patch_rows):
        there = pl.ds((row + 1) * cols, cols)
        for lane in range(0, depth, 128):
            lanes = pl.ds(lane, 128)
            block = mid[there, lanes]
            edge = right_edge[row : row + 1, lane : lane + 128]
            right[there, lanes] = jnp.where(last, edge, pltpu.roll(block, cols - 1, 0))
            edge = left_edge[row : row + 1, lane : lane + 128]
            left[there, lanes] = jnp.where(first, edge, pltpu.roll(block, 1, 0))

    senders = ((mid, 2), (mid, 0), (right, 1), (left, 1), (left, 2), (right, 0))

    def edges(step, carry):
        base = aligned(step * tile, tile)
        here = pl.ds(base, tile)
        recv = recv_half[here, :]
        summed = jnp.zeros((tile, depth), jnp.float32)
        slope_total = jnp.zeros((tile, depth), jnp.float32)
        for which, (source, shift) in enumerate(senders):
            half = source[pl.ds(aligned(base + shift * cols, tile), tile), :] + recv
            value, slope = half_sum_and_slope(half)
            summed = summed + value
            slope_total = slope_total + slope
            slopes[which, pl.ds(aligned(base + cols, tile), tile), :] = to_bf16(slope)
        total[here, :] = summed
        slope_sum[here, :] = slope_total
        return carry

    lax.fori_loop(0, rows // tile, edges, 0)

    per_source = long_senders.shape[1]
    coarse_lane = lax.broadcasted_iota(jnp.int32, (1, coarse.shape[0]), 1)
    slot_lane = lax.broadcasted_iota(jnp.int32, (1, coarse_count), 1)
    for source in range(lon_count):
        first_id = place_of(source) * coarse_count
        for edge in range(per_source):
            row = pl.ds(source * per_source + edge, 1)
            send_hot[row, :] = to_f32(coarse_lane == first_id + long_senders[source, edge])
            recv_hot[row, :] = to_f32(slot_lane == long_receivers[source, edge])
    for source in range(lon_count):
        coarse[pl.ds(source * coarse_count, coarse_count), :] = far[
            pl.ds(source * pack, coarse_count), :
        ]
    coarse_recv = 0.5 * (dot(gathered[pl.ds(0, coarse_count), :], w_recv[...]) + edge_bias[...])
    long_half = dot_exact(send_hot[...], coarse[...]) + dot_exact(
        recv_hot[...], coarse_recv
    )
    long_value, long_slope = half_sum_and_slope(long_half)
    coarse_d[...] = dot_exact_tn(recv_hot[...], long_value)
    for k in range(coarse_count):
        spot = pl.ds(slots[k], 1)
        total[spot, :] = total[spot, :] + coarse_d[pl.ds(k, 1), :]

    step_rows = 256
    blocks = [pl.ds(start, step_rows) for start in range(0, rows, step_rows)]
    loads[5].wait()
    loads[6].wait()
    for block in blocks:
        agg_b[block, :] = to_bf16(total[block, :])
        work[block, :] = 0.5 * (
            dot(nodes[block, :], w_self[...])
            + dot(agg_b[block, :], w_agg[...])
            + node_bias[...]
        )

    def activate(step, carry):
        here = pl.ds(aligned(step * tile, tile), tile)
        half = work[here, :]
        hidden_b[here, :] = to_bf16(half + half * jnp.tanh(half))
        return carry

    lax.fori_loop(0, rows // tile, activate, 0, unroll=4)
    loads[7].wait()
    for block in blocks:
        total[block, :] = dot(hidden_b[block, :], w_out[...])

    wide = 64
    loads[8].wait()

    def normalise(step, gain_sum):
        here = pl.ds(aligned(step * wide, wide), wide)
        output = total[here, :]
        cot = to_f32(cotangent[here, :])
        d_norm = cot * gain[...]
        d_mean = jnp.mean(d_norm, axis=-1, keepdims=True)
        centred = output - jnp.mean(output, axis=-1, keepdims=True)
        inv_std = lax.rsqrt(jnp.mean(centred * centred, axis=-1, keepdims=True) + epsilon)
        normed = centred * inv_std
        new_nodes[here, :] = to_bf16(to_f32(nodes[here, :]) + gain[...] * normed)
        d_dot = jnp.mean(d_norm * normed, axis=-1, keepdims=True)
        d_out_b[here, :] = to_bf16(inv_std * (d_norm - d_mean - normed * d_dot))
        return gain_sum + eight_rows(cot * normed)

    nothing = jnp.zeros((8, depth), jnp.float32)
    sums[2] = lax.fori_loop(0, rows // wide, normalise, nothing, unroll=4)
    leave(new_nodes, results[0], out_sems.at[0])

    for block in blocks:
        total[block, :] = dot_nt(d_out_b[block, :], w_out[...])

    def deactivate(step, bias_sum):
        here = pl.ds(aligned(step * tile, tile), tile)
        slope = half_sum_and_slope(work[here, :])[1]
        d_pre = total[here, :] * (0.5 * slope)
        d_pre_b[here, :] = to_bf16(d_pre)
        return bias_sum + eight_rows(d_pre)

    sums[1] = lax.fori_loop(0, rows // tile, deactivate, nothing, unroll=4)
    leave(d_pre_b, results[1], out_sems.at[1])
    share = depth // (2 * lat_count)

    def put(which, half_at, values):
        block = to_bf16(values)
        for place in range(lat_count):
            grads[half_at ^ core, lat ^ place, pl.ds(which * share, share), :] = block[
                place * share : (place + 1) * share
            ]

    for half_at in range(2):
        columns = pl.ds(half_at * (depth // 2), depth // 2)
        put(2, half_at, dot_tn(nodes[:, columns], d_pre_b[...]))
        put(3, half_at, dot_tn(agg_b[:, columns], d_pre_b[...]))
        put(4, half_at, dot_tn(hidden_b[:, columns], d_out_b[...]))
    for part in range(2):
        for spot in range(lat_count):
            place = pl.ds(2 * share, 3 * share)
            leave(
                grads.at[part, spot, place],
                outs[part * lat_count + spot].at[place],
                grad_sems.at[part, spot, 0],
            )
    d_half[pl.ds(0, cols), :] = jnp.zeros((cols, depth), jnp.float32)
    d_half[pl.ds(rows + cols, cols), :] = jnp.zeros((cols, depth), jnp.float32)
    for which in (0, 4):
        slopes[which, pl.ds(0, cols), :] = jnp.zeros((cols, depth), jnp.bfloat16)
    for which in (1, 5):
        slopes[which, pl.ds(rows + cols, cols), :] = jnp.zeros((cols, depth), jnp.bfloat16)
    for start in range(0, rows, step_rows):
        d_sum = dot_nt(d_pre_b[pl.ds(start, step_rows), :], w_agg[...])
        d_half[pl.ds(start + cols, step_rows), :] = 0.5 * to_f32(to_bf16(d_sum))

    def slope_times(which, place, lanes):
        return to_f32(slopes[which, place, lanes]) * d_half[place, lanes]

    def receive(step, bias_sum):
        base = aligned(step * tile, tile)
        here = pl.ds(base, tile)
        value = d_half[pl.ds(aligned(base + cols, tile), tile), :] * slope_sum[here, :]
        total[here, :] = value
        return bias_sum + eight_rows(value)

    sums[0] = lax.fori_loop(0, rows // tile, receive, nothing, unroll=4)
    far[...] = jnp.zeros_like(far)

    edge_place = lax.broadcasted_iota(jnp.int32, (patch_rows, 1), 0)
    for lane in range(0, depth, 128):
        lanes = pl.ds(lane, 128)
        right_edge = jnp.zeros((patch_rows, 128), jnp.float32)
        left_edge = jnp.zeros((patch_rows, 128), jnp.float32)
        for row in range(patch_rows):
            above_row, out = pl.ds(row * cols, cols), pl.ds(row * cols, cols)
            here, below_row = pl.ds((row + 1) * cols, cols), pl.ds((row + 2) * cols, cols)
            to_mid = slope_times(0, above_row, lanes) + slope_times(1, below_row, lanes)
            to_right = slope_times(2, here, lanes) + slope_times(5, below_row, lanes)
            to_left = slope_times(3, here, lanes) + slope_times(4, above_row, lanes)
            work[out, lanes] = (
                to_mid
                + jnp.where(first, 0.0, pltpu.roll(to_right, 1, 0))
                + jnp.where(last, 0.0, pltpu.roll(to_left, cols - 1, 0))
            )
            right_edge = jnp.where(edge_place == row, to_right[cols - 1 : cols], right_edge)
            left_edge = jnp.where(edge_place == row, to_left[0:1], left_edge)
        far[pl.ds(aligned(right_at + coarse_count, 16), patch_rows), lanes] = right_edge
        far[pl.ds(aligned(left_at + coarse_count + patch_rows, 16), patch_rows), lanes] = left_edge
    row_first, row_last = pl.ds(cols, cols), pl.ds(rows, cols)
    sixteen = lax.broadcasted_iota(jnp.int32, (16, 1), 0)
    for lane in range(0, depth, 128):
        lanes = pl.ds(lane, 128)
        to_right = slope_times(5, row_first, lanes)
        to_left = slope_times(4, row_last, lanes)
        up = slope_times(1, row_first, lanes) + jnp.where(first, 0.0, pltpu.roll(to_right, 1, 0))
        down = slope_times(0, row_last, lanes) + jnp.where(
            last, 0.0, pltpu.roll(to_left, cols - 1, 0)
        )
        near_d[upper, lanes] = to_bf16(up)
        near_d[lower, lanes] = to_bf16(down)
        corner = jnp.where(sixteen == 0, to_right[cols - 1 : cols], 0.0)
        far[pl.ds(aligned(right_at + corner_at, 16), 16), lanes] = corner
        corner = jnp.where(sixteen == 15, to_left[0:1], 0.0)
        far[pl.ds(aligned(left_at + corner_at, 16), 16), lanes] = corner
    d_up[...] = near_d[upper, :]
    d_down[...] = near_d[lower, :]
    leave(d_up, results[4], out_sems.at[4])
    leave(d_down, results[5], out_sems.at[5])

    for k in range(coarse_count):
        coarse_d[pl.ds(k, 1), :] = d_half[pl.ds(slots[k] + cols, 1), :]
    long_d = dot_exact(recv_hot[...], coarse_d[...]) * long_slope
    sums[0] += eight_rows(long_d)
    coarse_d[...] = dot_exact_tn(recv_hot[...], long_d)
    for k in range(coarse_count):
        spot = pl.ds(slots[k], 1)
        total[spot, :] = total[spot, :] + coarse_d[pl.ds(k, 1), :]
    coarse[...] = dot_exact_tn(send_hot[...], long_d)
    for source in range(lon_count):
        far[pl.ds(source * pack, coarse_count), :] = coarse[
            pl.ds(source * coarse_count, coarse_count), :
        ]
    d_gathered[...] = to_bf16(far[same, :])
    d_crossed[...] = to_bf16(far[cross, :])
    leave(d_gathered, results[6], out_sems.at[6])
    leave(d_crossed, results[7], out_sems.at[7])
    for block in blocks:
        d_recv_b[block, :] = to_bf16(total[block, :])
        agg_b[block, :] = to_bf16(work[block, :])
    leave(d_recv_b, results[2], out_sems.at[2])
    leave(agg_b, results[3], out_sems.at[3])
    for half_at in range(2):
        columns = pl.ds(half_at * (depth // 2), depth // 2)
        put(0, half_at, dot_tn(nodes[:, columns], agg_b[...])
            + dot_tn(near_nodes[:, columns], near_d[...])
            + dot_tn(gathered[:, columns], d_gathered[...])
            + dot_tn(crossed[:, columns], d_crossed[...]))
        put(1, half_at, dot_tn(nodes[:, columns], d_recv_b[...]))
    place = lax.broadcasted_iota(jnp.int32, (16, depth), 0)
    vectors = jnp.zeros((16, depth), jnp.float32)
    for which in range(3):
        vectors = jnp.where(place == which, jnp.sum(sums[which], axis=0, keepdims=True), vectors)
    for part in range(2):
        for spot in range(lat_count):
            grads[part, spot, pl.ds(5 * share, 16), :] = to_bf16(vectors)
    for part in range(2):
        for spot in range(lat_count):
            for k, place in ((1, pl.ds(0, 2 * share)), (2, pl.ds(5 * share, 16))):
                leave(
                    grads.at[part, spot, place],
                    outs[part * lat_count + spot].at[place],
                    grad_sems.at[part, spot, k],
                )
    for copy in leaving:
        copy.wait()


def update(dims, ints, vectors, arrays):
    patch_rows, cols, lon_count, coarse_count, lat_count = dims
    rows, depth = patch_rows * cols, vectors[0].shape[-1]
    share = depth // (2 * lat_count)
    edge_count = ints[1].shape[0] * ints[1].shape[1]
    coarse_ids = lon_count * coarse_count
    far_rows = lon_count * (coarse_count + 2 * patch_rows + 16)
    near_rows = 2 * cols
    long_rows = rows + 2 * cols
    out = lambda *size: jax.ShapeDtypeStruct(size, jnp.bfloat16)
    full = lambda *size: pltpu.VMEM(size, jnp.float32)
    half = lambda *size: pltpu.VMEM(size, jnp.bfloat16)
    smem, vmem = pl.BlockSpec(memory_space=pltpu.SMEM), pl.BlockSpec(memory_space=pltpu.VMEM)
    anywhere = pl.BlockSpec(memory_space=pl.ANY)
    weight = half(depth, depth)
    return pl.pallas_call(
        functools.partial(update_kernel, dims),
        in_specs=[smem] * len(ints) + [vmem] * len(vectors) + [anywhere] * len(arrays),
        out_specs=[anywhere] * (8 + 2 * lat_count),
        out_shape=[out(rows, depth)] * 4
        + [out(cols, depth)] * 2
        + [out(far_rows // 2, depth)] * 2
        + [out(5 * share + 16, depth)] * (2 * lat_count),
        scratch_shapes=[half(near_rows, depth)]
        + [half(far_rows // 2, depth)] * 2
        + [weight, half(rows, depth)]
        + [weight] * 4
        + [half(rows, depth)]
        + [half(cols, depth)] * 2
        + [half(far_rows // 2, depth)] * 2
        + [half(rows, depth)] * 3
        + [full(long_rows, depth)] * 3
        + [half(6, long_rows, depth)]
        + [full(rows, depth)] * 4
        + [half(rows, depth)] * 3
        + [full(long_rows, depth), full(far_rows, depth)]
        + [half(near_rows, depth)]
        + [
            full(3, 8, depth),
            full(coarse_ids, depth),
            full(coarse_count, depth),
            full(edge_count, coarse_ids),
            full(edge_count, coarse_count),
            half(2, lat_count, 5 * share + 16, depth),
            pltpu.SemaphoreType.DMA((9,)),
            pltpu.SemaphoreType.DMA((2,)),
            pltpu.SemaphoreType.DMA((8,)),
            pltpu.SemaphoreType.DMA((2, lat_count, 3)),
        ],
        compiler_params=pltpu.CompilerParams(vmem_limit_bytes=63 * MIB),
        cost_estimate=pl.CostEstimate(
            flops=26 * rows * depth * depth, bytes_accessed=20_000_000, transcendentals=0
        ),
        name="update",
    )(*ints, *vectors, *arrays)


def finish_kernel(dims, scale, slots, *refs):
    patch_rows, cols, _, coarse_count, lat_count = dims
    rows = patch_rows * cols
    (
        cotangent,
        d_pre_b,
        d_recv_b,
        d_send,
        from_below,
        from_above,
        back,
        w_self,
        w_recv,
        w_send,
        summed,
        grad_nodes,
        *vectors,
        total,
    ) = refs
    step_rows = 256
    for start in range(0, rows, step_rows):
        block = pl.ds(start, step_rows)
        total[block, :] = to_f32(d_send[block, :])
    for start, part in ((rows - cols, from_below), (0, from_above)):
        total[pl.ds(start, cols), :] += to_f32(part[...])
    for which, vector in enumerate(vectors):
        vector[...] = scale * summed[pl.ds(summed.shape[0] - 8 + which, 1), :]
    returned = back[...]
    for row in range(patch_rows):
        for spot, at in ((row * cols, 0), (row * cols + cols - 1, patch_rows)):
            one = coarse_count + at + row
            total[pl.ds(spot, 1), :] += returned[one : one + 1]
    for k in range(coarse_count):
        total[pl.ds(slots[k], 1), :] += returned[k : k + 1]
    for start in range(0, rows, step_rows):
        block = pl.ds(start, step_rows)
        grad_nodes[block, :] = to_bf16(
            to_f32(cotangent[block, :])
            + dot_nt(d_pre_b[block, :], w_self[...])
            + dot_nt(d_recv_b[block, :], w_recv[...])
            + dot_nt(to_bf16(total[block, :]), w_send[...])
        )


def finish(dims, scale, slots, arrays):
    rows, depth = arrays[0].shape
    smem, vmem = pl.BlockSpec(memory_space=pltpu.SMEM), pl.BlockSpec(memory_space=pltpu.VMEM)
    return pl.pallas_call(
        functools.partial(finish_kernel, dims, scale),
        in_specs=[smem] + [vmem] * len(arrays),
        out_specs=[vmem] * 4,
        out_shape=[jax.ShapeDtypeStruct((rows, depth), jnp.bfloat16)]
        + [jax.ShapeDtypeStruct((1, depth), jnp.float32)] * 3,
        scratch_shapes=[pltpu.VMEM((rows, depth), jnp.float32)],
        compiler_params=pltpu.CompilerParams(vmem_limit_bytes=63 * MIB),
        cost_estimate=pl.CostEstimate(
            flops=6 * rows * depth * depth, bytes_accessed=8_000_000, transcendentals=0
        ),
        name="finish",
    )(slots, *arrays)


def swapped(values, axis, bit):
    count = lax.axis_size(axis)
    return lax.ppermute(values, axis, [(i, i ^ bit) for i in range(count)])


def summed_part(mine, other, d_crossed, returning, borders):
    lat_count, depth = len(mine), mine[0].shape[-1]
    chip_count = lax.axis_size("lon") // 2
    chip = lax.axis_index("lon") // 2
    share = depth // (2 * lat_count)
    order = list(range(lat_count - 1, -1, -1))
    crossed = {step: swapped(other[step], "lon", 1) for step in order}
    messages = [to_bf16(to_f32(mine[step]) + to_f32(crossed[step])) for step in order[:-1]]
    messages[0], d_crossed = lax.optimization_barrier((messages[0], d_crossed))
    received = [swapped(part, "lat", step) for part, step in zip(messages, order)]
    received, returned = lax.optimization_barrier((received, returning(d_crossed)))
    total = to_f32(mine[0]) + to_f32(crossed[0])
    for part in received:
        total = total + to_f32(part)
    total = to_bf16(total)
    vectors = total[5 * share : 5 * share + 8]
    parts = total[: 5 * share].reshape(5, chip_count, share // chip_count, depth)

    def message_for(step):
        part = lax.dynamic_index_in_dim(parts, chip ^ step, axis=1, keepdims=False)
        return jnp.concatenate([part.reshape(-1, depth), vectors])

    received = [swapped(message_for(step), "lon", 2 * step) for step in range(1, chip_count)]
    received[0], returned = lax.optimization_barrier((received[0], returned))
    received, bordered = lax.optimization_barrier((received, borders(returned)))
    total = to_f32(message_for(0))
    for part in received:
        total = total + to_f32(part)
    return total, returned, bordered


def gathered_share(total, lat_count):
    depth = total.shape[-1]
    share = depth // (2 * lat_count)
    chip_count = lax.axis_size("lon") // 2
    chip = lax.axis_index("lon") // 2
    part = to_bf16(total[: 5 * share // chip_count])
    parts = jnp.stack([part] + [swapped(part, "lon", 2 * k) for k in range(1, chip_count)])
    parts = parts[chip ^ jnp.arange(chip_count)].reshape(chip_count, 5, -1, depth)
    return jnp.transpose(parts, (1, 0, 2, 3)).reshape(5 * share, depth)


def unpack_kernel(pieces, scale, *refs):
    count = len(refs)
    held, staged, load_sems, sems = refs[count - 4 :]
    outs = refs[count - 9 : count - 4]
    depth = outs[0].shape[-1]
    share = depth // (2 * lax.axis_size("lat"))
    core, lat = lax.axis_index("lon") % 2, lax.axis_index("lat")
    loads = [
        pltpu.make_async_copy(refs[k], held.at[k], load_sems.at[k]) for k in range(len(pieces))
    ]
    for load in loads:
        load.start()
    copies = []
    for k, (flip, step) in enumerate(pieces):
        loads[k].wait()
        start = (core ^ flip) * (depth // 2) + (lat ^ step) * share
        place = pl.ds(aligned(start, share), share)
        for which in range(5):
            staged[k, which] = scale * to_f32(held[k, pl.ds(which * share, share), :])
            copies.append(
                pltpu.make_async_copy(
                    staged.at[k, which], outs[which].at[place], sems.at[k, which]
                )
            )
            copies[-1].start()
    for copy in copies:
        copy.wait()


def unpack(pieces, scale, shares, begun=()):
    depth = shares[0].shape[-1]
    rows = shares[0].shape[0]
    anywhere = pl.BlockSpec(memory_space=pl.ANY)
    return pl.pallas_call(
        functools.partial(unpack_kernel, pieces, scale),
        in_specs=[anywhere] * (len(shares) + len(begun)),
        out_specs=[anywhere] * 5,
        out_shape=[jax.ShapeDtypeStruct((depth, depth), jnp.float32)] * 5,
        scratch_shapes=[
            pltpu.VMEM((len(shares), rows, depth), jnp.bfloat16),
            pltpu.VMEM((len(shares), 5, rows // 5, depth), jnp.float32),
            pltpu.SemaphoreType.DMA((len(shares),)),
            pltpu.SemaphoreType.DMA((len(shares), 5)),
        ],
        input_output_aliases={len(shares) + k: k for k in range(len(begun))},
        compiler_params=pltpu.CompilerParams(vmem_limit_bytes=10 * MIB),
        cost_estimate=pl.CostEstimate(flops=0, bytes_accessed=8_000_000, transcendentals=0),
        name=f"unpack_{len(pieces)}",
    )(*shares, *begun)


def on_device(
    nodes,
    cotangent,
    w_send,
    w_recv,
    edge_bias,
    w_self,
    w_agg,
    node_bias,
    w_out,
    gain,
    coarse_slots,
    long_senders,
    long_receivers,
):
    patch_rows, cols, depth = nodes.shape
    rows = patch_rows * cols
    lat_count, lon_count = lax.axis_size("lat"), lax.axis_size("lon")
    chip_count = lon_count // 2
    lon = lax.axis_index("lon")
    scale = float(rows * lat_count * lon_count) ** (-0.5)
    slots = coarse_slots.reshape(-1)
    coarse_count = slots.shape[0]
    dims = (patch_rows, cols, lon_count, coarse_count, lat_count)
    flat = nodes.reshape(rows, depth)
    cot = cotangent.reshape(rows, depth)

    down = [(i, i + 1) for i in range(lat_count - 1)]
    up = [(i + 1, i) for i in range(lat_count - 1)]

    above = lax.ppermute(flat[-cols:], "lat", down)
    below = lax.ppermute(flat[:cols], "lat", up)
    packed = pack_nodes(cols, slots, flat)
    filler = jnp.zeros((14, depth), jnp.bfloat16)
    packed = jnp.concatenate([packed, above[:1], filler, below[-1:]])
    chips = [swapped(packed, "lon", 2 * k) for k in range(1, chip_count)]
    gathered = jnp.concatenate([packed, *chips])
    crossed = swapped(gathered, "lon", 1)
    outs = update(
        dims,
        (slots, long_senders.reshape(lon_count, -1), long_receivers.reshape(lon_count, -1)),
        (edge_bias[None], node_bias[None], gain[None]),
        (
            above,
            below,
            gathered,
            crossed,
            w_send,
            flat,
            w_recv,
            w_self,
            w_agg,
            w_out,
            cot,
        ),
    )
    new_nodes, d_pre_b, d_recv_b, d_send, d_up, d_down, d_gathered, d_crossed = outs[:8]
    mine, other = outs[8 : 8 + lat_count], outs[8 + lat_count :]

    def returning(d_crossed):
        chips = to_bf16(to_f32(d_gathered) + to_f32(swapped(d_crossed, "lon", 1)))
        parts = chips.reshape(chip_count, -1, depth)
        received = [swapped(parts[step], "lon", 2 * step) for step in range(1, chip_count)]
        return sum([to_f32(one) for one in received], to_f32(parts[0]))

    def borders(back):
        corners = to_bf16(back[-16:])
        ups = jnp.concatenate([to_bf16(to_f32(d_up[:1]) + to_f32(corners[:1])), d_up[1:]])
        downs = jnp.concatenate([d_down[:-1], to_bf16(to_f32(d_down[-1:]) + to_f32(corners[-1:]))])
        return lax.ppermute(ups, "lat", up), lax.ppermute(downs, "lat", down)

    total, back, bordered = summed_part(mine, other, d_crossed, returning, borders)
    grad_nodes, *vectors = finish(
        dims,
        scale,
        slots,
        (
            cot,
            d_pre_b,
            d_recv_b,
            d_send,
            *bordered,
            back,
            w_self,
            w_recv,
            w_send,
            total,
        ),
    )

    ready = gathered_share(total, lat_count)
    shares = [swapped(ready, "lat", step) for step in range(1, lat_count)]
    outs = unpack([(0, 0)], scale, [ready])
    shares, grad_nodes, outs = lax.optimization_barrier((shares, grad_nodes, outs))
    crossed = [swapped(part, "lon", 1) for part in (ready, *shares)]
    pieces = [(1, 0)] + [(flip, step) for step in range(1, lat_count) for flip in range(2)]
    parts = [crossed[step] if flip else shares[step - 1] for flip, step in pieces]
    outs = unpack(pieces, scale, parts, outs)
    return (
        new_nodes.reshape(patch_rows, cols, depth),
        grad_nodes.reshape(patch_rows, cols, depth),
        outs[0],
        outs[1],
        vectors[0][0],
        outs[2],
        outs[3],
        vectors[1][0],
        outs[4],
        vectors[2][0],
    )


def solution(mesh):
    patches = P("lat", "lon", None)
    edges = P("lat", "lon", None, None)
    return jax.shard_map(
        on_device,
        mesh=mesh,
        in_specs=(patches, patches) + (P(),) * 8 + (patches, edges, edges),
        out_specs=(patches, patches) + (P(),) * 8,
        check_vma=False,
    )
```

```python
import functools

import jax
import jax.numpy as jnp
from jax import lax
from jax.experimental import pallas as pl
from jax.experimental.pallas import tpu as pltpu
from jax.sharding import PartitionSpec as P

epsilon = 1e-05
EXACT = lax.Precision.HIGHEST
ABSENT = -1000.0
MIB = 1024 * 1024


def dot(left, right):
    return jnp.dot(left, right, preferred_element_type=jnp.float32)


def dot_nt(left, right):
    return lax.dot_general(left, right, (((1,), (1,)), ((), ())), preferred_element_type=jnp.float32)


def dot_tn(left, right):
    return lax.dot_general(left, right, (((0,), (0,)), ((), ())), preferred_element_type=jnp.float32)


def dot_exact(left, right):
    return jnp.dot(left, right, preferred_element_type=jnp.float32, precision=EXACT)


def dot_exact_tn(left, right):
    return lax.dot_general(
        left, right, (((0,), (0,)), ((), ())), preferred_element_type=jnp.float32, precision=EXACT
    )


def to_bf16(values):
    return values.astype(jnp.bfloat16)


def to_f32(values):
    return values.astype(jnp.float32)


def half_sum_and_slope(half):
    curve = jnp.tanh(half)
    part = half * curve
    return half + part, (1.0 + curve) * (1.0 + half - part)


def eight_rows(values):
    return jnp.sum(values.reshape(-1, 8, values.shape[-1]), axis=0)


def aligned(start, multiple):
    return pl.multiple_of(start, multiple)


def pack_kernel(cols, slots, nodes, packed):
    rows = nodes.shape[0]
    count, patch_rows = slots.shape[0], rows // cols
    size = count + 2 * patch_rows
    place = lax.broadcasted_iota(jnp.int32, (size, 1), 0)
    core = lax.axis_index("lon") % 2
    outer = jnp.where(core == 0, 0, cols - 1)
    wanted = jnp.where(
        place < count + patch_rows,
        (place - count) * cols + outer,
        (place - count - patch_rows) * cols + cols - 1 - outer,
    )
    for k in range(count):
        wanted = jnp.where(place == k, slots[k], wanted)
    column = lax.broadcasted_iota(jnp.int32, (size, rows), 1)
    packed[...] = to_bf16(dot(to_bf16(to_f32(column == wanted)), nodes[...]))


def pack_nodes(cols, slots, nodes):
    rows, depth = nodes.shape
    count = slots.shape[0] + 2 * (rows // cols)
    smem, vmem = pl.BlockSpec(memory_space=pltpu.SMEM), pl.BlockSpec(memory_space=pltpu.VMEM)
    return pl.pallas_call(
        functools.partial(pack_kernel, cols),
        in_specs=[smem, vmem],
        out_specs=vmem,
        out_shape=jax.ShapeDtypeStruct((count, depth), jnp.bfloat16),
        name="pack_nodes",
    )(slots, nodes)


def update_kernel(dims, slots, long_senders, long_receivers, edge_bias, node_bias, gain, *refs):
    patch_rows, cols, lon_count, coarse_count, lat_count = dims
    refs = iter(refs)
    take = lambda count: [next(refs) for _ in range(count)]
    sources, results, outs = take(11), take(8), take(2 * lat_count)
    (
        near_nodes,
        gathered,
        crossed,
        w_send,
        nodes,
        w_recv,
        w_self,
        w_agg,
        w_out,
        cotangent,
    ) = held = take(10)
    d_up, d_down, d_gathered, d_crossed, new_nodes, d_pre_b, d_recv_b = kept = take(7)
    (
        mid,
        right,
        left,
        slopes,
        slope_sum,
        recv_half,
        total,
        work,
        agg_b,
        hidden_b,
        d_out_b,
        d_half,
        far,
        near_d,
        sums,
        coarse,
        coarse_d,
        send_hot,
        recv_hot,
        grads,
        in_sems,
        near_sems,
        out_sems,
        grad_sems,
    ) = take(24)
    rows = patch_rows * cols
    depth = nodes.shape[-1]
    pack = coarse_count + patch_rows + 8
    chip_count = lon_count // 2
    half_far = chip_count * pack + patch_rows + 16
    lat, lon = lax.axis_index("lat"), lax.axis_index("lon")
    core, chip = lon % 2, lon // 2
    top_valid, bottom_valid = lat > 0, lat < lat_count - 1
    even_lat = 1 - lat % 2

    def place_of(other):
        apart = other ^ lon
        return (apart % 2) * chip_count + apart // 2

    outer_chip = (chip + chip_count - 1 + 2 * core) % chip_count
    outer_at = half_far + (chip ^ outer_chip) * pack + coarse_count
    inner_at = half_far + chip_count * pack
    right_at = jnp.where(core == 0, inner_at, outer_at)
    left_at = jnp.where(core == 0, outer_at, inner_at)
    tile = 16

    upper, lower = pl.ds(0, cols), pl.ds(cols, cols)
    arriving = [
        pltpu.make_async_copy(
            source, near_nodes.at[pl.ds(aligned(start, cols), cols)], near_sems.at[k]
        )
        for k, (source, start) in enumerate(zip(sources[:2], (even_lat * cols, cols - even_lat * cols)))
    ]
    loads = {}
    for k, (source, target) in enumerate(zip(sources[2:], held[1:])):
        loads[k] = pltpu.make_async_copy(source, target, in_sems.at[k])
    for copy in (loads[3], loads[2], loads[4], *arriving, loads[0], loads[1]):
        copy.start()
    for k in range(5, 9):
        loads[k].start()
    leaving = []

    def leave(source, target, sem):
        leaving.append(pltpu.make_async_copy(source, target, sem))
        leaving[-1].start()

    for k in (3, 2):
        loads[k].wait()
    mid[pl.ds(cols, rows), :] = 0.5 * to_f32(to_bf16(dot(nodes[...], w_send[...])))
    loads[4].wait()
    recv_half[...] = 0.5 * (dot(nodes[...], w_recv[...]) + edge_bias[...])
    for copy in (*arriving, loads[0], loads[1]):
        copy.wait()
    near_half = 0.5 * to_f32(to_bf16(dot(near_nodes[...], w_send[...])))
    same, cross = pl.ds(0, half_far), pl.ds(half_far, half_far)
    far[same, :] = 0.5 * to_f32(to_bf16(dot(gathered[...], w_send[...])))
    far[cross, :] = 0.5 * to_f32(to_bf16(dot(crossed[...], w_send[...])))
    sums[...] = jnp.zeros_like(sums)
    first = lax.broadcasted_iota(jnp.int32, (cols, 1), 0) == 0
    last = lax.broadcasted_iota(jnp.int32, (cols, 1), 0) == cols - 1
    top = jnp.where(top_valid, near_half[:cols], ABSENT)
    bottom = jnp.where(bottom_valid, near_half[cols : 2 * cols], ABSENT)
    right_corner = pl.ds(aligned(right_at + patch_rows, 8), 8)
    left_corner = pl.ds(aligned(left_at + patch_rows, 8), 8)
    top_corner = jnp.where(top_valid, far[right_corner, :][0:1], ABSENT)
    bottom_corner = jnp.where(bottom_valid, far[left_corner, :][0:1], ABSENT)
    mid[pl.ds(0, cols), :] = top
    mid[pl.ds(rows + cols, cols), :] = bottom
    right[pl.ds(0, cols), :] = jnp.where(last, top_corner, pltpu.roll(top, cols - 1, 0))
    left[pl.ds(rows + cols, cols), :] = jnp.where(first, bottom_corner, pltpu.roll(bottom, 1, 0))

    right_place = pl.ds(aligned(right_at, 8), patch_rows)
    left_place = pl.ds(aligned(left_at, 8), patch_rows)
    right_edge, left_edge = far[right_place, :], far[left_place, :]
    for row in range(patch_rows):
        there = pl.ds((row + 1) * cols, cols)
        for lane in range(0, depth, 128):
            lanes = pl.ds(lane, 128)
            block = mid[there, lanes]
            edge = right_edge[row : row + 1, lane : lane + 128]
            right[there, lanes] = jnp.where(last, edge, pltpu.roll(block, cols - 1, 0))
            edge = left_edge[row : row + 1, lane : lane + 128]
            left[there, lanes] = jnp.where(first, edge, pltpu.roll(block, 1, 0))

    senders = ((mid, 2), (mid, 0), (right, 1), (left, 1), (left, 2), (right, 0))

    def edges(step, carry):
        base = aligned(step * tile, tile)
        here = pl.ds(base, tile)
        recv = recv_half[here, :]
        summed = jnp.zeros((tile, depth), jnp.float32)
        slope_total = jnp.zeros((tile, depth), jnp.float32)
        for which, (source, shift) in enumerate(senders):
            half = source[pl.ds(aligned(base + shift * cols, tile), tile), :] + recv
            value, slope = half_sum_and_slope(half)
            summed = summed + value
            slope_total = slope_total + slope
            slopes[which, pl.ds(aligned(base + cols, tile), tile), :] = to_bf16(slope)
        total[here, :] = summed
        slope_sum[here, :] = slope_total
        return carry

    lax.fori_loop(0, rows // tile, edges, 0)

    per_source = long_senders.shape[1]
    coarse_lane = lax.broadcasted_iota(jnp.int32, (1, coarse.shape[0]), 1)
    slot_lane = lax.broadcasted_iota(jnp.int32, (1, coarse_count), 1)
    for source in range(lon_count):
        first_id = place_of(source) * coarse_count
        for edge in range(per_source):
            row = pl.ds(source * per_source + edge, 1)
            send_hot[row, :] = to_f32(coarse_lane == first_id + long_senders[source, edge])
            recv_hot[row, :] = to_f32(slot_lane == long_receivers[source, edge])
    for source in range(lon_count):
        start = source // chip_count * half_far + source % chip_count * pack
        coarse[pl.ds(source * coarse_count, coarse_count), :] = far[pl.ds(start, coarse_count), :]
    coarse_recv = 0.5 * (dot(gathered[pl.ds(0, coarse_count), :], w_recv[...]) + edge_bias[...])
    long_half = dot_exact(send_hot[...], coarse[...]) + dot_exact(
        recv_hot[...], coarse_recv
    )
    long_value, long_slope = half_sum_and_slope(long_half)
    coarse_d[...] = dot_exact_tn(recv_hot[...], long_value)
    for k in range(coarse_count):
        spot = pl.ds(slots[k], 1)
        total[spot, :] = total[spot, :] + coarse_d[pl.ds(k, 1), :]

    step_rows = 256
    blocks = [pl.ds(start, step_rows) for start in range(0, rows, step_rows)]
    loads[5].wait()
    loads[6].wait()
    for block in blocks:
        agg_b[block, :] = to_bf16(total[block, :])
        work[block, :] = 0.5 * (
            dot(nodes[block, :], w_self[...])
            + dot(agg_b[block, :], w_agg[...])
            + node_bias[...]
        )

    def activate(step, carry):
        here = pl.ds(aligned(step * tile, tile), tile)
        half = work[here, :]
        hidden_b[here, :] = to_bf16(half + half * jnp.tanh(half))
        return carry

    lax.fori_loop(0, rows // tile, activate, 0, unroll=4)
    loads[7].wait()
    for block in blocks:
        total[block, :] = dot(hidden_b[block, :], w_out[...])

    wide = 64
    loads[8].wait()

    def normalise(step, gain_sum):
        here = pl.ds(aligned(step * wide, wide), wide)
        output = total[here, :]
        cot = to_f32(cotangent[here, :])
        d_norm = cot * gain[...]
        d_mean = jnp.mean(d_norm, axis=-1, keepdims=True)
        centred = output - jnp.mean(output, axis=-1, keepdims=True)
        inv_std = lax.rsqrt(jnp.mean(centred * centred, axis=-1, keepdims=True) + epsilon)
        normed = centred * inv_std
        new_nodes[here, :] = to_bf16(to_f32(nodes[here, :]) + gain[...] * normed)
        d_dot = jnp.mean(d_norm * normed, axis=-1, keepdims=True)
        d_out_b[here, :] = to_bf16(inv_std * (d_norm - d_mean - normed * d_dot))
        return gain_sum + eight_rows(cot * normed)

    nothing = jnp.zeros((8, depth), jnp.float32)
    sums[2] = lax.fori_loop(0, rows // wide, normalise, nothing, unroll=4)
    leave(new_nodes, results[0], out_sems.at[0])

    for block in blocks:
        total[block, :] = dot_nt(d_out_b[block, :], w_out[...])

    def deactivate(step, bias_sum):
        here = pl.ds(aligned(step * tile, tile), tile)
        slope = half_sum_and_slope(work[here, :])[1]
        d_pre = total[here, :] * (0.5 * slope)
        d_pre_b[here, :] = to_bf16(d_pre)
        return bias_sum + eight_rows(d_pre)

    sums[1] = lax.fori_loop(0, rows // tile, deactivate, nothing, unroll=4)
    leave(d_pre_b, results[1], out_sems.at[1])
    share = depth // (2 * lat_count)

    def put(which, half_at, values):
        block = to_bf16(values)
        for place in range(lat_count):
            grads[half_at ^ core, lat ^ place, pl.ds(which * share, share), :] = block[
                place * share : (place + 1) * share
            ]

    for half_at in range(2):
        columns = pl.ds(half_at * (depth // 2), depth // 2)
        put(2, half_at, dot_tn(nodes[:, columns], d_pre_b[...]))
        put(3, half_at, dot_tn(agg_b[:, columns], d_pre_b[...]))
        put(4, half_at, dot_tn(hidden_b[:, columns], d_out_b[...]))
    for part in range(2):
        for spot in range(lat_count):
            place = pl.ds(2 * share, 3 * share)
            leave(
                grads.at[part, spot, place],
                outs[part * lat_count + spot].at[place],
                grad_sems.at[part, spot, 0],
            )
    d_half[pl.ds(0, cols), :] = jnp.zeros((cols, depth), jnp.float32)
    d_half[pl.ds(rows + cols, cols), :] = jnp.zeros((cols, depth), jnp.float32)
    for which in (0, 4):
        slopes[which, pl.ds(0, cols), :] = jnp.zeros((cols, depth), jnp.bfloat16)
    for which in (1, 5):
        slopes[which, pl.ds(rows + cols, cols), :] = jnp.zeros((cols, depth), jnp.bfloat16)
    for start in range(0, rows, step_rows):
        d_sum = dot_nt(d_pre_b[pl.ds(start, step_rows), :], w_agg[...])
        d_half[pl.ds(start + cols, step_rows), :] = 0.5 * to_f32(to_bf16(d_sum))

    def slope_times(which, place, lanes):
        return to_f32(slopes[which, place, lanes]) * d_half[place, lanes]

    def receive(step, bias_sum):
        base = aligned(step * tile, tile)
        here = pl.ds(base, tile)
        value = d_half[pl.ds(aligned(base + cols, tile), tile), :] * slope_sum[here, :]
        total[here, :] = value
        return bias_sum + eight_rows(value)

    sums[0] = lax.fori_loop(0, rows // tile, receive, nothing, unroll=4)
    far[...] = jnp.zeros_like(far)

    edge_place = lax.broadcasted_iota(jnp.int32, (patch_rows, 1), 0)
    for lane in range(0, depth, 128):
        lanes = pl.ds(lane, 128)
        right_edge = jnp.zeros((patch_rows, 128), jnp.float32)
        left_edge = jnp.zeros((patch_rows, 128), jnp.float32)
        for row in range(patch_rows):
            above_row, out = pl.ds(row * cols, cols), pl.ds(row * cols, cols)
            here, below_row = pl.ds((row + 1) * cols, cols), pl.ds((row + 2) * cols, cols)
            to_mid = slope_times(0, above_row, lanes) + slope_times(1, below_row, lanes)
            to_right = slope_times(2, here, lanes) + slope_times(5, below_row, lanes)
            to_left = slope_times(3, here, lanes) + slope_times(4, above_row, lanes)
            work[out, lanes] = (
                to_mid
                + jnp.where(first, 0.0, pltpu.roll(to_right, 1, 0))
                + jnp.where(last, 0.0, pltpu.roll(to_left, cols - 1, 0))
            )
            right_edge = jnp.where(edge_place == row, to_right[cols - 1 : cols], right_edge)
            left_edge = jnp.where(edge_place == row, to_left[0:1], left_edge)
        far[right_place, lanes] = right_edge
        far[left_place, lanes] = left_edge
    row_first, row_last = pl.ds(cols, cols), pl.ds(rows, cols)
    eight = lax.broadcasted_iota(jnp.int32, (8, 1), 0)
    for lane in range(0, depth, 128):
        lanes = pl.ds(lane, 128)
        to_right = slope_times(5, row_first, lanes)
        to_left = slope_times(4, row_last, lanes)
        up = slope_times(1, row_first, lanes) + jnp.where(first, 0.0, pltpu.roll(to_right, 1, 0))
        down = slope_times(0, row_last, lanes) + jnp.where(
            last, 0.0, pltpu.roll(to_left, cols - 1, 0)
        )
        near_d[upper, lanes] = to_bf16(up)
        near_d[lower, lanes] = to_bf16(down)
        far[right_corner, lanes] = jnp.where(eight == 0, to_right[cols - 1 : cols], 0.0)
        far[left_corner, lanes] = jnp.where(eight == 0, to_left[0:1], 0.0)
    d_up[...] = near_d[upper, :]
    d_down[...] = near_d[lower, :]
    leave(d_up, results[4], out_sems.at[4])
    leave(d_down, results[5], out_sems.at[5])

    for k in range(coarse_count):
        coarse_d[pl.ds(k, 1), :] = d_half[pl.ds(slots[k] + cols, 1), :]
    long_d = dot_exact(recv_hot[...], coarse_d[...]) * long_slope
    sums[0] += eight_rows(long_d)
    coarse_d[...] = dot_exact_tn(recv_hot[...], long_d)
    for k in range(coarse_count):
        spot = pl.ds(slots[k], 1)
        total[spot, :] = total[spot, :] + coarse_d[pl.ds(k, 1), :]
    coarse[...] = dot_exact_tn(send_hot[...], long_d)
    for source in range(lon_count):
        start = source // chip_count * half_far + source % chip_count * pack
        far[pl.ds(start, coarse_count), :] = coarse[pl.ds(source * coarse_count, coarse_count), :]
    d_gathered[...] = to_bf16(far[same, :])
    d_crossed[...] = to_bf16(far[cross, :])
    leave(d_gathered, results[6], out_sems.at[6])
    leave(d_crossed, results[7], out_sems.at[7])
    for block in blocks:
        d_recv_b[block, :] = to_bf16(total[block, :])
        agg_b[block, :] = to_bf16(work[block, :])
    leave(d_recv_b, results[2], out_sems.at[2])
    leave(agg_b, results[3], out_sems.at[3])
    for half_at in range(2):
        columns = pl.ds(half_at * (depth // 2), depth // 2)
        put(0, half_at, dot_tn(nodes[:, columns], agg_b[...])
            + dot_tn(near_nodes[:, columns], near_d[...])
            + dot_tn(gathered[:, columns], d_gathered[...])
            + dot_tn(crossed[:, columns], d_crossed[...]))
        put(1, half_at, dot_tn(nodes[:, columns], d_recv_b[...]))
    place = lax.broadcasted_iota(jnp.int32, (16, depth), 0)
    vectors = jnp.zeros((16, depth), jnp.float32)
    for which in range(3):
        vectors = jnp.where(place == which, jnp.sum(sums[which], axis=0, keepdims=True), vectors)
    for part in range(2):
        for spot in range(lat_count):
            grads[part, spot, pl.ds(5 * share, 16), :] = to_bf16(vectors)
    for part in range(2):
        for spot in range(lat_count):
            for k, place in ((1, pl.ds(0, 2 * share)), (2, pl.ds(5 * share, 16))):
                leave(
                    grads.at[part, spot, place],
                    outs[part * lat_count + spot].at[place],
                    grad_sems.at[part, spot, k],
                )
    for copy in leaving:
        copy.wait()


def update(dims, ints, vectors, arrays):
    patch_rows, cols, lon_count, coarse_count, lat_count = dims
    rows, depth = patch_rows * cols, vectors[0].shape[-1]
    share = depth // (2 * lat_count)
    edge_count = ints[1].shape[0] * ints[1].shape[1]
    coarse_ids = lon_count * coarse_count
    far_rows = lon_count * (coarse_count + patch_rows + 8) + 2 * (patch_rows + 16)
    near_rows = 2 * cols
    long_rows = rows + 2 * cols
    out = lambda *size: jax.ShapeDtypeStruct(size, jnp.bfloat16)
    full = lambda *size: pltpu.VMEM(size, jnp.float32)
    half = lambda *size: pltpu.VMEM(size, jnp.bfloat16)
    smem, vmem = pl.BlockSpec(memory_space=pltpu.SMEM), pl.BlockSpec(memory_space=pltpu.VMEM)
    anywhere = pl.BlockSpec(memory_space=pl.ANY)
    weight = half(depth, depth)
    return pl.pallas_call(
        functools.partial(update_kernel, dims),
        in_specs=[smem] * len(ints) + [vmem] * len(vectors) + [anywhere] * len(arrays),
        out_specs=[anywhere] * (8 + 2 * lat_count),
        out_shape=[out(rows, depth)] * 4
        + [out(cols, depth)] * 2
        + [out(far_rows // 2, depth)] * 2
        + [out(5 * share + 16, depth)] * (2 * lat_count),
        scratch_shapes=[half(near_rows, depth)]
        + [half(far_rows // 2, depth)] * 2
        + [weight, half(rows, depth)]
        + [weight] * 4
        + [half(rows, depth)]
        + [half(cols, depth)] * 2
        + [half(far_rows // 2, depth)] * 2
        + [half(rows, depth)] * 3
        + [full(long_rows, depth)] * 3
        + [half(6, long_rows, depth)]
        + [full(rows, depth)] * 4
        + [half(rows, depth)] * 3
        + [full(long_rows, depth), full(far_rows, depth)]
        + [half(near_rows, depth)]
        + [
            full(3, 8, depth),
            full(coarse_ids, depth),
            full(coarse_count, depth),
            full(edge_count, coarse_ids),
            full(edge_count, coarse_count),
            half(2, lat_count, 5 * share + 16, depth),
            pltpu.SemaphoreType.DMA((9,)),
            pltpu.SemaphoreType.DMA((2,)),
            pltpu.SemaphoreType.DMA((8,)),
            pltpu.SemaphoreType.DMA((2, lat_count, 3)),
        ],
        compiler_params=pltpu.CompilerParams(vmem_limit_bytes=63 * MIB),
        cost_estimate=pl.CostEstimate(
            flops=26 * rows * depth * depth, bytes_accessed=20_000_000, transcendentals=0
        ),
        name="update",
    )(*ints, *vectors, *arrays)


def finish_kernel(dims, scale, slots, *refs):
    patch_rows, cols, _, coarse_count, lat_count = dims
    rows = patch_rows * cols
    (
        cotangent,
        d_pre_b,
        d_recv_b,
        d_send,
        one,
        two,
        back,
        w_self,
        w_recv,
        w_send,
        summed,
        grad_nodes,
        *vectors,
        total,
    ) = refs
    step_rows = 256
    for start in range(0, rows, step_rows):
        block = pl.ds(start, step_rows)
        total[block, :] = to_f32(d_send[block, :])
    start = (1 - lax.axis_index("lat") % 2) * (rows - cols)
    for start, part in ((start, one), (rows - cols - start, two)):
        total[pl.ds(aligned(start, cols), cols), :] += to_f32(part[...])
    for which, vector in enumerate(vectors):
        vector[...] = scale * summed[pl.ds(summed.shape[0] - 8 + which, 1), :]
    returned = back[...]
    outer = jnp.where(lax.axis_index("lon") % 2 == 0, 0, cols - 1)
    for row in range(patch_rows):
        for spot, at in ((outer, 0), (cols - 1 - outer, patch_rows)):
            one = coarse_count + at + row
            total[pl.ds(row * cols + spot, 1), :] += returned[one : one + 1]
    for k in range(coarse_count):
        total[pl.ds(slots[k], 1), :] += returned[k : k + 1]
    for start in range(0, rows, step_rows):
        block = pl.ds(start, step_rows)
        grad_nodes[block, :] = to_bf16(
            to_f32(cotangent[block, :])
            + dot_nt(d_pre_b[block, :], w_self[...])
            + dot_nt(d_recv_b[block, :], w_recv[...])
            + dot_nt(to_bf16(total[block, :]), w_send[...])
        )


def finish(dims, scale, slots, arrays):
    rows, depth = arrays[0].shape
    smem, vmem = pl.BlockSpec(memory_space=pltpu.SMEM), pl.BlockSpec(memory_space=pltpu.VMEM)
    return pl.pallas_call(
        functools.partial(finish_kernel, dims, scale),
        in_specs=[smem] + [vmem] * len(arrays),
        out_specs=[vmem] * 4,
        out_shape=[jax.ShapeDtypeStruct((rows, depth), jnp.bfloat16)]
        + [jax.ShapeDtypeStruct((1, depth), jnp.float32)] * 3,
        scratch_shapes=[pltpu.VMEM((rows, depth), jnp.float32)],
        compiler_params=pltpu.CompilerParams(vmem_limit_bytes=63 * MIB),
        cost_estimate=pl.CostEstimate(
            flops=6 * rows * depth * depth, bytes_accessed=8_000_000, transcendentals=0
        ),
        name="finish",
    )(slots, *arrays)


def swapped(values, axis, bit):
    count = lax.axis_size(axis)
    return lax.ppermute(values, axis, [(i, i ^ bit) for i in range(count)])


def summed_part(mine, other, d_crossed, returning, borders):
    lat_count, depth = len(mine), mine[0].shape[-1]
    chip_count = lax.axis_size("lon") // 2
    chip = lax.axis_index("lon") // 2
    share = depth // (2 * lat_count)
    order = list(range(lat_count - 1, -1, -1))
    crossed = {step: swapped(other[step], "lon", 1) for step in order}
    messages = [to_bf16(to_f32(mine[step]) + to_f32(crossed[step])) for step in order[:-1]]
    messages[0], d_crossed = lax.optimization_barrier((messages[0], d_crossed))
    received = [swapped(part, "lat", step) for part, step in zip(messages, order)]
    received, returned = lax.optimization_barrier((received, returning(d_crossed)))
    total = to_f32(mine[0]) + to_f32(crossed[0])
    for part in received:
        total = total + to_f32(part)
    total = to_bf16(total)
    vectors = total[5 * share : 5 * share + 8]
    parts = total[: 5 * share].reshape(5, chip_count, share // chip_count, depth)

    def message_for(step):
        part = lax.dynamic_index_in_dim(parts, chip ^ step, axis=1, keepdims=False)
        return jnp.concatenate([part.reshape(-1, depth), vectors])

    received = [swapped(message_for(step), "lon", 2 * step) for step in range(1, chip_count)]
    received[0], returned = lax.optimization_barrier((received[0], returned))
    received, bordered = lax.optimization_barrier((received, borders(returned)))
    total = to_f32(message_for(0))
    for part in received:
        total = total + to_f32(part)
    return total, returned, bordered


def gathered_share(total, lat_count):
    depth = total.shape[-1]
    share = depth // (2 * lat_count)
    chip_count = lax.axis_size("lon") // 2
    chip = lax.axis_index("lon") // 2
    part = to_bf16(total[: 5 * share // chip_count])
    parts = jnp.stack([part] + [swapped(part, "lon", 2 * k) for k in range(1, chip_count)])
    parts = parts[chip ^ jnp.arange(chip_count)].reshape(chip_count, 5, -1, depth)
    return jnp.transpose(parts, (1, 0, 2, 3)).reshape(5 * share, depth)


def unpack_kernel(pieces, scale, *refs):
    count = len(refs)
    held, staged, load_sems, sems = refs[count - 4 :]
    outs = refs[count - 9 : count - 4]
    depth = outs[0].shape[-1]
    share = depth // (2 * lax.axis_size("lat"))
    core, lat = lax.axis_index("lon") % 2, lax.axis_index("lat")
    loads = [
        pltpu.make_async_copy(refs[k], held.at[k], load_sems.at[k]) for k in range(len(pieces))
    ]
    for load in loads:
        load.start()
    copies = []
    for k, (flip, step) in enumerate(pieces):
        loads[k].wait()
        start = (core ^ flip) * (depth // 2) + (lat ^ step) * share
        place = pl.ds(aligned(start, share), share)
        for which in range(5):
            staged[k, which] = scale * to_f32(held[k, pl.ds(which * share, share), :])
            copies.append(
                pltpu.make_async_copy(
                    staged.at[k, which], outs[which].at[place], sems.at[k, which]
                )
            )
            copies[-1].start()
    for copy in copies:
        copy.wait()


def unpack(pieces, scale, shares, begun=()):
    depth = shares[0].shape[-1]
    rows = shares[0].shape[0]
    anywhere = pl.BlockSpec(memory_space=pl.ANY)
    return pl.pallas_call(
        functools.partial(unpack_kernel, pieces, scale),
        in_specs=[anywhere] * (len(shares) + len(begun)),
        out_specs=[anywhere] * 5,
        out_shape=[jax.ShapeDtypeStruct((depth, depth), jnp.float32)] * 5,
        scratch_shapes=[
            pltpu.VMEM((len(shares), rows, depth), jnp.bfloat16),
            pltpu.VMEM((len(shares), 5, rows // 5, depth), jnp.float32),
            pltpu.SemaphoreType.DMA((len(shares),)),
            pltpu.SemaphoreType.DMA((len(shares), 5)),
        ],
        input_output_aliases={len(shares) + k: k for k in range(len(begun))},
        compiler_params=pltpu.CompilerParams(vmem_limit_bytes=10 * MIB),
        cost_estimate=pl.CostEstimate(flops=0, bytes_accessed=8_000_000, transcendentals=0),
        name=f"unpack_{len(pieces)}",
    )(*shares, *begun)


def on_device(
    nodes,
    cotangent,
    w_send,
    w_recv,
    edge_bias,
    w_self,
    w_agg,
    node_bias,
    w_out,
    gain,
    coarse_slots,
    long_senders,
    long_receivers,
):
    patch_rows, cols, depth = nodes.shape
    rows = patch_rows * cols
    lat_count, lon_count = lax.axis_size("lat"), lax.axis_size("lon")
    chip_count = lon_count // 2
    lon = lax.axis_index("lon")
    scale = float(rows * lat_count * lon_count) ** (-0.5)
    slots = coarse_slots.reshape(-1)
    coarse_count = slots.shape[0]
    dims = (patch_rows, cols, lon_count, coarse_count, lat_count)
    flat = nodes.reshape(rows, depth)
    cot = cotangent.reshape(rows, depth)

    odd = lax.axis_index("lat") % 2 == 1
    firsts = [(i, i ^ 1) for i in range(lat_count)]
    seconds = [pair for i in range(1, lat_count - 1, 2) for pair in ((i, i + 1), (i + 1, i))]

    def paired(to_above, to_below):
        one = lax.ppermute(jnp.where(odd, to_above, to_below), "lat", firsts)
        return one, lax.ppermute(jnp.where(odd, to_below, to_above), "lat", seconds)

    one, two = paired(flat[:cols], flat[-cols:])
    packed = pack_nodes(cols, slots, flat)
    outer_is_left = lon % 2 == 0
    corners = jnp.where(odd, one[:1], two[:1]), jnp.where(odd, two[-1:], one[-1:])
    outer_corner = jnp.where(outer_is_left, corners[0], corners[1])
    inner_corner = jnp.where(outer_is_left, corners[1], corners[0])
    outer_end, filler = coarse_count + patch_rows, jnp.zeros((15, depth), jnp.bfloat16)
    message = jnp.concatenate([packed[:outer_end], outer_corner, filler[:7]])
    chips = [swapped(message, "lon", 2 * k) for k in range(1, chip_count)]
    gathered = jnp.concatenate([message, *chips, packed[outer_end:], inner_corner, filler])
    crossed = swapped(gathered, "lon", 1)
    outs = update(
        dims,
        (slots, long_senders.reshape(lon_count, -1), long_receivers.reshape(lon_count, -1)),
        (edge_bias[None], node_bias[None], gain[None]),
        (
            one,
            two,
            gathered,
            crossed,
            w_send,
            flat,
            w_recv,
            w_self,
            w_agg,
            w_out,
            cot,
        ),
    )
    new_nodes, d_pre_b, d_recv_b, d_send, d_up, d_down, d_gathered, d_crossed = outs[:8]
    mine, other = outs[8 : 8 + lat_count], outs[8 + lat_count :]

    def returning(d_crossed):
        chips = to_bf16(to_f32(d_gathered) + to_f32(swapped(d_crossed, "lon", 1)))
        inner = to_f32(chips[-patch_rows - 16 :])
        parts = chips[: -patch_rows - 16].reshape(chip_count, -1, depth)
        received = [swapped(parts[step], "lon", 2 * step) for step in range(1, chip_count)]
        return sum([to_f32(one) for one in received], to_f32(parts[0])), inner

    def borders(returned):
        outer_corner, inner_corner = returned[0][outer_end :][:1], returned[1][patch_rows:][:1]
        up_corner = jnp.where(outer_is_left, outer_corner, inner_corner)
        down_corner = jnp.where(outer_is_left, inner_corner, outer_corner)
        ups = jnp.concatenate([to_bf16(to_f32(d_up[:1]) + up_corner), d_up[1:]])
        downs = jnp.concatenate([d_down[:-1], to_bf16(to_f32(d_down[-1:]) + down_corner)])
        return paired(ups, downs)

    total, (back, inner), bordered = summed_part(mine, other, d_crossed, returning, borders)
    back = jnp.concatenate([back[:outer_end], inner[:patch_rows]])
    grad_nodes, *vectors = finish(
        dims,
        scale,
        slots,
        (
            cot,
            d_pre_b,
            d_recv_b,
            d_send,
            *bordered,
            back,
            w_self,
            w_recv,
            w_send,
            total,
        ),
    )

    ready = gathered_share(total, lat_count)
    shares = [swapped(ready, "lat", step) for step in range(1, lat_count)]
    outs = unpack([(0, 0)], scale, [ready])
    shares, grad_nodes, outs = lax.optimization_barrier((shares, grad_nodes, outs))
    crossed = [swapped(part, "lon", 1) for part in (ready, *shares)]
    pieces = [(1, 0)] + [(flip, step) for step in range(1, lat_count) for flip in range(2)]
    parts = [crossed[step] if flip else shares[step - 1] for flip, step in pieces]
    outs = unpack(pieces, scale, parts, outs)
    return (
        new_nodes.reshape(patch_rows, cols, depth),
        grad_nodes.reshape(patch_rows, cols, depth),
        outs[0],
        outs[1],
        vectors[0][0],
        outs[2],
        outs[3],
        vectors[1][0],
        outs[4],
        vectors[2][0],
    )


def solution(mesh):
    patches = P("lat", "lon", None)
    edges = P("lat", "lon", None, None)
    return jax.shard_map(
        on_device,
        mesh=mesh,
        in_specs=(patches, patches) + (P(),) * 8 + (patches, edges, edges),
        out_specs=(patches, patches) + (P(),) * 8,
        check_vma=False,
    )
```

```python
import functools

import jax
import jax.numpy as jnp
from jax import lax
from jax.experimental import pallas as pl
from jax.experimental.pallas import tpu as pltpu
from jax.sharding import PartitionSpec as P

epsilon = 1e-05
EXACT = lax.Precision.HIGHEST
ABSENT = -1000.0
MIB = 1024 * 1024


def dot(left, right):
    return jnp.dot(left, right, preferred_element_type=jnp.float32)


def dot_nt(left, right):
    return lax.dot_general(left, right, (((1,), (1,)), ((), ())), preferred_element_type=jnp.float32)


def dot_tn(left, right):
    return lax.dot_general(left, right, (((0,), (0,)), ((), ())), preferred_element_type=jnp.float32)


def dot_exact(left, right):
    return jnp.dot(left, right, preferred_element_type=jnp.float32, precision=EXACT)


def dot_exact_tn(left, right):
    return lax.dot_general(
        left, right, (((0,), (0,)), ((), ())), preferred_element_type=jnp.float32, precision=EXACT
    )


def to_bf16(values):
    return values.astype(jnp.bfloat16)


def to_f32(values):
    return values.astype(jnp.float32)


def half_sum_and_slope(half):
    curve = jnp.tanh(half)
    part = half * curve
    return half + part, (1.0 + curve) * (1.0 + half - part)


def eight_rows(values):
    return jnp.sum(values.reshape(-1, 8, values.shape[-1]), axis=0)


def aligned(start, multiple):
    return pl.multiple_of(start, multiple)


def pack_kernel(cols, slots, nodes, packed):
    rows = nodes.shape[0]
    count, patch_rows = slots.shape[0], rows // cols
    size = count + 2 * patch_rows
    place = lax.broadcasted_iota(jnp.int32, (size, 1), 0)
    core = lax.axis_index("lon") % 2
    outer = jnp.where(core == 0, 0, cols - 1)
    wanted = jnp.where(
        place < count + patch_rows,
        (place - count) * cols + outer,
        (place - count - patch_rows) * cols + cols - 1 - outer,
    )
    for k in range(count):
        wanted = jnp.where(place == k, slots[k], wanted)
    column = lax.broadcasted_iota(jnp.int32, (size, rows), 1)
    packed[...] = to_bf16(dot(to_bf16(to_f32(column == wanted)), nodes[...]))


def pack_nodes(cols, slots, nodes):
    rows, depth = nodes.shape
    count = slots.shape[0] + 2 * (rows // cols)
    smem, vmem = pl.BlockSpec(memory_space=pltpu.SMEM), pl.BlockSpec(memory_space=pltpu.VMEM)
    return pl.pallas_call(
        functools.partial(pack_kernel, cols),
        in_specs=[smem, vmem],
        out_specs=vmem,
        out_shape=jax.ShapeDtypeStruct((count, depth), jnp.bfloat16),
        name="pack_nodes",
    )(slots, nodes)


def update_kernel(dims, slots, long_senders, long_receivers, edge_bias, node_bias, gain, *refs):
    patch_rows, cols, lon_count, coarse_count, lat_count = dims
    refs = iter(refs)
    take = lambda count: [next(refs) for _ in range(count)]
    sources, results, outs = take(11), take(8), take(2 * lat_count)
    (
        near_nodes,
        gathered,
        crossed,
        w_send,
        nodes,
        w_recv,
        w_self,
        w_agg,
        w_out,
        cotangent,
    ) = held = take(10)
    d_up, d_down, d_gathered, d_crossed, new_nodes, d_pre_b, d_recv_b = kept = take(7)
    (
        mid,
        right,
        left,
        slopes,
        slope_sum,
        recv_half,
        total,
        work,
        agg_b,
        hidden_b,
        d_out_b,
        d_half,
        far,
        near_d,
        sums,
        coarse,
        coarse_d,
        send_hot,
        recv_hot,
        grads,
        in_sems,
        near_sems,
        out_sems,
        grad_sems,
    ) = take(24)
    rows = patch_rows * cols
    depth = nodes.shape[-1]
    pack = coarse_count + patch_rows + 8
    chip_count = lon_count // 2
    half_far = chip_count * pack + patch_rows + 16
    lat, lon = lax.axis_index("lat"), lax.axis_index("lon")
    core, chip = lon % 2, lon // 2
    top_valid, bottom_valid = lat > 0, lat < lat_count - 1
    even_lat = 1 - lat % 2

    def place_of(other):
        apart = other ^ lon
        return (apart % 2) * chip_count + apart // 2

    outer_chip = (chip + chip_count - 1 + 2 * core) % chip_count
    outer_at = half_far + (chip ^ outer_chip) * pack + coarse_count
    inner_at = half_far + chip_count * pack
    right_at = jnp.where(core == 0, inner_at, outer_at)
    left_at = jnp.where(core == 0, outer_at, inner_at)
    tile = 16

    upper, lower = pl.ds(0, cols), pl.ds(cols, cols)
    arriving = [
        pltpu.make_async_copy(
            source, near_nodes.at[pl.ds(aligned(start, cols), cols)], near_sems.at[k]
        )
        for k, (source, start) in enumerate(zip(sources[:2], (even_lat * cols, cols - even_lat * cols)))
    ]
    loads = {}
    for k, (source, target) in enumerate(zip(sources[2:], held[1:])):
        loads[k] = pltpu.make_async_copy(source, target, in_sems.at[k])
    for copy in (loads[3], loads[2], loads[4], *arriving, loads[0], loads[1]):
        copy.start()
    for k in range(5, 9):
        loads[k].start()
    leaving = []

    def leave(source, target, sem):
        leaving.append(pltpu.make_async_copy(source, target, sem))
        leaving[-1].start()

    for k in (3, 2):
        loads[k].wait()
    mid[pl.ds(cols, rows), :] = 0.5 * to_f32(to_bf16(dot(nodes[...], w_send[...])))
    loads[4].wait()
    recv_half[...] = 0.5 * (dot(nodes[...], w_recv[...]) + edge_bias[...])
    for copy in (*arriving, loads[0], loads[1]):
        copy.wait()
    near_half = 0.5 * to_f32(to_bf16(dot(near_nodes[...], w_send[...])))
    same, cross = pl.ds(0, half_far), pl.ds(half_far, half_far)
    far[same, :] = 0.5 * to_f32(to_bf16(dot(gathered[...], w_send[...])))
    far[cross, :] = 0.5 * to_f32(to_bf16(dot(crossed[...], w_send[...])))
    sums[...] = jnp.zeros_like(sums)
    first = lax.broadcasted_iota(jnp.int32, (cols, 1), 0) == 0
    last = lax.broadcasted_iota(jnp.int32, (cols, 1), 0) == cols - 1
    top = jnp.where(top_valid, near_half[:cols], ABSENT)
    bottom = jnp.where(bottom_valid, near_half[cols : 2 * cols], ABSENT)
    right_corner = pl.ds(aligned(right_at + patch_rows, 8), 8)
    left_corner = pl.ds(aligned(left_at + patch_rows, 8), 8)
    top_corner = jnp.where(top_valid, far[right_corner, :][0:1], ABSENT)
    bottom_corner = jnp.where(bottom_valid, far[left_corner, :][0:1], ABSENT)
    mid[pl.ds(0, cols), :] = top
    mid[pl.ds(rows + cols, cols), :] = bottom
    right[pl.ds(0, cols), :] = jnp.where(last, top_corner, pltpu.roll(top, cols - 1, 0))
    left[pl.ds(rows + cols, cols), :] = jnp.where(first, bottom_corner, pltpu.roll(bottom, 1, 0))

    right_place = pl.ds(aligned(right_at, 8), patch_rows)
    left_place = pl.ds(aligned(left_at, 8), patch_rows)
    right_edge, left_edge = far[right_place, :], far[left_place, :]
    for row in range(patch_rows):
        there = pl.ds((row + 1) * cols, cols)
        for lane in range(0, depth, 128):
            lanes = pl.ds(lane, 128)
            block = mid[there, lanes]
            edge = right_edge[row : row + 1, lane : lane + 128]
            right[there, lanes] = jnp.where(last, edge, pltpu.roll(block, cols - 1, 0))
            edge = left_edge[row : row + 1, lane : lane + 128]
            left[there, lanes] = jnp.where(first, edge, pltpu.roll(block, 1, 0))

    senders = ((mid, 2), (mid, 0), (right, 1), (left, 1), (left, 2), (right, 0))

    def edges(step, carry):
        base = aligned(step * tile, tile)
        here = pl.ds(base, tile)
        recv = recv_half[here, :]
        summed = jnp.zeros((tile, depth), jnp.float32)
        slope_total = jnp.zeros((tile, depth), jnp.float32)
        for which, (source, shift) in enumerate(senders):
            half = source[pl.ds(aligned(base + shift * cols, tile), tile), :] + recv
            value, slope = half_sum_and_slope(half)
            summed = summed + value
            slope_total = slope_total + slope
            slopes[which, pl.ds(aligned(base + cols, tile), tile), :] = to_bf16(slope)
        total[here, :] = summed
        slope_sum[here, :] = slope_total
        return carry

    lax.fori_loop(0, rows // tile, edges, 0)

    per_source = long_senders.shape[1]
    coarse_lane = lax.broadcasted_iota(jnp.int32, (1, coarse.shape[0]), 1)
    slot_lane = lax.broadcasted_iota(jnp.int32, (1, coarse_count), 1)
    for source in range(lon_count):
        first_id = place_of(source) * coarse_count
        for edge in range(per_source):
            row = pl.ds(source * per_source + edge, 1)
            send_hot[row, :] = to_f32(coarse_lane == first_id + long_senders[source, edge])
            recv_hot[row, :] = to_f32(slot_lane == long_receivers[source, edge])
    for source in range(lon_count):
        start = source // chip_count * half_far + source % chip_count * pack
        coarse[pl.ds(source * coarse_count, coarse_count), :] = far[pl.ds(start, coarse_count), :]
    coarse_recv = 0.5 * (dot(gathered[pl.ds(0, coarse_count), :], w_recv[...]) + edge_bias[...])
    long_half = dot_exact(send_hot[...], coarse[...]) + dot_exact(
        recv_hot[...], coarse_recv
    )
    long_value, long_slope = half_sum_and_slope(long_half)
    coarse_d[...] = dot_exact_tn(recv_hot[...], long_value)
    for k in range(coarse_count):
        spot = pl.ds(slots[k], 1)
        total[spot, :] = total[spot, :] + coarse_d[pl.ds(k, 1), :]

    step_rows = 256
    blocks = [pl.ds(start, step_rows) for start in range(0, rows, step_rows)]
    loads[5].wait()
    loads[6].wait()
    for block in blocks:
        agg_b[block, :] = to_bf16(total[block, :])
        work[block, :] = 0.5 * (
            dot(nodes[block, :], w_self[...])
            + dot(agg_b[block, :], w_agg[...])
            + node_bias[...]
        )

    def activate(step, carry):
        here = pl.ds(aligned(step * tile, tile), tile)
        half = work[here, :]
        hidden_b[here, :] = to_bf16(half + half * jnp.tanh(half))
        return carry

    lax.fori_loop(0, rows // tile, activate, 0, unroll=4)
    loads[7].wait()
    for block in blocks:
        total[block, :] = dot(hidden_b[block, :], w_out[...])

    wide = 64
    loads[8].wait()

    def normalise(step, gain_sum):
        here = pl.ds(aligned(step * wide, wide), wide)
        output = total[here, :]
        cot = to_f32(cotangent[here, :])
        d_norm = cot * gain[...]
        d_mean = jnp.mean(d_norm, axis=-1, keepdims=True)
        centred = output - jnp.mean(output, axis=-1, keepdims=True)
        inv_std = lax.rsqrt(jnp.mean(centred * centred, axis=-1, keepdims=True) + epsilon)
        normed = centred * inv_std
        new_nodes[here, :] = to_bf16(to_f32(nodes[here, :]) + gain[...] * normed)
        d_dot = jnp.mean(d_norm * normed, axis=-1, keepdims=True)
        d_out_b[here, :] = to_bf16(inv_std * (d_norm - d_mean - normed * d_dot))
        return gain_sum + eight_rows(cot * normed)

    nothing = jnp.zeros((8, depth), jnp.float32)
    sums[2] = lax.fori_loop(0, rows // wide, normalise, nothing, unroll=4)
    leave(new_nodes, results[0], out_sems.at[0])

    for block in blocks:
        total[block, :] = dot_nt(d_out_b[block, :], w_out[...])

    def deactivate(step, bias_sum):
        here = pl.ds(aligned(step * tile, tile), tile)
        slope = half_sum_and_slope(work[here, :])[1]
        d_pre = total[here, :] * (0.5 * slope)
        d_pre_b[here, :] = to_bf16(d_pre)
        return bias_sum + eight_rows(d_pre)

    sums[1] = lax.fori_loop(0, rows // tile, deactivate, nothing, unroll=4)
    leave(d_pre_b, results[1], out_sems.at[1])
    share = depth // (2 * lat_count)

    def put(which, half_at, values):
        block = to_bf16(values)
        for place in range(lat_count):
            grads[half_at ^ core, lat ^ place, pl.ds(which * share, share), :] = block[
                place * share : (place + 1) * share
            ]

    for half_at in range(2):
        columns = pl.ds(half_at * (depth // 2), depth // 2)
        put(2, half_at, dot_tn(nodes[:, columns], d_pre_b[...]))
        put(3, half_at, dot_tn(agg_b[:, columns], d_pre_b[...]))
        put(4, half_at, dot_tn(hidden_b[:, columns], d_out_b[...]))
    for part in range(2):
        for spot in range(lat_count):
            place = pl.ds(2 * share, 3 * share)
            leave(
                grads.at[part, spot, place],
                outs[part * lat_count + spot].at[place],
                grad_sems.at[part, spot, 0],
            )
    d_half[pl.ds(0, cols), :] = jnp.zeros((cols, depth), jnp.float32)
    d_half[pl.ds(rows + cols, cols), :] = jnp.zeros((cols, depth), jnp.float32)
    for which in (0, 4):
        slopes[which, pl.ds(0, cols), :] = jnp.zeros((cols, depth), jnp.bfloat16)
    for which in (1, 5):
        slopes[which, pl.ds(rows + cols, cols), :] = jnp.zeros((cols, depth), jnp.bfloat16)
    for start in range(0, rows, step_rows):
        d_sum = dot_nt(d_pre_b[pl.ds(start, step_rows), :], w_agg[...])
        d_half[pl.ds(start + cols, step_rows), :] = 0.5 * to_f32(to_bf16(d_sum))

    def slope_times(which, place, lanes):
        return to_f32(slopes[which, place, lanes]) * d_half[place, lanes]

    def receive(step, bias_sum):
        base = aligned(step * tile, tile)
        here = pl.ds(base, tile)
        value = d_half[pl.ds(aligned(base + cols, tile), tile), :] * slope_sum[here, :]
        total[here, :] = value
        return bias_sum + eight_rows(value)

    sums[0] = lax.fori_loop(0, rows // tile, receive, nothing, unroll=4)
    far[...] = jnp.zeros_like(far)

    edge_place = lax.broadcasted_iota(jnp.int32, (patch_rows, 1), 0)
    for lane in range(0, depth, 128):
        lanes = pl.ds(lane, 128)
        right_edge = jnp.zeros((patch_rows, 128), jnp.float32)
        left_edge = jnp.zeros((patch_rows, 128), jnp.float32)
        for row in range(patch_rows):
            above_row, out = pl.ds(row * cols, cols), pl.ds(row * cols, cols)
            here, below_row = pl.ds((row + 1) * cols, cols), pl.ds((row + 2) * cols, cols)
            to_mid = slope_times(0, above_row, lanes) + slope_times(1, below_row, lanes)
            to_right = slope_times(2, here, lanes) + slope_times(5, below_row, lanes)
            to_left = slope_times(3, here, lanes) + slope_times(4, above_row, lanes)
            work[out, lanes] = (
                to_mid
                + jnp.where(first, 0.0, pltpu.roll(to_right, 1, 0))
                + jnp.where(last, 0.0, pltpu.roll(to_left, cols - 1, 0))
            )
            right_edge = jnp.where(edge_place == row, to_right[cols - 1 : cols], right_edge)
            left_edge = jnp.where(edge_place == row, to_left[0:1], left_edge)
        far[right_place, lanes] = right_edge
        far[left_place, lanes] = left_edge
    row_first, row_last = pl.ds(cols, cols), pl.ds(rows, cols)
    eight = lax.broadcasted_iota(jnp.int32, (8, 1), 0)
    for lane in range(0, depth, 128):
        lanes = pl.ds(lane, 128)
        to_right = slope_times(5, row_first, lanes)
        to_left = slope_times(4, row_last, lanes)
        up = slope_times(1, row_first, lanes) + jnp.where(first, 0.0, pltpu.roll(to_right, 1, 0))
        down = slope_times(0, row_last, lanes) + jnp.where(
            last, 0.0, pltpu.roll(to_left, cols - 1, 0)
        )
        near_d[upper, lanes] = to_bf16(up)
        near_d[lower, lanes] = to_bf16(down)
        far[right_corner, lanes] = jnp.where(eight == 0, to_right[cols - 1 : cols], 0.0)
        far[left_corner, lanes] = jnp.where(eight == 0, to_left[0:1], 0.0)
    d_up[...] = near_d[upper, :]
    d_down[...] = near_d[lower, :]
    leave(d_up, results[4], out_sems.at[4])
    leave(d_down, results[5], out_sems.at[5])

    for k in range(coarse_count):
        coarse_d[pl.ds(k, 1), :] = d_half[pl.ds(slots[k] + cols, 1), :]
    long_d = dot_exact(recv_hot[...], coarse_d[...]) * long_slope
    sums[0] += eight_rows(long_d)
    coarse_d[...] = dot_exact_tn(recv_hot[...], long_d)
    for k in range(coarse_count):
        spot = pl.ds(slots[k], 1)
        total[spot, :] = total[spot, :] + coarse_d[pl.ds(k, 1), :]
    coarse[...] = dot_exact_tn(send_hot[...], long_d)
    for source in range(lon_count):
        start = source // chip_count * half_far + source % chip_count * pack
        far[pl.ds(start, coarse_count), :] = coarse[pl.ds(source * coarse_count, coarse_count), :]
    d_gathered[...] = to_bf16(far[same, :])
    d_crossed[...] = to_bf16(far[cross, :])
    leave(d_gathered, results[6], out_sems.at[6])
    leave(d_crossed, results[7], out_sems.at[7])
    for block in blocks:
        d_recv_b[block, :] = to_bf16(total[block, :])
        agg_b[block, :] = to_bf16(work[block, :])
    leave(d_recv_b, results[2], out_sems.at[2])
    leave(agg_b, results[3], out_sems.at[3])
    for half_at in range(2):
        columns = pl.ds(half_at * (depth // 2), depth // 2)
        put(0, half_at, dot_tn(nodes[:, columns], agg_b[...])
            + dot_tn(near_nodes[:, columns], near_d[...])
            + dot_tn(gathered[:, columns], d_gathered[...])
            + dot_tn(crossed[:, columns], d_crossed[...]))
        put(1, half_at, dot_tn(nodes[:, columns], d_recv_b[...]))
    place = lax.broadcasted_iota(jnp.int32, (16, depth), 0)
    vectors = jnp.zeros((16, depth), jnp.float32)
    for which in range(3):
        vectors = jnp.where(place == which, jnp.sum(sums[which], axis=0, keepdims=True), vectors)
    for part in range(2):
        for spot in range(lat_count):
            grads[part, spot, pl.ds(5 * share, 16), :] = to_bf16(vectors)
    for part in range(2):
        for spot in range(lat_count):
            for k, place in ((1, pl.ds(0, 2 * share)), (2, pl.ds(5 * share, 16))):
                leave(
                    grads.at[part, spot, place],
                    outs[part * lat_count + spot].at[place],
                    grad_sems.at[part, spot, k],
                )
    for copy in leaving:
        copy.wait()


def update(dims, ints, vectors, arrays):
    patch_rows, cols, lon_count, coarse_count, lat_count = dims
    rows, depth = patch_rows * cols, vectors[0].shape[-1]
    share = depth // (2 * lat_count)
    edge_count = ints[1].shape[0] * ints[1].shape[1]
    coarse_ids = lon_count * coarse_count
    far_rows = lon_count * (coarse_count + patch_rows + 8) + 2 * (patch_rows + 16)
    near_rows = 2 * cols
    long_rows = rows + 2 * cols
    out = lambda *size: jax.ShapeDtypeStruct(size, jnp.bfloat16)
    full = lambda *size: pltpu.VMEM(size, jnp.float32)
    half = lambda *size: pltpu.VMEM(size, jnp.bfloat16)
    smem, vmem = pl.BlockSpec(memory_space=pltpu.SMEM), pl.BlockSpec(memory_space=pltpu.VMEM)
    anywhere = pl.BlockSpec(memory_space=pl.ANY)
    weight = half(depth, depth)
    return pl.pallas_call(
        functools.partial(update_kernel, dims),
        in_specs=[smem] * len(ints) + [vmem] * len(vectors) + [anywhere] * len(arrays),
        out_specs=[anywhere] * (8 + 2 * lat_count),
        out_shape=[out(rows, depth)] * 4
        + [out(cols, depth)] * 2
        + [out(far_rows // 2, depth)] * 2
        + [out(5 * share + 16, depth)] * (2 * lat_count),
        scratch_shapes=[half(near_rows, depth)]
        + [half(far_rows // 2, depth)] * 2
        + [weight, half(rows, depth)]
        + [weight] * 4
        + [half(rows, depth)]
        + [half(cols, depth)] * 2
        + [half(far_rows // 2, depth)] * 2
        + [half(rows, depth)] * 3
        + [full(long_rows, depth)] * 3
        + [half(6, long_rows, depth)]
        + [full(rows, depth)] * 4
        + [half(rows, depth)] * 3
        + [full(long_rows, depth), full(far_rows, depth)]
        + [half(near_rows, depth)]
        + [
            full(3, 8, depth),
            full(coarse_ids, depth),
            full(coarse_count, depth),
            full(edge_count, coarse_ids),
            full(edge_count, coarse_count),
            half(2, lat_count, 5 * share + 16, depth),
            pltpu.SemaphoreType.DMA((9,)),
            pltpu.SemaphoreType.DMA((2,)),
            pltpu.SemaphoreType.DMA((8,)),
            pltpu.SemaphoreType.DMA((2, lat_count, 3)),
        ],
        compiler_params=pltpu.CompilerParams(vmem_limit_bytes=63 * MIB),
        cost_estimate=pl.CostEstimate(
            flops=26 * rows * depth * depth, bytes_accessed=20_000_000, transcendentals=0
        ),
        name="update",
    )(*ints, *vectors, *arrays)


def finish_kernel(dims, scale, slots, *refs):
    patch_rows, cols, _, coarse_count, lat_count = dims
    rows = patch_rows * cols
    (
        cotangent,
        d_pre_b,
        d_recv_b,
        d_send,
        one,
        two,
        back,
        w_self,
        w_recv,
        w_send,
        summed,
        grad_nodes,
        *vectors,
        total,
    ) = refs
    step_rows = 256
    for start in range(0, rows, step_rows):
        block = pl.ds(start, step_rows)
        total[block, :] = to_f32(d_send[block, :])
    start = (1 - lax.axis_index("lat") % 2) * (rows - cols)
    for start, part in ((start, one), (rows - cols - start, two)):
        total[pl.ds(aligned(start, cols), cols), :] += to_f32(part[...])
    for which, vector in enumerate(vectors):
        vector[...] = scale * summed[pl.ds(summed.shape[0] - 8 + which, 1), :]
    returned = back[...]
    outer = jnp.where(lax.axis_index("lon") % 2 == 0, 0, cols - 1)
    for row in range(patch_rows):
        for spot, at in ((outer, 0), (cols - 1 - outer, patch_rows)):
            one = coarse_count + at + row
            total[pl.ds(row * cols + spot, 1), :] += returned[one : one + 1]
    for k in range(coarse_count):
        total[pl.ds(slots[k], 1), :] += returned[k : k + 1]
    for start in range(0, rows, step_rows):
        block = pl.ds(start, step_rows)
        grad_nodes[block, :] = to_bf16(
            to_f32(cotangent[block, :])
            + dot_nt(d_pre_b[block, :], w_self[...])
            + dot_nt(d_recv_b[block, :], w_recv[...])
            + dot_nt(to_bf16(total[block, :]), w_send[...])
        )


def finish(dims, scale, slots, arrays):
    rows, depth = arrays[0].shape
    smem, vmem = pl.BlockSpec(memory_space=pltpu.SMEM), pl.BlockSpec(memory_space=pltpu.VMEM)
    return pl.pallas_call(
        functools.partial(finish_kernel, dims, scale),
        in_specs=[smem] + [vmem] * len(arrays),
        out_specs=[vmem] * 4,
        out_shape=[jax.ShapeDtypeStruct((rows, depth), jnp.bfloat16)]
        + [jax.ShapeDtypeStruct((1, depth), jnp.float32)] * 3,
        scratch_shapes=[pltpu.VMEM((rows, depth), jnp.float32)],
        compiler_params=pltpu.CompilerParams(vmem_limit_bytes=63 * MIB),
        cost_estimate=pl.CostEstimate(
            flops=6 * rows * depth * depth, bytes_accessed=8_000_000, transcendentals=0
        ),
        name="finish",
    )(slots, *arrays)


def swapped(values, axis, bit):
    count = lax.axis_size(axis)
    return lax.ppermute(values, axis, [(i, i ^ bit) for i in range(count)])


def summed_part(mine, other, d_crossed, returning, borders):
    lat_count, depth = len(mine), mine[0].shape[-1]
    chip_count = lax.axis_size("lon") // 2
    chip = lax.axis_index("lon") // 2
    share = depth // (2 * lat_count)
    order = list(range(lat_count - 1, -1, -1))
    crossed = {step: swapped(other[step], "lon", 1) for step in order}
    messages = [to_bf16(to_f32(mine[step]) + to_f32(crossed[step])) for step in order[:-1]]
    messages[0], d_crossed = lax.optimization_barrier((messages[0], d_crossed))
    received = [swapped(messages[lat_count - 1 - step], "lat", step) for step in order[-2::-1]]
    received, returned = lax.optimization_barrier((received, returning(d_crossed)))
    total = to_f32(mine[0]) + to_f32(crossed[0])
    for part in received:
        total = total + to_f32(part)
    total = to_bf16(total)
    vectors = total[5 * share : 5 * share + 8]
    parts = total[: 5 * share].reshape(5, chip_count, share // chip_count, depth)

    def message_for(step):
        part = lax.dynamic_index_in_dim(parts, chip ^ step, axis=1, keepdims=False)
        return jnp.concatenate([part.reshape(-1, depth), vectors])

    steps = [1, *range(chip_count - 1, 1, -1)]
    received = [swapped(message_for(step), "lon", 2 * step) for step in steps]
    received[0], returned = lax.optimization_barrier((received[0], returned))
    received, bordered = lax.optimization_barrier((received, borders(returned)))
    total = to_f32(message_for(0))
    for part in received:
        total = total + to_f32(part)
    return total, returned, bordered


def gathered_share(total, lat_count):
    depth = total.shape[-1]
    share = depth // (2 * lat_count)
    chip_count = lax.axis_size("lon") // 2
    chip = lax.axis_index("lon") // 2
    part = to_bf16(total[: 5 * share // chip_count])
    parts = jnp.stack([part] + [swapped(part, "lon", 2 * k) for k in range(1, chip_count)])
    parts = parts[chip ^ jnp.arange(chip_count)].reshape(chip_count, 5, -1, depth)
    return jnp.transpose(parts, (1, 0, 2, 3)).reshape(5 * share, depth)


def unpack_kernel(pieces, scale, *refs):
    count = len(refs)
    held, staged, load_sems, sems = refs[count - 4 :]
    outs = refs[count - 9 : count - 4]
    depth = outs[0].shape[-1]
    share = depth // (2 * lax.axis_size("lat"))
    core, lat = lax.axis_index("lon") % 2, lax.axis_index("lat")
    loads = [
        pltpu.make_async_copy(refs[k], held.at[k], load_sems.at[k]) for k in range(len(pieces))
    ]
    for load in loads:
        load.start()
    copies = []
    for k, (flip, step) in enumerate(pieces):
        loads[k].wait()
        start = (core ^ flip) * (depth // 2) + (lat ^ step) * share
        place = pl.ds(aligned(start, share), share)
        for which in range(5):
            staged[k, which] = scale * to_f32(held[k, pl.ds(which * share, share), :])
            copies.append(
                pltpu.make_async_copy(
                    staged.at[k, which], outs[which].at[place], sems.at[k, which]
                )
            )
            copies[-1].start()
    for copy in copies:
        copy.wait()


def unpack(pieces, scale, shares, begun=()):
    depth = shares[0].shape[-1]
    rows = shares[0].shape[0]
    anywhere = pl.BlockSpec(memory_space=pl.ANY)
    return pl.pallas_call(
        functools.partial(unpack_kernel, pieces, scale),
        in_specs=[anywhere] * (len(shares) + len(begun)),
        out_specs=[anywhere] * 5,
        out_shape=[jax.ShapeDtypeStruct((depth, depth), jnp.float32)] * 5,
        scratch_shapes=[
            pltpu.VMEM((len(shares), rows, depth), jnp.bfloat16),
            pltpu.VMEM((len(shares), 5, rows // 5, depth), jnp.float32),
            pltpu.SemaphoreType.DMA((len(shares),)),
            pltpu.SemaphoreType.DMA((len(shares), 5)),
        ],
        input_output_aliases={len(shares) + k: k for k in range(len(begun))},
        compiler_params=pltpu.CompilerParams(vmem_limit_bytes=10 * MIB),
        cost_estimate=pl.CostEstimate(flops=0, bytes_accessed=8_000_000, transcendentals=0),
        name=f"unpack_{len(pieces)}",
    )(*shares, *begun)


def on_device(
    nodes,
    cotangent,
    w_send,
    w_recv,
    edge_bias,
    w_self,
    w_agg,
    node_bias,
    w_out,
    gain,
    coarse_slots,
    long_senders,
    long_receivers,
):
    patch_rows, cols, depth = nodes.shape
    rows = patch_rows * cols
    lat_count, lon_count = lax.axis_size("lat"), lax.axis_size("lon")
    chip_count = lon_count // 2
    lon = lax.axis_index("lon")
    scale = float(rows * lat_count * lon_count) ** (-0.5)
    slots = coarse_slots.reshape(-1)
    coarse_count = slots.shape[0]
    dims = (patch_rows, cols, lon_count, coarse_count, lat_count)
    flat = nodes.reshape(rows, depth)
    cot = cotangent.reshape(rows, depth)

    odd = lax.axis_index("lat") % 2 == 1
    firsts = [(i, i ^ 1) for i in range(lat_count)]
    seconds = [pair for i in range(1, lat_count - 1, 2) for pair in ((i, i + 1), (i + 1, i))]

    def paired(to_above, to_below):
        two = lax.ppermute(jnp.where(odd, to_below, to_above), "lat", seconds)
        return lax.ppermute(jnp.where(odd, to_above, to_below), "lat", firsts), two

    one, two = paired(flat[:cols], flat[-cols:])
    packed = pack_nodes(cols, slots, flat)
    outer_is_left = lon % 2 == 0
    corners = jnp.where(odd, one[:1], two[:1]), jnp.where(odd, two[-1:], one[-1:])
    outer_corner = jnp.where(outer_is_left, corners[0], corners[1])
    inner_corner = jnp.where(outer_is_left, corners[1], corners[0])
    outer_end, filler = coarse_count + patch_rows, jnp.zeros((15, depth), jnp.bfloat16)
    message = jnp.concatenate([packed[:outer_end], outer_corner, filler[:7]])
    chips = [swapped(message, "lon", 2 * k) for k in range(chip_count - 1, 0, -1)][::-1]
    gathered = jnp.concatenate([message, *chips, packed[outer_end:], inner_corner, filler])
    crossed = swapped(gathered, "lon", 1)
    outs = update(
        dims,
        (slots, long_senders.reshape(lon_count, -1), long_receivers.reshape(lon_count, -1)),
        (edge_bias[None], node_bias[None], gain[None]),
        (
            one,
            two,
            gathered,
            crossed,
            w_send,
            flat,
            w_recv,
            w_self,
            w_agg,
            w_out,
            cot,
        ),
    )
    new_nodes, d_pre_b, d_recv_b, d_send, d_up, d_down, d_gathered, d_crossed = outs[:8]
    mine, other = outs[8 : 8 + lat_count], outs[8 + lat_count :]

    def returning(d_crossed):
        chips = to_bf16(to_f32(d_gathered) + to_f32(swapped(d_crossed, "lon", 1)))
        inner = to_f32(chips[-patch_rows - 16 :])
        parts = chips[: -patch_rows - 16].reshape(chip_count, -1, depth)
        steps = [1, *range(chip_count - 1, 1, -1)]
        received = [swapped(parts[step], "lon", 2 * step) for step in steps]
        return sum([to_f32(one) for one in received], to_f32(parts[0])), inner

    def borders(returned):
        outer_corner, inner_corner = returned[0][outer_end :][:1], returned[1][patch_rows:][:1]
        up_corner = jnp.where(outer_is_left, outer_corner, inner_corner)
        down_corner = jnp.where(outer_is_left, inner_corner, outer_corner)
        ups = jnp.concatenate([to_bf16(to_f32(d_up[:1]) + up_corner), d_up[1:]])
        downs = jnp.concatenate([d_down[:-1], to_bf16(to_f32(d_down[-1:]) + down_corner)])
        return paired(ups, downs)

    total, (back, inner), bordered = summed_part(mine, other, d_crossed, returning, borders)
    back = jnp.concatenate([back[:outer_end], inner[:patch_rows]])
    grad_nodes, *vectors = finish(
        dims,
        scale,
        slots,
        (
            cot,
            d_pre_b,
            d_recv_b,
            d_send,
            *bordered,
            back,
            w_self,
            w_recv,
            w_send,
            total,
        ),
    )

    ready = gathered_share(total, lat_count)
    shares = [swapped(ready, "lat", step) for step in range(lat_count - 1, 0, -1)][::-1]
    outs = unpack([(0, 0)], scale, [ready])
    shares, grad_nodes, outs = lax.optimization_barrier((shares, grad_nodes, outs))
    crossed = [swapped(part, "lon", 1) for part in (ready, *shares)]
    outs = unpack([(0, step) for step in range(1, lat_count)], scale, shares, outs)
    outs = unpack([(1, step) for step in range(lat_count)], scale, crossed, outs)
    return (
        new_nodes.reshape(patch_rows, cols, depth),
        grad_nodes.reshape(patch_rows, cols, depth),
        outs[0],
        outs[1],
        vectors[0][0],
        outs[2],
        outs[3],
        vectors[1][0],
        outs[4],
        vectors[2][0],
    )


def solution(mesh):
    patches = P("lat", "lon", None)
    edges = P("lat", "lon", None, None)
    return jax.shard_map(
        on_device,
        mesh=mesh,
        in_specs=(patches, patches) + (P(),) * 8 + (patches, edges, edges),
        out_specs=(patches, patches) + (P(),) * 8,
        check_vma=False,
    )
```
